128 devices in a mesh: section: 2 (over core), ctx: 4 (over z), exp: 16 (over x, y).
Axes of the slice: x: 4, y: 4, z: 4, core: 2. Of those that a mesh axis runs over, the one named last changes fastest.
Arguments:
- inputs: bfloat16 [2, 16, 512, 768], P(None, 'exp', 'ctx'), may hold values from -6 to 6
- cotangent: bfloat16 [2, 16, 512, 768], P(None, 'exp', 'ctx'), may hold values from -6 to 6
- routes: int32 [2, 2, 16, 512, 2], P('section', None, 'exp', 'ctx'), may hold values from 0 to 15, all different within a row; in each aligned block of 128 rows (0 to 127, 128 to 255, ..., all dimensions but the last counted through in order) at most 17 rows name the same one
- block_order: int32 [8], replicated, may hold values from 0 to 7, each once
- attn_gain: bfloat16 [2, 768], P('section', ('ctx', 'exp')), may hold values from 0.5 to 1.5
- qkv_weight: bfloat16 [2, 768, 2304], P('section', ('ctx', 'exp')), may hold values from -0.21875 to 0.21875
- out_weight: bfloat16 [2, 768, 768], P('section', ('ctx', 'exp')), may hold values from -4 to 4
- rel_bias: bfloat16 [2, 384], P('section', ('ctx', 'exp')), may hold values from -4 to 4
- moe_gain: bfloat16 [2, 768], P('section', ('ctx', 'exp')), may hold values from 0.5 to 1.5
- router_weight: bfloat16 [2, 768, 16], P('section', ('ctx', 'exp')), may hold values from -0.375 to 0.375
- expert_in: bfloat16 [2, 16, 768, 3072], P('section', 'exp', None, 'ctx'), may hold values from -0.21875 to 0.21875
- expert_out: bfloat16 [2, 16, 768, 3072], P('section', 'exp', None, 'ctx'), may hold values from -0.109375 to 0.109375
Outputs:
- layer_out: bfloat16 [2, 2, 16, 512, 768], P('section', None, 'exp', 'ctx')
- input_grad: float32 [2, 2, 16, 512, 768], P('section', None, 'exp', 'ctx')
- attn_gain_grad: float32 [2, 768], P('section', ('ctx', 'exp'))
- qkv_grad: float32 [2, 768, 2304], P('section', ('ctx', 'exp'))
- out_grad: float32 [2, 768, 768], P('section', ('ctx', 'exp'))
- bias_grad: float32 [2, 384], P('section', ('ctx', 'exp'))
- moe_gain_grad: float32 [2, 768], P('section', ('ctx', 'exp'))
- router_grad: float32 [2, 768, 16], P('section', ('ctx', 'exp'))
- expert_in_grad: float32 [2, 16, 768, 3072], P('section', 'exp', None, 'ctx')
- expert_out_grad: float32 [2, 16, 768, 3072], P('section', 'exp', None, 'ctx')
The draws below stay inside these ranges and needn't reach their ends.
Inputs may be any that keep to these rules, and one draw needn't show every extreme that they name: `routes`: within every aligned block of 128 rows (one micro-batch, one sequence, rows b * 128 onward) no expert is named by more than 17 of the block's assignments, a bound that some block reaches; the two experts of a token differ. A permutation: stored block j of every sequence, rows j * 64 onward, holds positions block_order[j] * 64 onward.
All inputs are finite; a program needn't handle non-finite values.
Results may differ from the reference program's by a relative error of at most 0.04.
Values may be sent and summed in bfloat16 or wider, within the bound.
A program may use at most 256 MiB of HBM per device.

```python
import math
import jax
import jax.numpy as jnp
import numpy as np
from jax import lax

D = 768
HEADS = 12
HEAD_DIM = 64
FF = 3072
BUCKETS = 32
REACH = 128
TOP = 2
MICRO = 2
SEQ = 512
EXPERTS = 16
ROWS = 128
CAP = 17
N_SECTION = 2
N_CTX = 4
N_EXP = 16


def block_levels(stream_key, dims, pieces, smallest, high):
    loudness = 1.0
    for position, blocks in pieces:
        steps = jax.random.uniform(jax.random.fold_in(jax.random.fold_in(stream_key, 6), position), (blocks,), jnp.float32, smallest / len(pieces), high / len(pieces))
        loudness = loudness * jnp.repeat(jnp.exp(steps), dims[position] // blocks).reshape((-1,) + (1,) * (len(dims) - 1 - position))
    return loudness


def deal_out(own_key, own, number, rows, number_of, top, bound, lean):
    ranking = jax.random.permutation(own_key, number_of)
    crowded, ordinary = portions_of(number_of, rows * top, bound, lean, True), portions_of(number_of, rows * top, bound, lean, False)
    places = jnp.arange(number_of)

    def named(sizes, rotation):
        used = int((sizes > 0).sum())
        fixed = max(1, used // 4)
        passed = fixed + (places - fixed + rotation * (used - fixed)) % max(1, number_of - fixed)
        return jnp.zeros((number_of,), jnp.int32).at[ranking[jnp.where(places < fixed, places, passed)]].set(jnp.asarray(sizes, jnp.int32))

    sizes = jnp.where(number % 4 == 0, named(crowded, number // 4), named(ordinary, number - number // 4 - 1))
    mixed = jax.random.permutation(jax.random.fold_in(own, 3), number_of)
    giver, receiver = mixed[0:number_of // 2 * 2:2], mixed[1:number_of // 2 * 2:2]
    margin = jnp.minimum(sizes[giver] - 1, bound - sizes[receiver]) // 2
    margin = jnp.where((giver == ranking[0]) | (receiver == ranking[0]) | (sizes[receiver] == 0), 0, jnp.maximum(margin, 0))
    passed = jax.random.randint(jax.random.fold_in(own, 4), (number_of // 2,), 0, 1 << 20) % (margin + 1)
    sizes = sizes.at[giver].add(-passed).at[receiver].add(passed)
    members = jnp.searchsorted(jnp.cumsum(sizes), jnp.arange(rows * top), side="right").astype(jnp.int32)
    table = members.reshape(top, rows).T
    table = table[jax.random.permutation(jax.random.fold_in(own, 1), rows)]
    rotation = jax.random.randint(jax.random.fold_in(own, 2), (rows, 1), 0, top)
    return jnp.take_along_axis(table, (jnp.arange(top)[None, :] + rotation) % top, axis=1)


def portions_of(amount, total, bound, slope, full):
    weights = [(1 << 20) // math.isqrt(grade ** slope) + 1 for grade in range(1, amount + 1)]
    largest = bound if full else min(bound, max(-(-total // amount), total * weights[0] // sum(weights)))
    least = 1 if total - largest >= amount - 1 else 0
    counts, spare = [largest] + [least] * (amount - 1), total - largest - least * (amount - 1)
    while spare > 0:
        free = [i for i in range(1, amount) if counts[i] < largest] or [i for i in range(1, amount) if counts[i] < bound]
        pool, left = sum([weights[i] for i in free]), spare
        for i in free:
            more = min(bound - counts[i], max(1, left * weights[i] // pool), spare)
            counts[i] = counts[i] + more
            spare = spare - more
    return np.array(counts)


def centred(own_key, extent, spread, most, shards=(), held_as=jnp.bfloat16):
    result = spread * jax.random.normal(own_key, extent, jnp.float32)
    if shards:
        result = result * block_levels(own_key, extent, shards, -0.22, 0.18)
    return jnp.clip(result, -most, most).astype(held_as)


def setup_inputs(seed: int = 0) -> dict:
    seeds = jax.random.split(jax.random.key(seed), 13)
    inputs = centred(seeds[0], (MICRO, N_EXP, SEQ, D), 1.0, 6.0, ((1, 16), (2, 4)))
    cotangent = centred(seeds[1], (MICRO, N_EXP, SEQ, D), 1.0, 6.0, ((1, 16), (2, 4)))
    routes_keys = jax.random.split(jax.random.fold_in(seeds[2], 1), N_SECTION * MICRO * N_EXP * SEQ // ROWS)
    routes_turns = jax.random.permutation(jax.random.fold_in(seeds[2], 3), N_SECTION * MICRO * N_EXP * SEQ // ROWS)
    routes = jax.vmap(lambda own, number: deal_out(jax.random.fold_in(seeds[2], 2), own, number, ROWS, EXPERTS, TOP, CAP, 1))(routes_keys, routes_turns).reshape((N_SECTION, MICRO, N_EXP, SEQ, TOP))
    block_order = jax.random.permutation(seeds[3], 2 * N_CTX).astype(jnp.int32)
    attn_gain = jnp.clip(1.0 + 0.1 * jax.random.normal(seeds[4], (N_SECTION, D), jnp.float32), 0.5, 1.5).astype(jnp.bfloat16)
    qkv_weight = centred(seeds[5], (N_SECTION, D, 3 * D), D ** -0.5, 0.21875, ((0, 2), (1, 64)))
    out_weight = centred(seeds[6], (N_SECTION, D, D), ((SEQ // 8) ** 0.5 / D ** 0.5), 4.0, ((0, 2), (1, 64)))
    rel_bias = centred(seeds[7], (N_SECTION, BUCKETS * HEADS), 1.0, 4.0, ((0, 2), (1, 64)))
    moe_gain = jnp.clip(1.0 + 0.1 * jax.random.normal(seeds[8], (N_SECTION, D), jnp.float32), 0.5, 1.5).astype(jnp.bfloat16)
    router_weight = centred(seeds[9], (N_SECTION, D, EXPERTS), (0.7 / D ** 0.5), 0.375, ((0, 2), (1, 64)))
    expert_in = centred(seeds[10], (N_SECTION, EXPERTS, D, FF), D ** -0.5, 0.21875, ((0, 2), (1, 16), (3, 4)))
    expert_out = centred(seeds[11], (N_SECTION, EXPERTS, D, FF), FF ** -0.5, 0.109375, ((0, 2), (1, 16), (3, 4)))
    return {"inputs": inputs, "cotangent": cotangent, "routes": routes, "block_order": block_order, "attn_gain": attn_gain, "qkv_weight": qkv_weight, "out_weight": out_weight, "rel_bias": rel_bias, "moe_gain": moe_gain, "router_weight": router_weight, "expert_in": expert_in, "expert_out": expert_out}


HIGH = lax.Precision.HIGHEST
EPS = 1e-06
NEG = -1e+30

@jax.custom_vjp
def low(v):
    return lax.optimization_barrier(v.astype(jnp.bfloat16)).astype(jnp.float32)

@jax.custom_vjp
def low_back(v):
    return v

def low_keep(v):
    return (low(v), None)

def low_pass(kept, grad):
    return (grad,)

def back_keep(v):
    return (v, None)

def back_low(kept, grad):
    return (low(grad),)
low.defvjp(low_keep, low_pass)
low_back.defvjp(back_keep, back_low)

def rms_norm(values, gain):
    return values * lax.rsqrt(lax.optimization_barrier(jnp.mean(values * values, -1, keepdims=True)) + EPS) * gain

def bucket_of(distance):
    half = BUCKETS // 2
    powers = np.arange(1, BUCKETS - half) / (BUCKETS - half)
    bounds = jnp.asarray(np.ceil(half * (REACH / half) ** powers).astype(np.int32))
    distance = jnp.maximum(distance, 0)
    above = (distance[..., None] >= bounds).astype(jnp.int32)
    return jnp.minimum(distance, half) + lax.optimization_barrier(jnp.sum(above, -1, dtype=jnp.int32))

def positions(block_order, seq_len):
    count = block_order.shape[0]
    span = seq_len // count
    index = jnp.arange(seq_len, dtype=jnp.int32)
    owner = (index // span)[:, None] == jnp.arange(count, dtype=jnp.int32)[None, :]
    start = lax.optimization_barrier(jnp.sum(jnp.where(owner, block_order[None, :], 0), -1, dtype=jnp.int32))
    return start * span + index % span

def slot_tables(route_rows, experts, capacity):
    tok_count, top_count = route_rows.shape
    route_hot = (route_rows[:, :, None] == jnp.arange(experts, dtype=jnp.int32)).astype(jnp.int32)
    flat_hot = route_hot.reshape(tok_count * top_count, experts)
    earlier = jnp.cumsum(flat_hot, 0, dtype=jnp.int32) - flat_hot
    slot_number = lax.optimization_barrier(jnp.sum(earlier * flat_hot, -1, dtype=jnp.int32)).reshape(tok_count, top_count)
    target = route_rows * capacity + slot_number
    slot_hot = target[:, :, None] == jnp.arange(experts * capacity, dtype=jnp.int32)
    return (route_hot, slot_hot)

def layer(carried, params, route_all, bucket_hot, visible):
    gain_one, w_qkv, w_proj, bias_flat, gain_two, w_router, w_up, w_down = params
    bias_table = bias_flat.reshape(BUCKETS, HEADS)
    bias_all = jnp.einsum('qkb,bh->hqk', bucket_hot, bias_table, precision=HIGH)
    score_scale = HEAD_DIM ** (-0.5)

    def attend(sequence):
        normed = low(rms_norm(sequence, gain_one))
        proj = low(low_back(jnp.dot(normed, w_qkv, precision=HIGH)))
        q_heads = proj[:, :D].reshape(SEQ, HEADS, HEAD_DIM)
        k_heads = proj[:, D:2 * D].reshape(SEQ, HEADS, HEAD_DIM)
        v_heads = proj[:, 2 * D:].reshape(SEQ, HEADS, HEAD_DIM)
        scores = jnp.einsum('qhd,khd->hqk', q_heads, k_heads, precision=HIGH) * score_scale
        scores = low_back(scores + bias_all)
        scores = jnp.where(visible[None], scores, NEG)
        probs = low(jax.nn.softmax(scores, -1))
        attended = jnp.einsum('hqk,khd->qhd', probs, v_heads, precision=HIGH)
        attended = low(low_back(attended)).reshape(SEQ, D)
        return sequence + low_back(jnp.dot(attended, w_proj, precision=HIGH))
    middle = lax.map(jax.checkpoint(attend), carried.reshape(MICRO * N_EXP, SEQ, D))
    blocks = middle.reshape(-1, ROWS, D)
    block_count = blocks.shape[0]
    route_blocks = route_all.reshape(block_count, ROWS, TOP)
    mixed = low(rms_norm(blocks, gain_two))
    logits = jnp.einsum('btd,de->bte', mixed, w_router, precision=HIGH)
    route_hot, slot_hot = jax.vmap(lambda part: slot_tables(part, EXPERTS, CAP))(route_blocks)
    route_float = route_hot.astype(jnp.float32)
    slot_float = slot_hot.astype(jnp.float32)
    chosen = lax.optimization_barrier(jnp.sum(route_float * logits[:, :, None, :], -1))
    gates = jax.nn.softmax(chosen, -1)
    placing = lax.optimization_barrier(jnp.sum(slot_float, 2))
    outgoing = low_back(jnp.einsum('bts,btd->bsd', placing, mixed, precision=HIGH))
    by_expert = outgoing.reshape(block_count, EXPERTS, CAP, D).transpose(1, 0, 2, 3)
    by_expert = by_expert.reshape(EXPERTS, block_count * CAP, D)

    def expert(operands):
        entering, up_matrix, down_matrix = operands
        before = low_back(jnp.dot(entering, up_matrix, precision=HIGH))
        hidden = low(jax.nn.gelu(before, approximate=True))
        return low(low_back(jnp.einsum('rf,df->rd', hidden, down_matrix, precision=HIGH)))
    returned = lax.map(jax.checkpoint(expert), (by_expert, w_up, w_down))
    back_rows = returned.reshape(EXPERTS, block_count, CAP, D).transpose(1, 0, 2, 3)
    back_rows = back_rows.reshape(block_count, EXPERTS * CAP, D)
    picked = jnp.einsum('btks,bsd->btkd', slot_float, back_rows, precision=HIGH)
    moe_out = lax.optimization_barrier(jnp.sum(gates[..., None] * picked, 2))
    return (blocks + moe_out).reshape(carried.shape)

def reference(inputs, cotangent, routes, block_order, attn_gain, qkv_weight, out_weight, rel_bias, moe_gain, router_weight, expert_in, expert_out):
    pos_all = positions(block_order, SEQ)
    distance = pos_all[:, None] - pos_all[None, :]
    visible = distance >= 0
    bucket_hot = (bucket_of(distance)[..., None] == jnp.arange(BUCKETS, dtype=jnp.int32)).astype(jnp.float32)
    weight_list = (attn_gain, qkv_weight, out_weight, rel_bias, moe_gain, router_weight, expert_in, expert_out)
    params_zero = tuple((part[0].astype(jnp.float32) for part in weight_list))
    params_one = tuple((part[1].astype(jnp.float32) for part in weight_list))

    def section_fn(route_section):

        def run(carried, *params):
            return layer(carried, params, route_section, bucket_hot, visible)
        return run
    first_out, first_back = jax.vjp(section_fn(routes[0]), inputs.astype(jnp.float32), *params_zero)
    handed = low(first_out)
    second_out, second_back = jax.vjp(section_fn(routes[1]), handed, *params_one)
    second_grads = second_back(cotangent.astype(jnp.float32))
    handed_grad = low(second_grads[0])
    first_grads = first_back(handed_grad)
    layer_out = jnp.stack([handed, second_out]).astype(jnp.bfloat16)
    input_grad = jnp.stack([first_grads[0], handed_grad])
    grads = [jnp.stack([first_grads[i + 1], second_grads[i + 1]]) for i in range(8)]
    return (layer_out, input_grad, grads[0], grads[1], grads[2], grads[3], grads[4], grads[5], grads[6], grads[7])
```

```python
import functools
import math

import jax
import jax.numpy as jnp
import numpy as np
from jax import lax
from jax.experimental import pallas as pl
from jax.experimental.pallas import tpu as pltpu
from jax.sharding import PartitionSpec as P

HEADS = 12
HEAD_DIM = 64
BUCKETS = 32
REACH = 128
TOP = 2
EPS = 1e-06
NEG = -1e30
SPAN = 64
KINDS = 4
MESH = pl.DeviceIdType.MESH
BF16 = jnp.bfloat16
F32 = jnp.float32
GELU_C = math.sqrt(2.0 / math.pi)


def dot(a, b, dims):
    return lax.dot_general(a, b, (dims, ((), ())), preferred_element_type=F32)


def mm(a, b):
    return dot(a, b, ((1,), (0,)))


def mm_nt(a, b):
    return dot(a, b, ((1,), (1,)))


def mm_tn(a, b):
    return dot(a, b, ((0,), (0,)))


def meet_neighbours(axis, count):
    me = lax.axis_index(axis)
    right, left = lax.rem(me + 1, count), lax.rem(me + count - 1, count)
    barrier = pltpu.get_barrier_semaphore()
    for neighbour in (left, right):
        pl.semaphore_signal(barrier, inc=1, device_id={axis: neighbour}, device_id_type=MESH)
    pl.semaphore_wait(barrier, 2)
    return me, right, left


def remote(src, dst, send, recv, k, axis, to):
    return pltpu.make_async_remote_copy(
        src_ref=src,
        dst_ref=dst,
        send_sem=send.at[k],
        recv_sem=recv.at[k],
        device_id={axis: to},
        device_id_type=MESH,
    )


def halves(rows):
    first = (rows // 2 + 15) // 16 * 16
    return (pl.ds(0, first), pl.ds(first, rows - first))


def gather_kernel(axis, rows, x_ref, out_ref, send, recv, own_sem):
    me, right, left = meet_neighbours(axis, 4)
    low, high = halves(rows)
    own = pltpu.make_async_copy(x_ref, out_ref.at[me], own_sem)

    def step(k, src, slot, part, to):
        return remote(src.at[part], out_ref.at[slot, part], send, recv, k, axis, to)

    to_right_low = step(0, x_ref, me, low, right)
    to_left_high = step(1, x_ref, me, high, left)
    to_right_high = step(2, x_ref, me, high, right)
    to_left_low = step(3, x_ref, me, low, left)
    to_right_low.start()
    to_left_high.start()
    to_right_high.start()
    to_left_low.start()
    own.start()
    to_right_low.wait_recv()
    on_right = step(4, out_ref.at[left], left, low, right)
    on_right.start()
    to_left_high.wait_recv()
    on_left = step(5, out_ref.at[right], right, high, left)
    on_left.start()
    to_right_high.wait_recv()
    to_left_low.wait_recv()
    on_right.wait_recv()
    on_left.wait_recv()
    for c in (to_right_low, to_left_high, to_right_high, to_left_low, on_right, on_left):
        c.wait_send()
    own.wait()


def ctx_gather(x, cid):
    rows, width = x.shape
    return pl.pallas_call(
        functools.partial(gather_kernel, "ctx", rows),
        out_shape=jax.ShapeDtypeStruct((4, rows, width), x.dtype),
        in_specs=[pl.BlockSpec(memory_space=pltpu.VMEM)],
        out_specs=pl.BlockSpec(memory_space=pltpu.VMEM),
        scratch_shapes=[
            pltpu.SemaphoreType.DMA((6,)),
            pltpu.SemaphoreType.DMA((6,)),
            pltpu.SemaphoreType.DMA,
        ],
        compiler_params=pltpu.CompilerParams(
            collective_id=cid, has_side_effects=True, vmem_limit_bytes=16 << 20
        ),
    )(x)


def scatter_kernel(
    axis, rows, x_ref, out_ref, far_l, far_r, sum_l, sum_r, in_l, in_r, send, recv
):
    me, right, left = meet_neighbours(axis, 4)
    far = lax.rem(me + 2, 4)
    low, high = halves(rows)
    n_low = low.size
    n_high = high.size

    def step(k, src, dst, to):
        return remote(src, dst, send, recv, k, axis, to)

    a = step(0, x_ref.at[far, low], far_l, right)
    b = step(1, x_ref.at[far, high], far_r, left)
    c = step(2, x_ref.at[right, high], in_l.at[high], right)
    d = step(3, x_ref.at[left, low], in_r.at[low], left)
    a.start()
    b.start()
    c.start()
    d.start()
    a.wait_recv()
    sum_r[...] = (x_ref[right, :n_low, :].astype(F32) + far_l[...].astype(F32)).astype(BF16)
    e = step(4, sum_r, in_l.at[low], right)
    e.start()
    b.wait_recv()
    sum_l[...] = (x_ref[left, n_low:, :].astype(F32) + far_r[...].astype(F32)).astype(BF16)
    f = step(5, sum_l, in_r.at[high], left)
    f.start()
    c.wait_recv()
    d.wait_recv()
    e.wait_recv()
    f.wait_recv()
    out_ref[...] = (
        x_ref[me].astype(F32) + in_l[...].astype(F32) + in_r[...].astype(F32)
    ).astype(out_ref.dtype)
    for s in (a, b, c, d, e, f):
        s.wait_send()


def ctx_scatter(x, dtype, cid):
    _, rows, width = x.shape
    low, high = halves(rows)
    v = lambda n: pltpu.VMEM((n, width), BF16)
    return pl.pallas_call(
        functools.partial(scatter_kernel, "ctx", rows),
        out_shape=jax.ShapeDtypeStruct((rows, width), dtype),
        in_specs=[pl.BlockSpec(memory_space=pltpu.VMEM)],
        out_specs=pl.BlockSpec(memory_space=pltpu.VMEM),
        scratch_shapes=[
            v(low.size),
            v(high.size),
            v(high.size),
            v(low.size),
            v(rows),
            v(rows),
            pltpu.SemaphoreType.DMA((6,)),
            pltpu.SemaphoreType.DMA((6,)),
        ],
        compiler_params=pltpu.CompilerParams(
            collective_id=cid, has_side_effects=True, vmem_limit_bytes=16 << 20
        ),
    )(x)


def bias_rows(tiles_ref, kind_ref, head, block):
    kind = kind_ref[block : block + 1, :]
    rows = jnp.where(kind == 3, tiles_ref[head, 3], NEG)
    for k in (2, 1, 0):
        rows = jnp.where(kind == k, tiles_ref[head, k], rows)
    return rows


def attend_kernel(heads, proj_ref, tiles_ref, kind_ref, out_ref, s_ref, p_ref):
    width = heads * HEAD_DIM
    seq = proj_ref.shape[0]
    parts = []
    for h in range(heads):
        q = proj_ref[:, h * HEAD_DIM : (h + 1) * HEAD_DIM]
        k = proj_ref[:, width + h * HEAD_DIM : width + (h + 1) * HEAD_DIM]
        v = proj_ref[:, 2 * width + h * HEAD_DIM : 2 * width + (h + 1) * HEAD_DIM]
        s_ref[...] = mm_nt(q, k)
        for b in range(seq // SPAN):
            at = slice(b * SPAN, (b + 1) * SPAN)
            s = s_ref[at, :] * HEAD_DIM**-0.5 + bias_rows(tiles_ref, kind_ref, h, b)
            e = jnp.exp(s - jnp.max(s, -1, keepdims=True))
            p_ref[at, :] = (e * (1.0 / jnp.sum(e, -1, keepdims=True))).astype(BF16)
        parts.append(mm(p_ref[...], v).astype(BF16))
    out_ref[...] = jnp.concatenate(parts, 1)


def attend(proj, tiles, kind):
    seq, width = proj.shape
    heads = width // (3 * HEAD_DIM)
    vm = pl.BlockSpec(memory_space=pltpu.VMEM)
    return pl.pallas_call(
        functools.partial(attend_kernel, heads),
        out_shape=jax.ShapeDtypeStruct((seq, width // 3), BF16),
        in_specs=[vm] * 3,
        out_specs=vm,
        scratch_shapes=[pltpu.VMEM((seq, seq), F32), pltpu.VMEM((seq, seq), BF16)],
        compiler_params=pltpu.CompilerParams(vmem_limit_bytes=32 << 20),
    )(proj, tiles, kind)


def attend_back_kernel(
    heads, proj_ref, da_ref, tiles_ref, kind_ref, dproj_ref, dtiles_ref, s_ref, dp_ref, p_ref, ds_ref
):
    width = heads * HEAD_DIM
    seq = proj_ref.shape[0]
    scale = HEAD_DIM**-0.5
    dq, dk, dv = [], [], []
    for h in range(heads):
        q = proj_ref[:, h * HEAD_DIM : (h + 1) * HEAD_DIM]
        k = proj_ref[:, width + h * HEAD_DIM : width + (h + 1) * HEAD_DIM]
        v = proj_ref[:, 2 * width + h * HEAD_DIM : 2 * width + (h + 1) * HEAD_DIM]
        da = da_ref[:, h * HEAD_DIM : (h + 1) * HEAD_DIM]
        s_ref[...] = mm_nt(q, k)
        dp_ref[...] = mm_nt(da, v)
        dtiles_ref[h] = jnp.zeros(dtiles_ref.shape[1:], F32)
        for b in range(seq // SPAN):
            at = slice(b * SPAN, (b + 1) * SPAN)
            s = s_ref[at, :] * scale + bias_rows(tiles_ref, kind_ref, h, b)
            e = jnp.exp(s - jnp.max(s, -1, keepdims=True))
            p = e * (1.0 / jnp.sum(e, -1, keepdims=True))
            dp = dp_ref[at, :]
            ds = p * (dp - jnp.sum(p * dp, -1, keepdims=True))
            p_ref[at, :] = p.astype(BF16)
            ds_ref[at, :] = ds.astype(BF16)
            kind = kind_ref[b : b + 1, :]
            for n in range(KINDS):
                dtiles_ref[h, n] += jnp.where(kind == n, ds, 0.0)
        p = p_ref[...]
        ds = ds_ref[...]
        dq.append((mm(ds, k) * scale).astype(BF16))
        dk.append((mm_tn(ds, q) * scale).astype(BF16))
        dv.append(mm_tn(p, da).astype(BF16))
    dproj_ref[...] = jnp.concatenate(dq + dk + dv, 1)


def attend_back(proj, da, tiles, kind):
    seq, width = proj.shape
    heads = width // (3 * HEAD_DIM)
    vm = pl.BlockSpec(memory_space=pltpu.VMEM)
    return pl.pallas_call(
        functools.partial(attend_back_kernel, heads),
        out_shape=(
            jax.ShapeDtypeStruct((seq, width), BF16),
            jax.ShapeDtypeStruct(tiles.shape, F32),
        ),
        in_specs=[vm] * 4,
        out_specs=(vm, vm),
        scratch_shapes=[
            pltpu.VMEM((seq, seq), F32),
            pltpu.VMEM((seq, seq), F32),
            pltpu.VMEM((seq, seq), BF16),
            pltpu.VMEM((seq, seq), BF16),
        ],
        compiler_params=pltpu.CompilerParams(vmem_limit_bytes=32 << 20),
    )(proj, da, tiles, kind)


def bucket_of(distance):
    half = BUCKETS // 2
    powers = np.arange(1, BUCKETS - half) / (BUCKETS - half)
    bounds = np.ceil(half * (REACH / half) ** powers).astype(np.int32)
    n = np.maximum(distance, 0)
    return np.minimum(n, half) + (n[..., None] >= bounds).sum(-1)


def tile_buckets():
    row, col = np.arange(SPAN)[:, None], np.arange(SPAN)[None, :]
    return np.stack([bucket_of(k * SPAN + row - col) for k in range(KINDS)])


def bias_tiles(table, seq):
    hot = (tile_buckets()[..., None] == np.arange(BUCKETS)).astype(np.float32)
    hot = jnp.asarray(hot.reshape(KINDS * SPAN * SPAN, BUCKETS), BF16)
    tiles = mm_nt(table.T.astype(BF16), hot).reshape(-1, KINDS, SPAN, SPAN)
    row, col = np.arange(SPAN)[:, None], np.arange(SPAN)[None, :]
    unseen = np.zeros((KINDS, SPAN, SPAN), bool)
    unseen[0] = row < col
    tiles = jnp.where(jnp.asarray(unseen), NEG, tiles)
    return jnp.tile(tiles, (1, 1, 1, seq // SPAN))


def bias_tiles_back(dtiles):
    heads, kinds, span, seq = dtiles.shape
    hot = (tile_buckets()[..., None] == np.arange(BUCKETS)).astype(np.float32)
    hot = jnp.asarray(hot.reshape(KINDS * SPAN * SPAN, BUCKETS), BF16)
    sums = jnp.sum(dtiles.reshape(heads, kinds, span, seq // span, span), 3)
    sums = sums.reshape(heads, -1)
    high = sums.astype(BF16)
    low = (sums - high.astype(F32)).astype(BF16)
    return (mm(high, hot) + mm(low, hot)).T


def norm_scale(v):
    return lax.rsqrt(jnp.mean(v * v, -1, keepdims=True) + EPS)


def norm(v, gain):
    return (v * norm_scale(v) * gain).astype(BF16)


def norm_back(v, gain, du):
    r = norm_scale(v)
    dug = du * gain
    dv = r * dug - v * (r * r * r) * jnp.mean(dug * v, -1, keepdims=True)
    return dv, jnp.sum(du * v * r, 0)


def gelu_parts(v):
    t = jnp.tanh(GELU_C * (v + 0.044715 * v * v * v))
    value = 0.5 * v * (1.0 + t)
    slope = 0.5 * (1.0 + t) + 0.5 * v * (1.0 - t * t) * GELU_C * (1.0 + 3 * 0.044715 * v * v)
    return value, slope


def slot_tables(routes, experts, capacity):
    rows = routes.shape[0]
    flat = routes.reshape(rows * TOP)
    hot = flat[:, None] == jnp.arange(experts, dtype=jnp.int32)
    before = np.tril(np.ones((rows * TOP, rows * TOP), np.float32), -1)
    earlier = mm(jnp.asarray(before, BF16), hot.astype(BF16))
    slot = jnp.sum(jnp.where(hot, earlier, 0.0), -1).astype(jnp.int32)
    target = (flat * capacity + slot).reshape(rows, TOP)
    slots = jnp.arange(experts * capacity, dtype=jnp.int32)
    slot_hot = [(target[:, c : c + 1] == slots).astype(BF16) for c in range(TOP)]
    route_hot = [(routes[:, c : c + 1] == jnp.arange(experts)).astype(F32) for c in range(TOP)]
    return route_hot, slot_hot


def exp_swap(x):
    return lax.all_to_all(x, "exp", split_axis=0, concat_axis=0, tiled=True)


def on_device(
    inputs,
    cotangent,
    routes,
    block_order,
    attn_gain,
    qkv_weight,
    out_weight,
    rel_bias,
    moe_gain,
    router_weight,
    expert_in,
    expert_out,
):
    rows, width = inputs.shape[2:]
    n_ctx, n_exp = lax.axis_size("ctx"), lax.axis_size("exp")
    seq = rows * n_ctx
    own_rows = qkv_weight.shape[1]
    heads = HEADS // n_ctx
    part = heads * HEAD_DIM
    capacity = rows * TOP // n_exp + max(1, rows * TOP // (16 * n_exp))
    slots = n_exp * capacity
    section = lax.axis_index("section")
    ctx = lax.axis_index("ctx")
    first = section == 0

    def both(mine):
        other = lax.ppermute(mine, "section", [(0, 1), (1, 0)])
        return jnp.where(first, mine, other), jnp.where(first, other, mine)

    small = jnp.concatenate(
        [attn_gain[0], moe_gain[0], rel_bias[0], router_weight[0].reshape(-1)]
    )
    n_small = small.shape[0]
    columns = qkv_weight[0].reshape(own_rows, 3, n_ctx, part).transpose(2, 0, 1, 3)
    columns = columns.reshape(n_ctx, own_rows, 3 * part)
    small_row = jnp.pad(small, (0, 3 * part - n_small))
    small_rows = jnp.broadcast_to(small_row, (n_ctx, 1, 3 * part))
    columns = jnp.concatenate([columns, small_rows], 1)
    columns = jnp.pad(columns, ((0, 0), (0, 15 - own_rows), (0, 0)))
    columns = lax.all_to_all(columns, "ctx", 0, 0, tiled=True)
    columns = lax.all_gather(columns.reshape(n_ctx * 16, 3 * part), "exp", axis=0)
    out_rows = lax.all_gather(jnp.pad(out_weight[0], ((0, 4), (0, 0))), "exp", axis=0)

    def dense(columns, out_rows):
        columns = columns.reshape(n_exp, n_ctx, 16, 3 * part).transpose(1, 0, 2, 3)
        w_qkv = columns[:, :, :own_rows].reshape(width, 3 * part)
        w_out = out_rows[:, :own_rows].reshape(part, width)
        small = columns[:, :, own_rows, :n_small]
        gain_one = small[:, :, :own_rows].reshape(width).astype(F32)
        gain_two = small[:, :, own_rows : 2 * own_rows].reshape(width).astype(F32)
        n_bias = BUCKETS * HEADS // (n_ctx * n_exp)
        table = small[:, :, 2 * own_rows : 2 * own_rows + n_bias].reshape(BUCKETS, HEADS)
        table = lax.dynamic_slice_in_dim(table, ctx * heads, heads, 1)
        router = small[:, :, 2 * own_rows + n_bias :].reshape(width, n_exp)
        return w_qkv, w_out, gain_one, gain_two, bias_tiles(table, seq), router

    weights = [
        (*dense(c, o), w_in, w_out)
        for c, o, w_in, w_out in zip(
            both(columns), both(out_rows), both(expert_in[0, 0]), both(expert_out[0, 0])
        )
    ]
    ahead = block_order[:, None] - block_order[None, :]
    kind = jnp.repeat(jnp.where(ahead < 0, -1, jnp.minimum(ahead, 3)), SPAN, 1)

    own_routes = routes[0, :, 0]
    kept = jnp.where(first, own_routes[0], own_routes[1])
    given = jnp.where(first, own_routes[1], own_routes[0])
    taken = lax.ppermute(given, "section", [(0, 1), (1, 0)])
    layer_routes = (jnp.where(first, kept, taken), jnp.where(first, taken, kept))
    tables = [slot_tables(r, n_exp, capacity) for r in layer_routes]

    def forward(x, layer):
        w_qkv, w_out, gain_one, gain_two, tiles, router, w_in, w_back = weights[layer]
        route_hot, slot_hot = tables[layer]
        normed = ctx_gather(norm(x, gain_one), 0).reshape(seq, width)
        proj = mm(normed, w_qkv).astype(BF16)
        attended = attend(proj, tiles, kind)
        branch = mm(attended, w_out).astype(BF16).reshape(n_ctx, rows, width)
        middle = x + ctx_scatter(branch, F32, 1)
        mixed = norm(middle, gain_two)
        logits = mm(mixed, router)
        chosen = [jnp.sum(h * logits, -1, keepdims=True) for h in route_hot]
        peak = jnp.maximum(chosen[0], chosen[1])
        raised = [jnp.exp(c - peak) for c in chosen]
        gates = [r / (raised[0] + raised[1]) for r in raised]
        placing = slot_hot[0] + slot_hot[1]
        outgoing = mm_tn(placing, mixed).astype(BF16).reshape(n_exp, capacity, width)
        entering = exp_swap(outgoing).reshape(slots, width)
        entering = ctx_gather(entering, 2).reshape(n_ctx * slots, width)
        pre = mm(entering, w_in)
        hidden = gelu_parts(pre)[0].astype(BF16)
        leaving = mm_nt(hidden, w_back).astype(BF16).reshape(n_ctx, slots, width)
        leaving = ctx_scatter(leaving, BF16, 3).reshape(n_exp, capacity, width)
        returned = exp_swap(leaving).reshape(slots, width)
        picked = [mm(h, returned) for h in slot_hot]
        y = middle + gates[0] * picked[0] + gates[1] * picked[1]
        keep = (x, normed, proj, attended, middle, mixed, gates, picked, entering, pre)
        return y, keep

    def backward(g, keep, layer):
        x, normed, proj, attended, middle, mixed, gates, picked, entering, pre = keep
        w_qkv, w_out, gain_one, gain_two, tiles, router, w_in, w_back = weights[layer]
        route_hot, slot_hot = tables[layer]
        dreturned = mm_tn(slot_hot[0], (gates[0] * g).astype(BF16)) + mm_tn(
            slot_hot[1], (gates[1] * g).astype(BF16)
        )
        dreturned = dreturned.astype(BF16).reshape(n_exp, capacity, width)
        darrived = exp_swap(dreturned).reshape(slots, width)
        darrived = ctx_gather(darrived, 2).reshape(n_ctx * slots, width)
        hidden, slope = gelu_parts(pre)
        dpre = (mm(darrived, w_back) * slope).astype(BF16)
        dentering = mm_nt(dpre, w_in).astype(BF16).reshape(n_ctx, slots, width)
        dentering = ctx_scatter(dentering, BF16, 3).reshape(n_exp, capacity, width)
        dleft = exp_swap(dentering).reshape(slots, width)
        d_in = mm_tn(entering, dpre)
        d_back = mm_tn(darrived, hidden.astype(BF16))
        dgates = [jnp.sum(g * p, -1, keepdims=True) for p in picked]
        mean = gates[0] * dgates[0] + gates[1] * dgates[1]
        dchosen = [a * (b - mean) for a, b in zip(gates, dgates)]
        dlogits = route_hot[0] * dchosen[0] + route_hot[1] * dchosen[1]
        dlogits = dlogits.astype(BF16)
        d_router = mm_tn(mixed, dlogits)
        dmixed = mm(slot_hot[0] + slot_hot[1], dleft) + mm_nt(dlogits, router)
        dnorm, d_gain_two = norm_back(middle, gain_two, dmixed)
        dmiddle = g + dnorm
        dbranch = ctx_gather(dmiddle.astype(BF16), 0).reshape(seq, width)
        d_out = mm_tn(attended, dbranch)
        dattended = mm_nt(dbranch, w_out).astype(BF16)
        dproj, dtiles = attend_back(proj, dattended, tiles, kind)
        d_qkv = mm_tn(normed, dproj)
        dnormed = mm_nt(dproj, w_qkv).astype(BF16).reshape(n_ctx, rows, width)
        dnormed = ctx_scatter(dnormed, F32, 1)
        dnorm, d_gain_one = norm_back(x, gain_one, dnormed)
        d_table = bias_tiles_back(dtiles)
        full = jnp.zeros((BUCKETS, HEADS), F32)
        d_table = lax.dynamic_update_slice_in_dim(full, d_table, ctx * heads, 1)
        owners = (n_ctx * n_exp, -1)
        d_small = jnp.concatenate(
            [
                d_gain_one.reshape(owners),
                d_gain_two.reshape(owners),
                d_table.reshape(owners),
                d_router.reshape(owners),
            ],
            1,
        )
        return dmiddle + dnorm, (d_in, d_back, d_qkv, d_out, d_small)

    def swap(x):
        return lax.ppermute(x, "section", [(0, 1), (1, 0)])

    x = jnp.where(first, inputs[0, 0], inputs[1, 0]).astype(F32)
    cot = jnp.where(first, cotangent[0, 0], cotangent[1, 0]).astype(F32)
    y0, keep0 = forward(x, 0)
    h = y0.astype(BF16)
    y1, keep1 = forward(h.astype(F32), 1)
    top = y1.astype(BF16)
    dh, grads1 = backward(cot, keep1, 1)
    dh = dh.astype(BF16)
    sent1 = [lax.ppermute(p.astype(BF16), "section", [(0, 1)]) for p in grads1]
    dx, grads0 = backward(dh.astype(F32), keep0, 0)
    sent0 = [lax.ppermute(p.astype(BF16), "section", [(1, 0)]) for p in grads0]
    d_in, d_back, d_qkv, d_out, d_small = [
        jnp.where(first, a, b) + (c.astype(F32) + d.astype(F32))
        for a, b, c, d in zip(grads0, grads1, sent0, sent1)
    ]

    d_qkv = d_qkv.reshape(n_ctx, n_exp, own_rows, 3 * part).transpose(1, 0, 2, 3)
    d_small = d_small.reshape(n_ctx, n_exp, -1).transpose(1, 0, 2)
    d_small = jnp.pad(d_small, ((0, 0), (0, 0), (0, 3 * part - n_small)))
    pieces = jnp.concatenate([d_qkv, d_small[:, :, None]], 2).astype(BF16)
    pieces = jnp.sum(exp_swap(pieces).astype(F32), 0)
    pieces = lax.all_to_all(pieces, "ctx", 0, 0, tiled=True)
    qkv_grad = pieces[:, :own_rows].reshape(n_ctx, own_rows, 3, part)
    qkv_grad = qkv_grad.transpose(1, 2, 0, 3).reshape(own_rows, 3 * width)
    small = jnp.sum(pieces[:, own_rows, :n_small], 0)
    n_bias = BUCKETS * HEADS // (n_ctx * n_exp)
    out_grad = exp_swap(d_out.reshape(n_exp, own_rows, width).astype(BF16))
    out_grad = jnp.sum(out_grad.astype(F32), 0)

    other = swap(jnp.where(first, top, h))
    layer_out = jnp.where(
        first, jnp.stack([h, other]), jnp.stack([other, top])
    ).reshape(1, 2, 1, rows, width)
    dh = dh.astype(F32)
    other = swap(jnp.where(first, dh, dx))
    input_grad = jnp.where(
        first, jnp.stack([dx, other]), jnp.stack([other, dh])
    ).reshape(1, 2, 1, rows, width)
    return (
        layer_out,
        input_grad,
        small[:own_rows][None],
        qkv_grad[None],
        out_grad[None],
        small[2 * own_rows : 2 * own_rows + n_bias][None],
        small[own_rows : 2 * own_rows][None],
        small[2 * own_rows + n_bias :].reshape(1, own_rows, n_exp),
        d_in[None, None],
        d_back[None, None],
    )


def solution(mesh):
    return jax.shard_map(
        on_device,
        mesh=mesh,
        in_specs=(
            P(None, "exp", "ctx", None),
            P(None, "exp", "ctx", None),
            P("section", None, "exp", "ctx", None),
            P(),
            P("section", ("ctx", "exp")),
            P("section", ("ctx", "exp"), None),
            P("section", ("ctx", "exp"), None),
            P("section", ("ctx", "exp")),
            P("section", ("ctx", "exp")),
            P("section", ("ctx", "exp"), None),
            P("section", "exp", None, "ctx"),
            P("section", "exp", None, "ctx"),
        ),
        out_specs=(
            P("section", None, "exp", "ctx", None),
            P("section", None, "exp", "ctx", None),
            P("section", ("ctx", "exp")),
            P("section", ("ctx", "exp"), None),
            P("section", ("ctx", "exp"), None),
            P("section", ("ctx", "exp")),
            P("section", ("ctx", "exp")),
            P("section", ("ctx", "exp"), None),
            P("section", "exp", None, "ctx"),
            P("section", "exp", None, "ctx"),
        ),
        check_vma=False,
    )
```

```python
import functools
import math

import jax
import jax.numpy as jnp
import numpy as np
from jax import lax
from jax.experimental import pallas as pl
from jax.experimental.pallas import tpu as pltpu
from jax.sharding import PartitionSpec as P

HEADS = 12
HEAD_DIM = 64
BUCKETS = 32
REACH = 128
TOP = 2
EPS = 1e-06
NEG = -1e30
SPAN = 64
KINDS = 4
MESH = pl.DeviceIdType.MESH
BF16 = jnp.bfloat16
F32 = jnp.float32
GELU_C = math.sqrt(2.0 / math.pi)


def dot(a, b, dims):
    return lax.dot_general(a, b, (dims, ((), ())), preferred_element_type=F32)


def mm(a, b):
    return dot(a, b, ((1,), (0,)))


def mm_nt(a, b):
    return dot(a, b, ((1,), (1,)))


def mm_tn(a, b):
    return dot(a, b, ((0,), (0,)))


def meet_neighbours(axis, count):
    me = lax.axis_index(axis)
    right, left = lax.rem(me + 1, count), lax.rem(me + count - 1, count)
    barrier = pltpu.get_barrier_semaphore()
    for neighbour in (left, right):
        pl.semaphore_signal(barrier, inc=1, device_id={axis: neighbour}, device_id_type=MESH)
    pl.semaphore_wait(barrier, 2)
    return me, right, left


def remote(src, dst, send, recv, k, axis, to):
    return pltpu.make_async_remote_copy(
        src_ref=src,
        dst_ref=dst,
        send_sem=send.at[k],
        recv_sem=recv.at[k],
        device_id={axis: to},
        device_id_type=MESH,
    )


def halves(rows):
    first = (rows // 2 + 15) // 16 * 16
    return (pl.ds(0, first), pl.ds(first, rows - first))


def gather_kernel(axis, rows, x_ref, out_ref, send, recv, own_sem):
    me, right, left = meet_neighbours(axis, 4)
    low, high = halves(rows)
    own = pltpu.make_async_copy(x_ref, out_ref.at[me], own_sem)

    def step(k, src, slot, part, to):
        return remote(src.at[part], out_ref.at[slot, part], send, recv, k, axis, to)

    to_right_low = step(0, x_ref, me, low, right)
    to_left_high = step(1, x_ref, me, high, left)
    to_right_high = step(2, x_ref, me, high, right)
    to_left_low = step(3, x_ref, me, low, left)
    to_right_low.start()
    to_left_high.start()
    to_right_high.start()
    to_left_low.start()
    own.start()
    to_right_low.wait_recv()
    on_right = step(4, out_ref.at[left], left, low, right)
    on_right.start()
    to_left_high.wait_recv()
    on_left = step(5, out_ref.at[right], right, high, left)
    on_left.start()
    to_right_high.wait_recv()
    to_left_low.wait_recv()
    on_right.wait_recv()
    on_left.wait_recv()
    for c in (to_right_low, to_left_high, to_right_high, to_left_low, on_right, on_left):
        c.wait_send()
    own.wait()


def ctx_gather(x, cid):
    rows, width = x.shape
    return pl.pallas_call(
        functools.partial(gather_kernel, "ctx", rows),
        out_shape=jax.ShapeDtypeStruct((4, rows, width), x.dtype),
        in_specs=[pl.BlockSpec(memory_space=pltpu.VMEM)],
        out_specs=pl.BlockSpec(memory_space=pltpu.VMEM),
        scratch_shapes=[
            pltpu.SemaphoreType.DMA((6,)),
            pltpu.SemaphoreType.DMA((6,)),
            pltpu.SemaphoreType.DMA,
        ],
        compiler_params=pltpu.CompilerParams(
            collective_id=cid, has_side_effects=True, vmem_limit_bytes=16 << 20
        ),
    )(x)


def scatter_kernel(
    axis, rows, x_ref, out_ref, far_l, far_r, sum_l, sum_r, in_l, in_r, send, recv
):
    me, right, left = meet_neighbours(axis, 4)
    far = lax.rem(me + 2, 4)
    low, high = halves(rows)
    n_low = low.size
    n_high = high.size

    def step(k, src, dst, to):
        return remote(src, dst, send, recv, k, axis, to)

    a = step(0, x_ref.at[far, low], far_l, right)
    b = step(1, x_ref.at[far, high], far_r, left)
    c = step(2, x_ref.at[right, high], in_l.at[high], right)
    d = step(3, x_ref.at[left, low], in_r.at[low], left)
    a.start()
    b.start()
    c.start()
    d.start()
    a.wait_recv()
    sum_r[...] = (x_ref[right, :n_low, :].astype(F32) + far_l[...].astype(F32)).astype(BF16)
    e = step(4, sum_r, in_l.at[low], right)
    e.start()
    b.wait_recv()
    sum_l[...] = (x_ref[left, n_low:, :].astype(F32) + far_r[...].astype(F32)).astype(BF16)
    f = step(5, sum_l, in_r.at[high], left)
    f.start()
    c.wait_recv()
    d.wait_recv()
    e.wait_recv()
    f.wait_recv()
    out_ref[...] = (
        x_ref[me].astype(F32) + in_l[...].astype(F32) + in_r[...].astype(F32)
    ).astype(out_ref.dtype)
    for s in (a, b, c, d, e, f):
        s.wait_send()


def ctx_scatter(x, dtype, cid):
    _, rows, width = x.shape
    low, high = halves(rows)
    v = lambda n: pltpu.VMEM((n, width), BF16)
    return pl.pallas_call(
        functools.partial(scatter_kernel, "ctx", rows),
        out_shape=jax.ShapeDtypeStruct((rows, width), dtype),
        in_specs=[pl.BlockSpec(memory_space=pltpu.VMEM)],
        out_specs=pl.BlockSpec(memory_space=pltpu.VMEM),
        scratch_shapes=[
            v(low.size),
            v(high.size),
            v(high.size),
            v(low.size),
            v(rows),
            v(rows),
            pltpu.SemaphoreType.DMA((6,)),
            pltpu.SemaphoreType.DMA((6,)),
        ],
        compiler_params=pltpu.CompilerParams(
            collective_id=cid, has_side_effects=True, vmem_limit_bytes=16 << 20
        ),
    )(x)


PAD = 32


class Exchange:
    def __init__(self, src, dst, send, recv):
        self.src, self.dst, self.send, self.recv = src, dst, send, recv
        self.me, self.count = lax.axis_index("exp"), lax.axis_size("exp")

    def copy(self, k):
        peer = lax.rem(self.me + k, self.count)
        return remote(
            self.src.at[peer], self.dst.at[self.me], self.send, self.recv, k, "exp", peer
        )

    def each(self, act):
        def body(k, carry):
            act(self.copy(k))
            return carry

        lax.fori_loop(1, self.count, body, 0)

    def start(self):
        self.each(lambda c: c.start())
        self.dst[self.me] = self.src[self.me]

    def wait_recv(self):
        self.each(lambda c: c.wait_recv())

    def wait_send(self):
        self.each(lambda c: c.wait_send())


def meet_all():
    barrier = pltpu.get_barrier_semaphore()
    me, count = lax.axis_index("exp"), lax.axis_size("exp")

    def greet(k, carry):
        peer = lax.rem(me + k, count)
        pl.semaphore_signal(barrier, inc=1, device_id={"exp": peer}, device_id_type=MESH)
        return carry

    lax.fori_loop(1, count, greet, 0)
    ctx = lax.axis_index("ctx")
    right, left = lax.rem(ctx + 1, 4), lax.rem(ctx + 3, 4)
    for neighbour in (left, right):
        pl.semaphore_signal(barrier, inc=1, device_id={"ctx": neighbour}, device_id_type=MESH)
    pl.semaphore_wait(barrier, count + 1)
    return ctx, right, left


def run_experts(
    rows, out_ref, sel_ref, all_ref, ret_ref, block, beside_one, beside_two, scratch
):
    (inbox, part, far_l, far_r, sum_l, sum_r, in_l, in_r, res) = scratch[:9]
    s_in, r_in, s_out, r_out, s_ag, r_ag, s_rs, r_rs = scratch[9:]
    me, right, left = meet_all()
    far = lax.rem(me + 2, 4)
    low, high = halves(rows)
    n_low = low.size
    flat = inbox.shape[0] * inbox.shape[1]
    width = inbox.shape[2]

    arriving = Exchange(out_ref, inbox, s_in, r_in)
    arriving.start()
    arriving.wait_recv()
    all_ref[me] = mm(sel_ref[...], inbox[...].reshape(flat, width)).astype(BF16)

    def pass_on(k, slot, half, to):
        at = all_ref.at[slot, half]
        return remote(at, at, s_ag, r_ag, k, "ctx", to)

    to_right_low = pass_on(0, me, low, right)
    to_left_high = pass_on(1, me, high, left)
    to_right_high = pass_on(2, me, high, right)
    to_left_low = pass_on(3, me, low, left)
    on_right = pass_on(4, left, low, right)
    on_left = pass_on(5, right, high, left)
    to_right_low.start()
    to_left_high.start()
    to_right_high.start()
    to_left_low.start()

    def send(k, src, dst, to):
        return remote(src, dst, s_rs, r_rs, k, "ctx", to)

    a = send(0, part.at[far, low], far_l, right)
    b = send(1, part.at[far, high], far_r, left)
    c = send(2, part.at[right, high], in_l.at[high], right)
    d = send(3, part.at[left, low], in_r.at[low], left)
    e = send(4, sum_r, in_l.at[low], right)
    f = send(5, sum_l, in_r.at[high], left)

    block(me, part)
    to_right_low.wait_recv()
    on_right.start()
    to_left_high.wait_recv()
    on_left.start()
    to_right_high.wait_recv()
    block(left, part)
    d.start()
    to_left_low.wait_recv()
    block(right, part)
    c.start()
    on_right.wait_recv()
    on_left.wait_recv()
    block(far, part)
    a.start()
    b.start()
    beside_one()
    a.wait_recv()
    sum_r[...] = (part[right, :n_low, :].astype(F32) + far_l[...].astype(F32)).astype(BF16)
    e.start()
    b.wait_recv()
    sum_l[...] = (part[left, n_low:, :].astype(F32) + far_r[...].astype(F32)).astype(BF16)
    f.start()
    beside_two()
    for x in (c, d, e, f):
        x.wait_recv()
    total = part[me].astype(F32) + in_l[...].astype(F32) + in_r[...].astype(F32)
    padded = mm_tn(sel_ref[...], total.astype(BF16)).astype(BF16)
    res[...] = padded.reshape(res.shape)
    leaving = Exchange(res, ret_ref, s_out, r_out)
    leaving.start()
    leaving.wait_recv()
    for x in (to_right_low, to_left_high, to_right_high, to_left_low, on_right, on_left):
        x.wait_send()
    for x in (a, b, c, d, e, f):
        x.wait_send()
    arriving.wait_send()
    leaving.wait_send()


def expert_scratch(experts, rows, width):
    low, high = halves(rows)
    v = lambda *shape: pltpu.VMEM((*shape, width), BF16)
    return [
        v(experts, PAD),
        v(4, rows),
        v(low.size),
        v(high.size),
        v(high.size),
        v(low.size),
        v(rows),
        v(rows),
        v(experts, PAD),
        *[pltpu.SemaphoreType.DMA((experts,))] * 4,
        *[pltpu.SemaphoreType.DMA((6,))] * 4,
    ]


def experts_kernel(rows, out_ref, sel_ref, w_in, w_back, ret_ref, all_ref, pre_ref, *scratch):
    def block(j, part):
        pre = mm(all_ref[j], w_in[...])
        pre_ref[j] = pre
        hidden = gelu_parts(pre)[0].astype(BF16)
        part[j] = mm_nt(hidden, w_back[...]).astype(BF16)

    nothing = lambda: None
    run_experts(rows, out_ref, sel_ref, all_ref, ret_ref, block, nothing, nothing, scratch)


def experts_back_kernel(
    rows, out_ref, sel_ref, w_in, w_back, ent_ref, pre_ref, ret_ref, d_in, d_back,
    all_ref, hid_ref, dpre_ref, *scratch
):
    width = w_in.shape[0]

    def block(j, part):
        hidden, slope = gelu_parts(pre_ref[j])
        hid_ref[j] = hidden.astype(BF16)
        dpre = (mm(all_ref[j], w_back[...]) * slope).astype(BF16)
        dpre_ref[j] = dpre
        part[j] = mm_nt(dpre, w_in[...]).astype(BF16)

    def flat(ref):
        return ref[...].reshape(4 * rows, ref.shape[2])

    def beside_one():
        d_back[...] = mm_tn(flat(all_ref), flat(hid_ref))

    def beside_two():
        d_in[...] = mm_tn(flat(ent_ref), flat(dpre_ref))

    run_experts(rows, out_ref, sel_ref, all_ref, ret_ref, block, beside_one, beside_two, scratch)


def selection(experts, capacity):
    sel = np.zeros((experts * capacity, experts, PAD), np.float32)
    for e in range(experts):
        for s in range(capacity):
            sel[e * capacity + s, e, s] = 1
    return jnp.asarray(sel.reshape(experts * capacity, experts * PAD), BF16)


def experts_forward(outgoing, sel, w_in, w_back):
    experts, _, width = outgoing.shape
    rows = sel.shape[0]
    vm = pl.BlockSpec(memory_space=pltpu.VMEM)
    return pl.pallas_call(
        functools.partial(experts_kernel, rows),
        out_shape=(
            jax.ShapeDtypeStruct(outgoing.shape, BF16),
            jax.ShapeDtypeStruct((4, rows, width), BF16),
            jax.ShapeDtypeStruct((4, rows, w_in.shape[1]), F32),
        ),
        in_specs=[vm] * 4,
        out_specs=(vm,) * 3,
        scratch_shapes=expert_scratch(experts, rows, width),
        compiler_params=pltpu.CompilerParams(
            collective_id=2, has_side_effects=True, vmem_limit_bytes=48 << 20
        ),
    )(outgoing, sel, w_in, w_back)


def experts_backward(outgoing, sel, w_in, w_back, entering, pre):
    experts, _, width = outgoing.shape
    rows, hid = sel.shape[0], w_in.shape[1]
    vm = pl.BlockSpec(memory_space=pltpu.VMEM)
    return pl.pallas_call(
        functools.partial(experts_back_kernel, rows),
        out_shape=(
            jax.ShapeDtypeStruct(outgoing.shape, BF16),
            jax.ShapeDtypeStruct(w_in.shape, F32),
            jax.ShapeDtypeStruct(w_back.shape, F32),
        ),
        in_specs=[vm] * 6,
        out_specs=(vm,) * 3,
        scratch_shapes=[
            pltpu.VMEM((4, rows, width), BF16),
            pltpu.VMEM((4, rows, hid), BF16),
            pltpu.VMEM((4, rows, hid), BF16),
            *expert_scratch(experts, rows, width),
        ],
        compiler_params=pltpu.CompilerParams(
            collective_id=3, has_side_effects=True, vmem_limit_bytes=48 << 20
        ),
    )(outgoing, sel, w_in, w_back, entering, pre)


def bias_rows(tiles_ref, kind_ref, head, block):
    kind = kind_ref[block : block + 1, :]
    rows = jnp.where(kind == 3, tiles_ref[head, 3], NEG)
    for k in (2, 1, 0):
        rows = jnp.where(kind == k, tiles_ref[head, k], rows)
    return rows


def attend_kernel(heads, proj_ref, tiles_ref, kind_ref, out_ref, s_ref, p_ref):
    width = heads * HEAD_DIM
    seq = proj_ref.shape[0]
    parts = []
    for h in range(heads):
        q = proj_ref[:, h * HEAD_DIM : (h + 1) * HEAD_DIM]
        k = proj_ref[:, width + h * HEAD_DIM : width + (h + 1) * HEAD_DIM]
        v = proj_ref[:, 2 * width + h * HEAD_DIM : 2 * width + (h + 1) * HEAD_DIM]
        s_ref[...] = mm_nt(q, k)
        for b in range(seq // SPAN):
            at = slice(b * SPAN, (b + 1) * SPAN)
            s = s_ref[at, :] * HEAD_DIM**-0.5 + bias_rows(tiles_ref, kind_ref, h, b)
            e = jnp.exp(s - jnp.max(s, -1, keepdims=True))
            p_ref[at, :] = (e * (1.0 / jnp.sum(e, -1, keepdims=True))).astype(BF16)
        parts.append(mm(p_ref[...], v).astype(BF16))
    out_ref[...] = jnp.concatenate(parts, 1)


def attend(proj, tiles, kind):
    seq, width = proj.shape
    heads = width // (3 * HEAD_DIM)
    vm = pl.BlockSpec(memory_space=pltpu.VMEM)
    return pl.pallas_call(
        functools.partial(attend_kernel, heads),
        out_shape=jax.ShapeDtypeStruct((seq, width // 3), BF16),
        in_specs=[vm] * 3,
        out_specs=vm,
        scratch_shapes=[pltpu.VMEM((seq, seq), F32), pltpu.VMEM((seq, seq), BF16)],
        compiler_params=pltpu.CompilerParams(vmem_limit_bytes=32 << 20),
    )(proj, tiles, kind)


def attend_back_kernel(
    heads, proj_ref, da_ref, tiles_ref, kind_ref, dproj_ref, dtiles_ref, s_ref, dp_ref, p_ref, ds_ref
):
    width = heads * HEAD_DIM
    seq = proj_ref.shape[0]
    scale = HEAD_DIM**-0.5
    dq, dk, dv = [], [], []
    for h in range(heads):
        q = proj_ref[:, h * HEAD_DIM : (h + 1) * HEAD_DIM]
        k = proj_ref[:, width + h * HEAD_DIM : width + (h + 1) * HEAD_DIM]
        v = proj_ref[:, 2 * width + h * HEAD_DIM : 2 * width + (h + 1) * HEAD_DIM]
        da = da_ref[:, h * HEAD_DIM : (h + 1) * HEAD_DIM]
        s_ref[...] = mm_nt(q, k)
        dp_ref[...] = mm_nt(da, v)
        dtiles_ref[h] = jnp.zeros(dtiles_ref.shape[1:], F32)
        for b in range(seq // SPAN):
            at = slice(b * SPAN, (b + 1) * SPAN)
            s = s_ref[at, :] * scale + bias_rows(tiles_ref, kind_ref, h, b)
            e = jnp.exp(s - jnp.max(s, -1, keepdims=True))
            p = e * (1.0 / jnp.sum(e, -1, keepdims=True))
            dp = dp_ref[at, :]
            ds = p * (dp - jnp.sum(p * dp, -1, keepdims=True))
            p_ref[at, :] = p.astype(BF16)
            ds_ref[at, :] = ds.astype(BF16)
            kind = kind_ref[b : b + 1, :]
            for n in range(KINDS):
                dtiles_ref[h, n] += jnp.where(kind == n, ds, 0.0)
        p = p_ref[...]
        ds = ds_ref[...]
        dq.append((mm(ds, k) * scale).astype(BF16))
        dk.append((mm_tn(ds, q) * scale).astype(BF16))
        dv.append(mm_tn(p, da).astype(BF16))
    dproj_ref[...] = jnp.concatenate(dq + dk + dv, 1)


def attend_back(proj, da, tiles, kind):
    seq, width = proj.shape
    heads = width // (3 * HEAD_DIM)
    vm = pl.BlockSpec(memory_space=pltpu.VMEM)
    return pl.pallas_call(
        functools.partial(attend_back_kernel, heads),
        out_shape=(
            jax.ShapeDtypeStruct((seq, width), BF16),
            jax.ShapeDtypeStruct(tiles.shape, F32),
        ),
        in_specs=[vm] * 4,
        out_specs=(vm, vm),
        scratch_shapes=[
            pltpu.VMEM((seq, seq), F32),
            pltpu.VMEM((seq, seq), F32),
            pltpu.VMEM((seq, seq), BF16),
            pltpu.VMEM((seq, seq), BF16),
        ],
        compiler_params=pltpu.CompilerParams(vmem_limit_bytes=32 << 20),
    )(proj, da, tiles, kind)


def bucket_of(distance):
    half = BUCKETS // 2
    powers = np.arange(1, BUCKETS - half) / (BUCKETS - half)
    bounds = np.ceil(half * (REACH / half) ** powers).astype(np.int32)
    n = np.maximum(distance, 0)
    return np.minimum(n, half) + (n[..., None] >= bounds).sum(-1)


def tile_buckets():
    row, col = np.arange(SPAN)[:, None], np.arange(SPAN)[None, :]
    return np.stack([bucket_of(k * SPAN + row - col) for k in range(KINDS)])


def bias_tiles(table, seq):
    hot = (tile_buckets()[..., None] == np.arange(BUCKETS)).astype(np.float32)
    hot = jnp.asarray(hot.reshape(KINDS * SPAN * SPAN, BUCKETS), BF16)
    tiles = mm_nt(table.T.astype(BF16), hot).reshape(-1, KINDS, SPAN, SPAN)
    row, col = np.arange(SPAN)[:, None], np.arange(SPAN)[None, :]
    unseen = np.zeros((KINDS, SPAN, SPAN), bool)
    unseen[0] = row < col
    tiles = jnp.where(jnp.asarray(unseen), NEG, tiles)
    return jnp.tile(tiles, (1, 1, 1, seq // SPAN))


def bias_tiles_back(dtiles):
    heads, kinds, span, seq = dtiles.shape
    hot = (tile_buckets()[..., None] == np.arange(BUCKETS)).astype(np.float32)
    hot = jnp.asarray(hot.reshape(KINDS * SPAN * SPAN, BUCKETS), BF16)
    sums = jnp.sum(dtiles.reshape(heads, kinds, span, seq // span, span), 3)
    sums = sums.reshape(heads, -1)
    high = sums.astype(BF16)
    low = (sums - high.astype(F32)).astype(BF16)
    return (mm(high, hot) + mm(low, hot)).T


def norm_scale(v):
    return lax.rsqrt(jnp.mean(v * v, -1, keepdims=True) + EPS)


def norm(v, gain):
    return (v * norm_scale(v) * gain).astype(BF16)


def norm_back(v, gain, du):
    r = norm_scale(v)
    dug = du * gain
    dv = r * dug - v * (r * r * r) * jnp.mean(dug * v, -1, keepdims=True)
    return dv, jnp.sum(du * v * r, 0)


def gelu_parts(v):
    t = jnp.tanh(GELU_C * (v + 0.044715 * v * v * v))
    value = 0.5 * v * (1.0 + t)
    slope = 0.5 * (1.0 + t) + 0.5 * v * (1.0 - t * t) * GELU_C * (1.0 + 3 * 0.044715 * v * v)
    return value, slope


def slot_tables(routes, experts):
    rows = routes.shape[0]
    flat = routes.reshape(rows * TOP)
    hot = flat[:, None] == jnp.arange(experts, dtype=jnp.int32)
    before = np.tril(np.ones((rows * TOP, rows * TOP), np.float32), -1)
    earlier = mm(jnp.asarray(before, BF16), hot.astype(BF16))
    slot = jnp.sum(jnp.where(hot, earlier, 0.0), -1).astype(jnp.int32)
    target = (flat * PAD + slot).reshape(rows, TOP)
    slots = jnp.arange(experts * PAD, dtype=jnp.int32)
    slot_hot = [(target[:, c : c + 1] == slots).astype(BF16) for c in range(TOP)]
    route_hot = [(routes[:, c : c + 1] == jnp.arange(experts)).astype(F32) for c in range(TOP)]
    return route_hot, slot_hot


def exp_swap(x):
    return lax.all_to_all(x, "exp", split_axis=0, concat_axis=0, tiled=True)


def on_device(
    inputs,
    cotangent,
    routes,
    block_order,
    attn_gain,
    qkv_weight,
    out_weight,
    rel_bias,
    moe_gain,
    router_weight,
    expert_in,
    expert_out,
):
    rows, width = inputs.shape[2:]
    n_ctx, n_exp = lax.axis_size("ctx"), lax.axis_size("exp")
    seq = rows * n_ctx
    own_rows = qkv_weight.shape[1]
    heads = HEADS // n_ctx
    part = heads * HEAD_DIM
    capacity = rows * TOP // n_exp + max(1, rows * TOP // (16 * n_exp))
    slots = n_exp * PAD
    sel = selection(n_exp, capacity)
    section = lax.axis_index("section")
    ctx = lax.axis_index("ctx")
    first = section == 0

    def both(mine):
        other = lax.ppermute(mine, "section", [(0, 1), (1, 0)])
        return jnp.where(first, mine, other), jnp.where(first, other, mine)

    small = jnp.concatenate(
        [attn_gain[0], moe_gain[0], rel_bias[0], router_weight[0].reshape(-1)]
    )
    n_small = small.shape[0]
    columns = qkv_weight[0].reshape(own_rows, 3, n_ctx, part).transpose(2, 0, 1, 3)
    columns = columns.reshape(n_ctx, own_rows, 3 * part)
    small_row = jnp.pad(small, (0, 3 * part - n_small))
    small_rows = jnp.broadcast_to(small_row, (n_ctx, 1, 3 * part))
    columns = jnp.concatenate([columns, small_rows], 1)
    columns = jnp.pad(columns, ((0, 0), (0, 15 - own_rows), (0, 0)))
    columns = lax.all_to_all(columns, "ctx", 0, 0, tiled=True)
    columns = lax.all_gather(columns.reshape(n_ctx * 16, 3 * part), "exp", axis=0)
    out_rows = lax.all_gather(jnp.pad(out_weight[0], ((0, 4), (0, 0))), "exp", axis=0)

    def dense(columns, out_rows):
        columns = columns.reshape(n_exp, n_ctx, 16, 3 * part).transpose(1, 0, 2, 3)
        w_qkv = columns[:, :, :own_rows].reshape(width, 3 * part)
        w_out = out_rows[:, :own_rows].reshape(part, width)
        small = columns[:, :, own_rows, :n_small]
        gain_one = small[:, :, :own_rows].reshape(width).astype(F32)
        gain_two = small[:, :, own_rows : 2 * own_rows].reshape(width).astype(F32)
        n_bias = BUCKETS * HEADS // (n_ctx * n_exp)
        table = small[:, :, 2 * own_rows : 2 * own_rows + n_bias].reshape(BUCKETS, HEADS)
        table = lax.dynamic_slice_in_dim(table, ctx * heads, heads, 1)
        router = small[:, :, 2 * own_rows + n_bias :].reshape(width, n_exp)
        return w_qkv, w_out, gain_one, gain_two, bias_tiles(table, seq), router

    weights = [
        (*dense(c, o), w_in, w_out)
        for c, o, w_in, w_out in zip(
            both(columns), both(out_rows), both(expert_in[0, 0]), both(expert_out[0, 0])
        )
    ]
    ahead = block_order[:, None] - block_order[None, :]
    kind = jnp.repeat(jnp.where(ahead < 0, -1, jnp.minimum(ahead, 3)), SPAN, 1)

    own_routes = routes[0, :, 0]
    kept = jnp.where(first, own_routes[0], own_routes[1])
    given = jnp.where(first, own_routes[1], own_routes[0])
    taken = lax.ppermute(given, "section", [(0, 1), (1, 0)])
    layer_routes = (jnp.where(first, kept, taken), jnp.where(first, taken, kept))
    tables = [slot_tables(r, n_exp) for r in layer_routes]

    def forward(x, layer):
        w_qkv, w_out, gain_one, gain_two, tiles, router, w_in, w_back = weights[layer]
        route_hot, slot_hot = tables[layer]
        normed = ctx_gather(norm(x, gain_one), 0).reshape(seq, width)
        proj = mm(normed, w_qkv).astype(BF16)
        attended = attend(proj, tiles, kind)
        branch = mm(attended, w_out).astype(BF16).reshape(n_ctx, rows, width)
        middle = x + ctx_scatter(branch, F32, 1)
        mixed = norm(middle, gain_two)
        logits = mm(mixed, router)
        chosen = [jnp.sum(h * logits, -1, keepdims=True) for h in route_hot]
        peak = jnp.maximum(chosen[0], chosen[1])
        raised = [jnp.exp(c - peak) for c in chosen]
        gates = [r / (raised[0] + raised[1]) for r in raised]
        placing = slot_hot[0] + slot_hot[1]
        outgoing = mm_tn(placing, mixed).astype(BF16).reshape(n_exp, PAD, width)
        returned, entering, pre = experts_forward(outgoing, sel, w_in, w_back)
        returned = returned.reshape(slots, width)
        picked = [mm(h, returned) for h in slot_hot]
        y = middle + gates[0] * picked[0] + gates[1] * picked[1]
        keep = (x, normed, proj, attended, middle, mixed, gates, picked, entering, pre)
        return y, keep

    def backward(g, keep, layer):
        x, normed, proj, attended, middle, mixed, gates, picked, entering, pre = keep
        w_qkv, w_out, gain_one, gain_two, tiles, router, w_in, w_back = weights[layer]
        route_hot, slot_hot = tables[layer]
        dreturned = mm_tn(slot_hot[0], (gates[0] * g).astype(BF16)) + mm_tn(
            slot_hot[1], (gates[1] * g).astype(BF16)
        )
        dreturned = dreturned.astype(BF16).reshape(n_exp, PAD, width)
        dleft, d_in, d_back = experts_backward(dreturned, sel, w_in, w_back, entering, pre)
        dleft = dleft.reshape(slots, width)
        dgates = [jnp.sum(g * p, -1, keepdims=True) for p in picked]
        mean = gates[0] * dgates[0] + gates[1] * dgates[1]
        dchosen = [a * (b - mean) for a, b in zip(gates, dgates)]
        dlogits = route_hot[0] * dchosen[0] + route_hot[1] * dchosen[1]
        dlogits = dlogits.astype(BF16)
        d_router = mm_tn(mixed, dlogits)
        dmixed = mm(slot_hot[0] + slot_hot[1], dleft) + mm_nt(dlogits, router)
        dnorm, d_gain_two = norm_back(middle, gain_two, dmixed)
        dmiddle = g + dnorm
        dbranch = ctx_gather(dmiddle.astype(BF16), 0).reshape(seq, width)
        d_out = mm_tn(attended, dbranch)
        dattended = mm_nt(dbranch, w_out).astype(BF16)
        dproj, dtiles = attend_back(proj, dattended, tiles, kind)
        d_qkv = mm_tn(normed, dproj)
        dnormed = mm_nt(dproj, w_qkv).astype(BF16).reshape(n_ctx, rows, width)
        dnormed = ctx_scatter(dnormed, F32, 1)
        dnorm, d_gain_one = norm_back(x, gain_one, dnormed)
        d_table = bias_tiles_back(dtiles)
        full = jnp.zeros((BUCKETS, HEADS), F32)
        d_table = lax.dynamic_update_slice_in_dim(full, d_table, ctx * heads, 1)
        owners = (n_ctx * n_exp, -1)
        d_small = jnp.concatenate(
            [
                d_gain_one.reshape(owners),
                d_gain_two.reshape(owners),
                d_table.reshape(owners),
                d_router.reshape(owners),
            ],
            1,
        )
        return dmiddle + dnorm, (d_in, d_back, d_qkv, d_out, d_small)

    def swap(x):
        return lax.ppermute(x, "section", [(0, 1), (1, 0)])

    x = jnp.where(first, inputs[0, 0], inputs[1, 0]).astype(F32)
    cot = jnp.where(first, cotangent[0, 0], cotangent[1, 0]).astype(F32)
    y0, keep0 = forward(x, 0)
    h = y0.astype(BF16)
    y1, keep1 = forward(h.astype(F32), 1)
    top = y1.astype(BF16)
    dh, grads1 = backward(cot, keep1, 1)
    dh = dh.astype(BF16)
    sent1 = [lax.ppermute(p.astype(BF16), "section", [(0, 1)]) for p in grads1]
    dx, grads0 = backward(dh.astype(F32), keep0, 0)
    sent0 = [lax.ppermute(p.astype(BF16), "section", [(1, 0)]) for p in grads0]
    d_in, d_back, d_qkv, d_out, d_small = [
        jnp.where(first, a, b) + (c.astype(F32) + d.astype(F32))
        for a, b, c, d in zip(grads0, grads1, sent0, sent1)
    ]

    d_qkv = d_qkv.reshape(n_ctx, n_exp, own_rows, 3 * part).transpose(1, 0, 2, 3)
    d_small = d_small.reshape(n_ctx, n_exp, -1).transpose(1, 0, 2)
    d_small = jnp.pad(d_small, ((0, 0), (0, 0), (0, 3 * part - n_small)))
    pieces = jnp.concatenate([d_qkv, d_small[:, :, None]], 2).astype(BF16)
    pieces = jnp.sum(exp_swap(pieces).astype(F32), 0)
    pieces = lax.all_to_all(pieces, "ctx", 0, 0, tiled=True)
    qkv_grad = pieces[:, :own_rows].reshape(n_ctx, own_rows, 3, part)
    qkv_grad = qkv_grad.transpose(1, 2, 0, 3).reshape(own_rows, 3 * width)
    small = jnp.sum(pieces[:, own_rows, :n_small], 0)
    n_bias = BUCKETS * HEADS // (n_ctx * n_exp)
    out_grad = exp_swap(d_out.reshape(n_exp, own_rows, width).astype(BF16))
    out_grad = jnp.sum(out_grad.astype(F32), 0)

    other = swap(jnp.where(first, top, h))
    layer_out = jnp.where(
        first, jnp.stack([h, other]), jnp.stack([other, top])
    ).reshape(1, 2, 1, rows, width)
    dh = dh.astype(F32)
    other = swap(jnp.where(first, dh, dx))
    input_grad = jnp.where(
        first, jnp.stack([dx, other]), jnp.stack([other, dh])
    ).reshape(1, 2, 1, rows, width)
    return (
        layer_out,
        input_grad,
        small[:own_rows][None],
        qkv_grad[None],
        out_grad[None],
        small[2 * own_rows : 2 * own_rows + n_bias][None],
        small[own_rows : 2 * own_rows][None],
        small[2 * own_rows + n_bias :].reshape(1, own_rows, n_exp),
        d_in[None, None],
        d_back[None, None],
    )


def solution(mesh):
    return jax.shard_map(
        on_device,
        mesh=mesh,
        in_specs=(
            P(None, "exp", "ctx", None),
            P(None, "exp", "ctx", None),
            P("section", None, "exp", "ctx", None),
            P(),
            P("section", ("ctx", "exp")),
            P("section", ("ctx", "exp"), None),
            P("section", ("ctx", "exp"), None),
            P("section", ("ctx", "exp")),
            P("section", ("ctx", "exp")),
            P("section", ("ctx", "exp"), None),
            P("section", "exp", None, "ctx"),
            P("section", "exp", None, "ctx"),
        ),
        out_specs=(
            P("section", None, "exp", "ctx", None),
            P("section", None, "exp", "ctx", None),
            P("section", ("ctx", "exp")),
            P("section", ("ctx", "exp"), None),
            P("section", ("ctx", "exp"), None),
            P("section", ("ctx", "exp")),
            P("section", ("ctx", "exp")),
            P("section", ("ctx", "exp"), None),
            P("section", "exp", None, "ctx"),
            P("section", "exp", None, "ctx"),
        ),
        check_vma=False,
    )
```

```python
import functools
import math

import jax
import jax.numpy as jnp
import numpy as np
from jax import lax
from jax.experimental import pallas as pl
from jax.experimental.pallas import tpu as pltpu
from jax.sharding import PartitionSpec as P

HEADS = 12
HEAD_DIM = 64
BUCKETS = 32
REACH = 128
TOP = 2
EPS = 1e-06
NEG = -1e30
SPAN = 64
KINDS = 4
MESH = pl.DeviceIdType.MESH
BF16 = jnp.bfloat16
F32 = jnp.float32
GELU_C = math.sqrt(2.0 / math.pi)


def dot(a, b, dims):
    return lax.dot_general(a, b, (dims, ((), ())), preferred_element_type=F32)


def mm(a, b):
    return dot(a, b, ((1,), (0,)))


def mm_nt(a, b):
    return dot(a, b, ((1,), (1,)))


def mm_tn(a, b):
    return dot(a, b, ((0,), (0,)))


def meet_neighbours(axis, count):
    me = lax.axis_index(axis)
    right, left = lax.rem(me + 1, count), lax.rem(me + count - 1, count)
    barrier = pltpu.get_barrier_semaphore()
    for neighbour in (left, right):
        pl.semaphore_signal(barrier, inc=1, device_id={axis: neighbour}, device_id_type=MESH)
    pl.semaphore_wait(barrier, 2)
    return me, right, left


def remote(src, dst, send, recv, k, axis, to):
    return pltpu.make_async_remote_copy(
        src_ref=src,
        dst_ref=dst,
        send_sem=send.at[k],
        recv_sem=recv.at[k],
        device_id={axis: to},
        device_id_type=MESH,
    )


def halves(rows):
    first = (rows // 2 + 15) // 16 * 16
    return (pl.ds(0, first), pl.ds(first, rows - first))


def ring_copy(send, recv, k, src, dst, to):
    return remote(src, dst, send, recv, k, "ctx", to)


class RingGather:
    def __init__(self, all_ref, rows, ids, send, recv):
        me, right, left = ids
        low, high = halves(rows)

        def pass_on(k, slot, half, to):
            at = all_ref.at[slot, half]
            return ring_copy(send, recv, k, at, at, to)

        self.first = (
            pass_on(0, me, low, right),
            pass_on(1, me, high, left),
            pass_on(2, me, high, right),
            pass_on(3, me, low, left),
        )
        self.second = (pass_on(4, left, low, right), pass_on(5, right, high, left))

    def start(self):
        for c in self.first:
            c.start()

    def forward(self):
        self.first[0].wait_recv()
        self.second[0].start()
        self.first[1].wait_recv()
        self.second[1].start()

    def wait_left(self):
        self.first[2].wait_recv()

    def wait_right(self):
        self.first[3].wait_recv()

    def wait_far(self):
        for c in self.second:
            c.wait_recv()

    def wait_send(self):
        for c in self.first + self.second:
            c.wait_send()


class RingScatter:
    def __init__(self, part, rows, ids, bufs, send, recv):
        me, right, left = ids
        far = lax.rem(me + 2, 4)
        low, high = halves(rows)
        far_l, far_r, sum_l, sum_r, in_l, in_r = bufs
        self.part, self.ids, self.n_low, self.bufs = part, ids, low.size, bufs
        copy = functools.partial(ring_copy, send, recv)
        self.far = (
            copy(0, part.at[far, low], far_l, right),
            copy(1, part.at[far, high], far_r, left),
        )
        self.right = copy(2, part.at[right, high], in_l.at[high], right)
        self.left = copy(3, part.at[left, low], in_r.at[low], left)
        self.sums = (
            copy(4, sum_r, in_l.at[low], right),
            copy(5, sum_l, in_r.at[high], left),
        )

    def send_far(self):
        for c in self.far:
            c.start()

    def send_left(self):
        self.left.start()

    def send_right(self):
        self.right.start()

    def send_sums(self):
        me, right, left = self.ids
        far_l, far_r, sum_l, sum_r, in_l, in_r = self.bufs
        n = self.n_low
        self.far[0].wait_recv()
        sum_r[...] = (self.part[right, :n, :].astype(F32) + far_l[...].astype(F32)).astype(BF16)
        self.sums[0].start()
        self.far[1].wait_recv()
        sum_l[...] = (self.part[left, n:, :].astype(F32) + far_r[...].astype(F32)).astype(BF16)
        self.sums[1].start()

    def total(self):
        for c in (self.right, self.left, *self.sums):
            c.wait_recv()
        in_l, in_r = self.bufs[4:]
        return self.part[self.ids[0]].astype(F32) + in_l[...].astype(F32) + in_r[...].astype(F32)

    def wait_send(self):
        for c in (*self.far, self.right, self.left, *self.sums):
            c.wait_send()


def scatter_buffers(rows, width):
    low, high = halves(rows)
    sizes = (low.size, high.size, high.size, low.size, rows, rows)
    return [pltpu.VMEM((n, width), BF16) for n in sizes]


PAD = 32


class Exchange:
    def __init__(self, src, dst, send, recv):
        self.src, self.dst, self.send, self.recv = src, dst, send, recv
        self.me, self.count = lax.axis_index("exp"), lax.axis_size("exp")

    def copy(self, k):
        peer = lax.rem(self.me + k, self.count)
        return remote(
            self.src.at[peer], self.dst.at[self.me], self.send, self.recv, k, "exp", peer
        )

    def each(self, act):
        def body(k, carry):
            act(self.copy(k))
            return carry

        lax.fori_loop(1, self.count, body, 0)

    def start(self):
        self.each(lambda c: c.start())
        self.dst[self.me] = self.src[self.me]

    def wait_recv(self):
        self.each(lambda c: c.wait_recv())

    def wait_send(self):
        self.each(lambda c: c.wait_send())


def meet_all():
    barrier = pltpu.get_barrier_semaphore()
    me, count = lax.axis_index("exp"), lax.axis_size("exp")

    def greet(k, carry):
        peer = lax.rem(me + k, count)
        pl.semaphore_signal(barrier, inc=1, device_id={"exp": peer}, device_id_type=MESH)
        return carry

    lax.fori_loop(1, count, greet, 0)
    ctx = lax.axis_index("ctx")
    right, left = lax.rem(ctx + 1, 4), lax.rem(ctx + 3, 4)
    for neighbour in (left, right):
        pl.semaphore_signal(barrier, inc=1, device_id={"ctx": neighbour}, device_id_type=MESH)
    pl.semaphore_wait(barrier, count + 1)
    return ctx, right, left


def run_experts(
    rows, out_ref, sel_ref, all_ref, ret_ref, block, beside_one, beside_two, scratch
):
    inbox, part, res = scratch[:3]
    bufs = scratch[3:9]
    s_in, r_in, s_out, r_out, s_ag, r_ag, s_rs, r_rs = scratch[9:]
    ids = meet_all()
    me, right, left = ids
    far = lax.rem(me + 2, 4)
    flat = inbox.shape[0] * inbox.shape[1]
    width = inbox.shape[2]

    arriving = Exchange(out_ref, inbox, s_in, r_in)
    arriving.start()
    arriving.wait_recv()
    all_ref[me] = mm(sel_ref[...], inbox[...].reshape(flat, width)).astype(BF16)
    gather = RingGather(all_ref, rows, ids, s_ag, r_ag)
    scatter = RingScatter(part, rows, ids, bufs, s_rs, r_rs)
    gather.start()
    block(me, part)
    gather.forward()
    gather.wait_left()
    block(left, part)
    scatter.send_left()
    gather.wait_right()
    block(right, part)
    scatter.send_right()
    gather.wait_far()
    block(far, part)
    scatter.send_far()
    beside_one()
    scatter.send_sums()
    beside_two()
    padded = mm_tn(sel_ref[...], scatter.total().astype(BF16)).astype(BF16)
    res[...] = padded.reshape(res.shape)
    leaving = Exchange(res, ret_ref, s_out, r_out)
    leaving.start()
    leaving.wait_recv()
    gather.wait_send()
    scatter.wait_send()
    arriving.wait_send()
    leaving.wait_send()


def expert_scratch(experts, rows, width):
    v = lambda *shape: pltpu.VMEM((*shape, width), BF16)
    return [
        v(experts, PAD),
        v(4, rows),
        v(experts, PAD),
        *scatter_buffers(rows, width),
        *[pltpu.SemaphoreType.DMA((experts,))] * 4,
        *[pltpu.SemaphoreType.DMA((6,))] * 4,
    ]


def experts_kernel(rows, out_ref, sel_ref, w_in, w_back, ret_ref, all_ref, pre_ref, *scratch):
    def block(j, part):
        pre = mm(all_ref[j], w_in[...])
        pre_ref[j] = pre
        hidden = gelu_parts(pre)[0].astype(BF16)
        part[j] = mm_nt(hidden, w_back[...]).astype(BF16)

    nothing = lambda: None
    run_experts(rows, out_ref, sel_ref, all_ref, ret_ref, block, nothing, nothing, scratch)


def experts_back_kernel(
    rows, out_ref, sel_ref, w_in, w_back, ent_ref, pre_ref, ret_ref, d_in, d_back, e_in, e_back,
    all_ref, hid_ref, dpre_ref, *scratch
):
    width = w_in.shape[0]

    def block(j, part):
        hidden, slope = gelu_parts(pre_ref[j])
        hid_ref[j] = hidden.astype(BF16)
        dpre = (mm(all_ref[j], w_back[...]) * slope).astype(BF16)
        dpre_ref[j] = dpre
        part[j] = mm_nt(dpre, w_in[...]).astype(BF16)

    def flat(ref):
        return ref[...].reshape(4 * rows, ref.shape[2])

    def beside_one():
        grad = mm_tn(flat(all_ref), flat(hid_ref))
        d_back[...] = grad
        e_back[...] = grad.astype(BF16)

    def beside_two():
        grad = mm_tn(flat(ent_ref), flat(dpre_ref))
        d_in[...] = grad
        e_in[...] = grad.astype(BF16)

    run_experts(rows, out_ref, sel_ref, all_ref, ret_ref, block, beside_one, beside_two, scratch)


def selection(experts, capacity):
    sel = np.zeros((experts * capacity, experts, PAD), np.float32)
    for e in range(experts):
        for s in range(capacity):
            sel[e * capacity + s, e, s] = 1
    return jnp.asarray(sel.reshape(experts * capacity, experts * PAD), BF16)


def experts_forward(outgoing, sel, w_in, w_back):
    experts, _, width = outgoing.shape
    rows = sel.shape[0]
    vm = pl.BlockSpec(memory_space=pltpu.VMEM)
    return pl.pallas_call(
        functools.partial(experts_kernel, rows),
        out_shape=(
            jax.ShapeDtypeStruct(outgoing.shape, BF16),
            jax.ShapeDtypeStruct((4, rows, width), BF16),
            jax.ShapeDtypeStruct((4, rows, w_in.shape[1]), F32),
        ),
        in_specs=[vm] * 4,
        out_specs=(vm,) * 3,
        scratch_shapes=expert_scratch(experts, rows, width),
        compiler_params=pltpu.CompilerParams(
            collective_id=2, has_side_effects=True, vmem_limit_bytes=48 << 20
        ),
    )(outgoing, sel, w_in, w_back)


def experts_backward(outgoing, sel, w_in, w_back, entering, pre):
    experts, _, width = outgoing.shape
    rows, hid = sel.shape[0], w_in.shape[1]
    vm = pl.BlockSpec(memory_space=pltpu.VMEM)
    return pl.pallas_call(
        functools.partial(experts_back_kernel, rows),
        out_shape=(
            jax.ShapeDtypeStruct(outgoing.shape, BF16),
            jax.ShapeDtypeStruct(w_in.shape, F32),
            jax.ShapeDtypeStruct(w_back.shape, F32),
            jax.ShapeDtypeStruct(w_in.shape, BF16),
            jax.ShapeDtypeStruct(w_back.shape, BF16),
        ),
        in_specs=[vm] * 6,
        out_specs=(vm,) * 5,
        scratch_shapes=[
            pltpu.VMEM((4, rows, width), BF16),
            pltpu.VMEM((4, rows, hid), BF16),
            pltpu.VMEM((4, rows, hid), BF16),
            *expert_scratch(experts, rows, width),
        ],
        compiler_params=pltpu.CompilerParams(
            collective_id=3, has_side_effects=True, vmem_limit_bytes=48 << 20
        ),
    )(outgoing, sel, w_in, w_back, entering, pre)


def bucket_bounds():
    half = BUCKETS // 2
    powers = np.arange(1, BUCKETS - half) / (BUCKETS - half)
    return [int(m) for m in np.ceil(half * (REACH / half) ** powers)]


def tile_buckets(kind):
    row = lax.broadcasted_iota(jnp.int32, (SPAN, 2 * SPAN), 0)
    col = lax.broadcasted_iota(jnp.int32, (SPAN, 2 * SPAN), 1)
    ahead = kind * SPAN + row - lax.rem(col, SPAN)
    n = jnp.maximum(ahead, 0)
    bucket = jnp.minimum(n, BUCKETS // 2)
    for bound in bucket_bounds():
        bucket += (n >= bound).astype(jnp.int32)
    return ahead, bucket


def tile_range(kind):
    half = BUCKETS // 2
    ends = [max(kind * SPAN + r - c, 0) for r, c in ((0, SPAN - 1), (SPAN - 1, 0))]
    first, last = (min(n, half) + sum(n >= m for m in bucket_bounds()) for n in ends)
    return range(first, last + 1)


def make_tiles(table_ref, tiles_ref, heads):
    repeat = tiles_ref.shape[3] // (2 * SPAN)
    for k in range(KINDS - 1):
        ahead, bucket = tile_buckets(k)
        for h in range(heads):
            tile = jnp.full(bucket.shape, NEG, F32)
            for b in tile_range(k):
                tile = jnp.where(bucket == b, table_ref[b : b + 1, h : h + 1], tile)
            tile = jnp.where(ahead < 0, NEG, tile)
            tiles_ref[h, k] = jnp.concatenate([tile] * repeat, 1)


def bias_rows(tiles_ref, table_ref, kind_ref, head, block):
    kind = kind_ref[block : block + 1, :]
    last = table_ref[BUCKETS - 1 : BUCKETS, head : head + 1]
    rows = jnp.where(kind == 3, last, NEG)
    for k in (2, 1, 0):
        rows = jnp.where(kind == k, tiles_ref[head, k], rows)
    return rows


def head_columns(ref, group, head, heads):
    at = (group * heads + head) * HEAD_DIM
    return ref[:, at : at + HEAD_DIM]


def meet_ring(partner):
    barrier = pltpu.get_barrier_semaphore()
    ctx = lax.axis_index("ctx")
    right, left = lax.rem(ctx + 1, 4), lax.rem(ctx + 3, 4)
    for neighbour in (left, right):
        pl.semaphore_signal(barrier, inc=1, device_id={"ctx": neighbour}, device_id_type=MESH)
    if partner is not None:
        pl.semaphore_signal(barrier, inc=1, device_id={"section": partner}, device_id_type=MESH)
    pl.semaphore_wait(barrier, 2 if partner is None else 3)
    return ctx, right, left


def attend_kernel(
    heads, x_ref, gain_ref, w_qkv, w_out, table_ref, kind_ref,
    middle_ref, all_ref, proj_ref, att_ref,
    tiles_ref, s_ref, p_ref, part, *scratch
):
    bufs, (s_ag, r_ag, s_rs, r_rs) = scratch[:6], scratch[6:]
    ids = meet_ring(None)
    me, right, left = ids
    far = lax.rem(me + 2, 4)
    rows, width = x_ref.shape
    seq = 4 * rows
    all_ref[me] = norm(x_ref[...], gain_ref[...])
    gather = RingGather(all_ref, rows, ids, s_ag, r_ag)
    gather.start()
    make_tiles(table_ref, tiles_ref, heads)
    gather.forward()
    gather.wait_left()
    gather.wait_right()
    gather.wait_far()
    proj_ref[...] = mm(all_ref[...].reshape(seq, width), w_qkv[...]).astype(BF16)
    parts = []
    for h in range(heads):
        q, k, v = (head_columns(proj_ref, g, h, heads) for g in range(3))
        s_ref[...] = mm_nt(q, k)
        for b in range(seq // SPAN):
            at = slice(b * SPAN, (b + 1) * SPAN)
            s = s_ref[at, :] * HEAD_DIM**-0.5 + bias_rows(tiles_ref, table_ref, kind_ref, h, b)
            e = jnp.exp(s - jnp.max(s, -1, keepdims=True))
            p_ref[at, :] = (e * (1.0 / jnp.sum(e, -1, keepdims=True))).astype(BF16)
        parts.append(mm(p_ref[...], v).astype(BF16))
    att_ref[...] = jnp.concatenate(parts, 1).reshape(att_ref.shape)
    scatter = RingScatter(part, rows, ids, bufs, s_rs, r_rs)
    part[far] = mm(att_ref[far], w_out[...]).astype(BF16)
    scatter.send_far()
    part[right] = mm(att_ref[right], w_out[...]).astype(BF16)
    scatter.send_right()
    part[left] = mm(att_ref[left], w_out[...]).astype(BF16)
    scatter.send_left()
    part[me] = mm(att_ref[me], w_out[...]).astype(BF16)
    scatter.send_sums()
    middle_ref[...] = x_ref[...] + scatter.total()
    gather.wait_send()
    scatter.wait_send()


def attend(x, gain, w_qkv, w_out, table, kind):
    rows, width = x.shape
    seq = 4 * rows
    part = w_out.shape[0]
    heads = part // HEAD_DIM
    vm = pl.BlockSpec(memory_space=pltpu.VMEM)
    return pl.pallas_call(
        functools.partial(attend_kernel, heads),
        out_shape=(
            jax.ShapeDtypeStruct(x.shape, F32),
            jax.ShapeDtypeStruct((4, rows, width), BF16),
            jax.ShapeDtypeStruct((seq, 3 * part), BF16),
            jax.ShapeDtypeStruct((4, rows, part), BF16),
        ),
        in_specs=[vm] * 6,
        out_specs=(vm,) * 4,
        scratch_shapes=[
            pltpu.VMEM((heads, KINDS - 1, SPAN, seq), F32),
            pltpu.VMEM((seq, seq), F32),
            pltpu.VMEM((seq, seq), BF16),
            pltpu.VMEM((4, rows, width), BF16),
            *scatter_buffers(rows, width),
            *[pltpu.SemaphoreType.DMA((6,))] * 4,
        ],
        compiler_params=pltpu.CompilerParams(
            collective_id=0, has_side_effects=True, vmem_limit_bytes=48 << 20
        ),
    )(x, gain, w_qkv, w_out, table, kind)


def attend_back_kernel(
    heads, dmid_ref, all_ref, proj_ref, att_ref, w_qkv, w_out, table_ref, kind_ref,
    e_in, e_back, perm_ref, perm_out_ref,
    dnormed_ref, pq_ref, po_ref, dtable_ref, got_in, got_back, got_pq, got_po,
    tiles_ref, dtiles_ref, s_ref, dp_ref, p_ref, ds_ref, da_ref, dproj_ref, db_ref, part, *scratch
):
    bufs, (s_ag, r_ag, s_rs, r_rs, s_x, r_x) = scratch[:6], scratch[6:]
    partner = 1 - lax.axis_index("section")
    ids = meet_ring(partner)
    me, right, left = ids
    far = lax.rem(me + 2, 4)
    rows, width = dmid_ref.shape
    seq = 4 * rows
    scale = HEAD_DIM**-0.5

    def across(k, src, dst):
        return remote(src, dst, s_x, r_x, k, "section", partner)

    crossing = [
        across(0, e_in, got_in),
        across(1, e_back, got_back),
        across(2, pq_ref, got_pq),
        across(3, po_ref, got_po),
    ]
    db_ref[me] = dmid_ref[...].astype(BF16)
    gather = RingGather(db_ref, rows, ids, s_ag, r_ag)
    gather.start()
    crossing[0].start()
    crossing[1].start()
    make_tiles(table_ref, tiles_ref, heads)
    gather.forward()
    gather.wait_left()
    gather.wait_right()
    gather.wait_far()
    da_ref[...] = mm_nt(db_ref[...].reshape(seq, width), w_out[...]).astype(BF16)
    dq, dk, dv = [], [], []
    for h in range(heads):
        q, k, v = (head_columns(proj_ref, g, h, heads) for g in range(3))
        da = head_columns(da_ref, 0, h, heads)
        s_ref[...] = mm_nt(q, k)
        dp_ref[...] = mm_nt(da, v)
        dtiles_ref[...] = jnp.zeros(dtiles_ref.shape, F32)
        for b in range(seq // SPAN):
            at = slice(b * SPAN, (b + 1) * SPAN)
            s = s_ref[at, :] * scale + bias_rows(tiles_ref, table_ref, kind_ref, h, b)
            e = jnp.exp(s - jnp.max(s, -1, keepdims=True))
            p = e * (1.0 / jnp.sum(e, -1, keepdims=True))
            dp = dp_ref[at, :]
            ds = p * (dp - jnp.sum(p * dp, -1, keepdims=True))
            p_ref[at, :] = p.astype(BF16)
            ds_ref[at, :] = ds.astype(BF16)
            kind = kind_ref[b : b + 1, :]
            for n in range(KINDS):
                dtiles_ref[n] += jnp.where(kind == n, ds, 0.0)
        for n in range(KINDS):
            folded = dtiles_ref[n, :, : 2 * SPAN]
            for m in range(1, seq // (2 * SPAN)):
                folded = folded + dtiles_ref[n, :, m * 2 * SPAN : (m + 1) * 2 * SPAN]
            dtiles_ref[n, :, : 2 * SPAN] = folded
        sums = [jnp.zeros((1, 2 * SPAN), F32)] * BUCKETS
        for n in range(KINDS - 1):
            bucket = tile_buckets(n)[1]
            folded = dtiles_ref[n, :, : 2 * SPAN]
            for b in tile_range(n):
                hit = jnp.where(bucket == b, folded, 0.0)
                sums[b] = sums[b] + jnp.sum(hit, 0, keepdims=True)
        rest = dtiles_ref[KINDS - 1, :, : 2 * SPAN]
        sums[-1] = sums[-1] + jnp.sum(rest, 0, keepdims=True)
        dtable_ref[h] = jnp.concatenate(sums, 0)
        p = p_ref[...]
        ds = ds_ref[...]
        dq.append((mm(ds, k) * scale).astype(BF16))
        dk.append((mm_tn(ds, q) * scale).astype(BF16))
        dv.append(mm_tn(p, da).astype(BF16))
    dproj_ref[...] = jnp.concatenate(dq + dk + dv, 1).reshape(dproj_ref.shape)
    scatter = RingScatter(part, rows, ids, bufs, s_rs, r_rs)
    part[far] = mm_nt(dproj_ref[far], w_qkv[...]).astype(BF16)
    scatter.send_far()
    part[right] = mm_nt(dproj_ref[right], w_qkv[...]).astype(BF16)
    scatter.send_right()
    part[left] = mm_nt(dproj_ref[left], w_qkv[...]).astype(BF16)
    scatter.send_left()
    part[me] = mm_nt(dproj_ref[me], w_qkv[...]).astype(BF16)
    dproj = dproj_ref[...].reshape(seq, dproj_ref.shape[2])
    d_qkv = mm_tn(all_ref[...].reshape(seq, width), dproj).astype(BF16)
    pq_ref[...] = mm(perm_ref[...], d_qkv).astype(BF16)
    crossing[2].start()
    scatter.send_sums()
    d_out = mm_tn(att_ref[...].reshape(seq, att_ref.shape[2]), db_ref[...].reshape(seq, width))
    po_ref[...] = mm(perm_out_ref[...], d_out.astype(BF16)).astype(BF16)
    crossing[3].start()
    dnormed_ref[...] = scatter.total()
    gather.wait_send()
    scatter.wait_send()
    for c in crossing:
        c.wait()


def attend_back(dmiddle, normed, proj, att, w_qkv, w_out, table, kind, e_in, e_back, perm, perm_out):
    rows, width = dmiddle.shape
    seq = 4 * rows
    part = w_out.shape[0]
    heads = part // HEAD_DIM
    vm = pl.BlockSpec(memory_space=pltpu.VMEM)
    pq = jax.ShapeDtypeStruct((perm.shape[0], 3 * part), BF16)
    po = jax.ShapeDtypeStruct((perm_out.shape[0], width), BF16)
    return pl.pallas_call(
        functools.partial(attend_back_kernel, heads),
        out_shape=(
            jax.ShapeDtypeStruct((rows, width), F32),
            pq,
            po,
            jax.ShapeDtypeStruct((heads, BUCKETS, 2 * SPAN), F32),
            jax.ShapeDtypeStruct(e_in.shape, BF16),
            jax.ShapeDtypeStruct(e_back.shape, BF16),
            pq,
            po,
        ),
        in_specs=[vm] * 12,
        out_specs=(vm,) * 8,
        scratch_shapes=[
            pltpu.VMEM((heads, KINDS - 1, SPAN, seq), F32),
            pltpu.VMEM((KINDS, SPAN, seq), F32),
            pltpu.VMEM((seq, seq), F32),
            pltpu.VMEM((seq, seq), F32),
            pltpu.VMEM((seq, seq), BF16),
            pltpu.VMEM((seq, seq), BF16),
            pltpu.VMEM((seq, part), BF16),
            pltpu.VMEM((4, rows, 3 * part), BF16),
            pltpu.VMEM((4, rows, width), BF16),
            pltpu.VMEM((4, rows, width), BF16),
            *scatter_buffers(rows, width),
            *[pltpu.SemaphoreType.DMA((6,))] * 4,
            *[pltpu.SemaphoreType.DMA((4,))] * 2,
        ],
        compiler_params=pltpu.CompilerParams(
            collective_id=1, has_side_effects=True, vmem_limit_bytes=52 << 20
        ),
    )(dmiddle, normed, proj, att, w_qkv, w_out, table, kind, e_in, e_back, perm, perm_out)


def meet_everyone():
    barrier = pltpu.get_barrier_semaphore()
    peers = [("exp", 16), ("ctx", 4), ("section", 2)]
    for axis, count in peers:
        me = lax.axis_index(axis)

        def greet(k, carry, axis=axis, me=me, count=count):
            peer = lax.rem(me + k, count)
            pl.semaphore_signal(barrier, inc=1, device_id={axis: peer}, device_id_type=MESH)
            return carry

        lax.fori_loop(1, count, greet, 0)
    pl.semaphore_wait(barrier, sum(count - 1 for _, count in peers))


def ctx_exchange(src, dst, send, recv):
    me = lax.axis_index("ctx")
    copies = []
    for k in (1, 3, 2):
        peer = lax.rem(me + k, 4)
        copies.append(remote(src.at[peer], dst.at[me], send, recv, k, "ctx", peer))
    return copies


def weights_kernel(
    cols_ref, outp_ref, w_in, w_back, perm_ref, perm_out_ref, pick_ref,
    w_qkv, w_out, small_ref, both_in, both_back,
    zin, grid, grid_out, s_z, r_z, s_q, r_q, s_o, r_o, s_fq, r_fq, s_fo, r_fo, s_x, r_x, s_own
):
    meet_everyone()
    section, ctx, exp = (lax.axis_index(a) for a in ("section", "ctx", "exp"))
    partner = 1 - section
    count = grid.shape[1]
    turn = ctx_exchange(cols_ref, zin, s_z, r_z)
    for c in turn:
        c.start()
    zin[ctx] = cols_ref[ctx]
    grid_out[section, exp] = outp_ref[...]

    def spread(ref, send, recv, k):
        peer = lax.rem(exp + k, count)
        at = ref.at[section, exp]
        return remote(at, at, send, recv, k, "exp", peer)

    def forward(ref, send, recv, k):
        at = ref.at[section, lax.rem(exp + count - k, count)]
        return remote(at, at, send, recv, k, "section", partner)

    def each(act, first=1):
        def body(k, carry):
            act(k)
            return carry

        lax.fori_loop(first, count, body, 0)

    each(lambda k: spread(grid_out, s_o, r_o, k).start())
    for c in turn:
        c.wait_recv()
    grid[section, exp] = zin[...].reshape(grid.shape[2:])
    each(lambda k: spread(grid, s_q, r_q, k).start())
    forward(grid, s_fq, r_fq, 0).start()
    forward(grid_out, s_fo, r_fo, 0).start()
    own_in = pltpu.make_async_copy(w_in, both_in.at[section], s_own.at[0])
    own_back = pltpu.make_async_copy(w_back, both_back.at[section], s_own.at[1])
    own_in.start()
    own_back.start()
    cross_in = remote(w_in, both_in.at[section], s_x, r_x, 0, "section", partner)
    cross_back = remote(w_back, both_back.at[section], s_x, r_x, 1, "section", partner)

    def relay(ref, s, r, sf, rf, k):
        spread(ref, s, r, k).wait_recv()
        forward(ref, sf, rf, k).start()

    each(lambda k: relay(grid_out, s_o, r_o, s_fo, r_fo, k))
    each(lambda k: relay(grid, s_q, r_q, s_fq, r_fq, k))
    cross_in.start()
    cross_back.start()

    def unpack(layer):
        flat = grid[layer].reshape(perm_ref.shape[0], grid.shape[3])
        w_qkv[layer] = mm_tn(perm_ref[...], flat).astype(BF16)
        small_ref[layer] = mm(pick_ref[...], flat)
        flat = grid_out[layer].reshape(perm_out_ref.shape[0], grid_out.shape[3])
        w_out[layer] = mm_tn(perm_out_ref[...], flat).astype(BF16)

    unpack(section)
    each(lambda k: forward(grid_out, s_fo, r_fo, k).wait_recv(), 0)
    each(lambda k: forward(grid, s_fq, r_fq, k).wait_recv(), 0)
    unpack(partner)
    each(lambda k: spread(grid_out, s_o, r_o, k).wait_send())
    each(lambda k: spread(grid, s_q, r_q, k).wait_send())
    each(lambda k: forward(grid_out, s_fo, r_fo, k).wait_send(), 0)
    each(lambda k: forward(grid, s_fq, r_fq, k).wait_send(), 0)
    for c in turn:
        c.wait_send()
    own_in.wait()
    own_back.wait()
    cross_in.wait()
    cross_back.wait()


def gather_weights(cols, outp, w_in, w_back, perm, perm_out, pick):
    width, part = outp.shape[1], cols.shape[2]
    count = perm_out.shape[0] // 16
    vm = pl.BlockSpec(memory_space=pltpu.VMEM)
    dma = lambda n: pltpu.SemaphoreType.DMA((n,))
    return pl.pallas_call(
        weights_kernel,
        out_shape=(
            jax.ShapeDtypeStruct((2, width, part), BF16),
            jax.ShapeDtypeStruct((2, perm_out.shape[1], width), BF16),
            jax.ShapeDtypeStruct((2, pick.shape[0], part), F32),
            jax.ShapeDtypeStruct((2, *w_in.shape), BF16),
            jax.ShapeDtypeStruct((2, *w_back.shape), BF16),
        ),
        in_specs=[vm] * 7,
        out_specs=(vm,) * 5,
        scratch_shapes=[
            pltpu.VMEM(cols.shape, BF16),
            pltpu.VMEM((2, count, 64, part), BF16),
            pltpu.VMEM((2, count, 16, width), BF16),
            dma(4), dma(4), *[dma(count)] * 8, dma(2), dma(2), dma(2),
        ],
        compiler_params=pltpu.CompilerParams(
            collective_id=4, has_side_effects=True, vmem_limit_bytes=48 << 20
        ),
    )(cols, outp, w_in, w_back, perm, perm_out, pick)


def owners_kernel(
    pq0, pq1, gq0, gq1, po0, po1, go0, go1, small_ref, spread_ref,
    in0, in1, gin0, gin1, back0, back1, gback0, gback1,
    turned, out_grad, d_in, d_back,
    got_small, pieces, box, pieces_out, box_out, summed, s_s, r_s, s_q, r_q, s_o, r_o, s_z, r_z
):
    meet_everyone()
    section, ctx, exp = (lax.axis_index(a) for a in ("section", "ctx", "exp"))
    partner = 1 - section
    first = section == 0
    cross = remote(small_ref.at[partner], got_small, s_s, r_s, 0, "section", partner)
    cross.start()

    def chosen(a, b, c, d):
        return jnp.where(first, a[...], b[...]).astype(F32) + jnp.where(
            first, c[...], d[...]
        ).astype(F32)

    pieces_out[...] = chosen(po0, po1, go0, go1).astype(BF16).reshape(pieces_out.shape)
    swap_out = Exchange(pieces_out, box_out, s_o, r_o)
    swap_out.start()
    dense = chosen(pq0, pq1, gq0, gq1)
    cross.wait_recv()
    small = small_ref[section] + got_small[...]
    wide = mm(spread_ref[...], small.astype(BF16))
    n = wide.shape[1]
    dense = jnp.concatenate([dense[:, :n] + wide, dense[:, n:]], 1)
    pieces[...] = dense.astype(BF16).reshape(pieces.shape)
    swap = Exchange(pieces, box, s_q, r_q)
    swap.start()
    d_in[...] = chosen(in0, in1, gin0, gin1)
    d_back[...] = chosen(back0, back1, gback0, gback1)
    swap_out.wait_recv()
    total = box_out[0].astype(F32)
    for k in range(1, box_out.shape[0]):
        total = total + box_out[k].astype(F32)
    out_grad[...] = total
    swap.wait_recv()
    total = box[0].astype(F32)
    for k in range(1, box.shape[0]):
        total = total + box[k].astype(F32)
    summed[...] = total.reshape(summed.shape)
    turn = ctx_exchange(summed, turned, s_z, r_z)
    for c in turn:
        c.start()
    turned[ctx] = summed[ctx]
    for c in turn:
        c.wait()
    cross.wait_send()
    swap.wait_send()
    swap_out.wait_send()


def sum_at_owners(pq, gq, po, go, small, spread, d_in, g_in, d_back, g_back, count):
    rows, part = pq[0].shape
    out_rows, width = po[0].shape
    vm = pl.BlockSpec(memory_space=pltpu.VMEM)
    dma = lambda n: pltpu.SemaphoreType.DMA((n,))
    own = (rows // count, part)
    own_out = (out_rows // count, width)
    quarter = (4, rows // count // 4, part)
    return pl.pallas_call(
        owners_kernel,
        out_shape=(
            jax.ShapeDtypeStruct(quarter, F32),
            jax.ShapeDtypeStruct(own_out, F32),
            jax.ShapeDtypeStruct(d_in[0].shape, F32),
            jax.ShapeDtypeStruct(d_back[0].shape, F32),
        ),
        in_specs=[vm] * 18,
        out_specs=(vm,) * 4,
        scratch_shapes=[
            pltpu.VMEM(small.shape[1:], F32),
            pltpu.VMEM((count, *own), BF16),
            pltpu.VMEM((count, *own), BF16),
            pltpu.VMEM((count, *own_out), BF16),
            pltpu.VMEM((count, *own_out), BF16),
            pltpu.VMEM(quarter, F32),
            dma(1), dma(1), *[dma(count)] * 4, dma(4), dma(4),
        ],
        compiler_params=pltpu.CompilerParams(
            collective_id=5, has_side_effects=True, vmem_limit_bytes=52 << 20
        ),
    )(*pq, *gq, *po, *go, small, spread, *d_in, *g_in, *d_back, *g_back)


def packing(n_ctx, n_exp, own_rows):
    blocks = n_ctx * n_exp
    perm = np.zeros((blocks, 16, blocks, own_rows), np.float32)
    pick = np.zeros((blocks, blocks, 16), np.float32)
    perm_out = np.zeros((n_exp, 16, n_exp, own_rows), np.float32)
    for e in range(n_exp):
        for i in range(own_rows):
            perm_out[e, i, e, i] = 1
        for c in range(n_ctx):
            for i in range(own_rows):
                perm[e * n_ctx + c, i, c * n_exp + e, i] = 1
            pick[c * n_exp + e, e * n_ctx + c, own_rows] = 1
    perm = perm.reshape(blocks * 16, blocks * own_rows)
    pick = pick.reshape(blocks, blocks * 16)
    perm_out = perm_out.reshape(n_exp * 16, n_exp * own_rows)
    return tuple(jnp.asarray(m, BF16) for m in (perm, pick, pick.T.copy(), perm_out))


def norm_scale(v):
    return lax.rsqrt(jnp.mean(v * v, -1, keepdims=True) + EPS)


def norm(v, gain):
    return (v * norm_scale(v) * gain).astype(BF16)


def norm_back(v, gain, du):
    r = norm_scale(v)
    dug = du * gain
    dv = r * dug - v * (r * r * r) * jnp.mean(dug * v, -1, keepdims=True)
    return dv, jnp.sum(du * v * r, 0)


def gelu_parts(v):
    t = jnp.tanh(GELU_C * (v + 0.044715 * v * v * v))
    value = 0.5 * v * (1.0 + t)
    slope = 0.5 * (1.0 + t) + 0.5 * v * (1.0 - t * t) * GELU_C * (1.0 + 3 * 0.044715 * v * v)
    return value, slope


def slot_tables(routes, experts):
    rows = routes.shape[0]
    flat = routes.reshape(rows * TOP)
    hot = flat[:, None] == jnp.arange(experts, dtype=jnp.int32)
    before = np.tril(np.ones((rows * TOP, rows * TOP), np.float32), -1)
    earlier = mm(jnp.asarray(before, BF16), hot.astype(BF16))
    slot = jnp.sum(jnp.where(hot, earlier, 0.0), -1).astype(jnp.int32)
    target = (flat * PAD + slot).reshape(rows, TOP)
    slots = jnp.arange(experts * PAD, dtype=jnp.int32)
    slot_hot = [(target[:, c : c + 1] == slots).astype(BF16) for c in range(TOP)]
    route_hot = [(routes[:, c : c + 1] == jnp.arange(experts)).astype(F32) for c in range(TOP)]
    return route_hot, slot_hot


def on_device(
    inputs,
    cotangent,
    routes,
    block_order,
    attn_gain,
    qkv_weight,
    out_weight,
    rel_bias,
    moe_gain,
    router_weight,
    expert_in,
    expert_out,
):
    rows, width = inputs.shape[2:]
    n_ctx, n_exp = lax.axis_size("ctx"), lax.axis_size("exp")
    seq = rows * n_ctx
    own_rows = qkv_weight.shape[1]
    heads = HEADS // n_ctx
    part = heads * HEAD_DIM
    capacity = rows * TOP // n_exp + max(1, rows * TOP // (16 * n_exp))
    slots = n_exp * PAD
    sel = selection(n_exp, capacity)
    section = lax.axis_index("section")
    ctx = lax.axis_index("ctx")
    first = section == 0

    perm, pick, place, perm_out = packing(n_ctx, n_exp, own_rows)
    small = jnp.concatenate(
        [attn_gain[0], moe_gain[0], rel_bias[0], router_weight[0].reshape(-1)]
    )
    n_small = small.shape[0]
    columns = qkv_weight[0].reshape(own_rows, 3, n_ctx, part).transpose(2, 0, 1, 3)
    columns = columns.reshape(n_ctx, own_rows, 3 * part)
    small_row = jnp.pad(small, (0, 3 * part - n_small))
    small_rows = jnp.broadcast_to(small_row, (n_ctx, 1, 3 * part))
    columns = jnp.concatenate([columns, small_rows], 1)
    columns = jnp.pad(columns, ((0, 0), (0, 15 - own_rows), (0, 0)))
    out_rows = jnp.pad(out_weight[0], ((0, 16 - own_rows), (0, 0)))
    w_qkv_both, w_out_both, small_both, w_in_both, w_back_both = gather_weights(
        columns, out_rows, expert_in[0, 0], expert_out[0, 0], perm, perm_out, pick
    )
    n_bias = BUCKETS * HEADS // (n_ctx * n_exp)

    def dense(layer):
        small = small_both[layer]
        gain_one = small[:, :own_rows].reshape(1, width)
        gain_two = small[:, own_rows : 2 * own_rows].reshape(1, width)
        table = small[:, 2 * own_rows : 2 * own_rows + n_bias].reshape(BUCKETS, HEADS)
        table = lax.dynamic_slice_in_dim(table, ctx * heads, heads, 1)
        router = small[:, 2 * own_rows + n_bias : n_small].reshape(width, n_exp).astype(BF16)
        return (
            w_qkv_both[layer], w_out_both[layer], gain_one, gain_two, table, router,
            w_in_both[layer], w_back_both[layer],
        )

    weights = [dense(0), dense(1)]
    ahead = block_order[:, None] - block_order[None, :]
    kind = jnp.repeat(jnp.where(ahead < 0, -1, jnp.minimum(ahead, 3)), SPAN, 1)

    own_routes = routes[0, :, 0]
    kept = jnp.where(first, own_routes[0], own_routes[1])
    given = jnp.where(first, own_routes[1], own_routes[0])
    taken = lax.ppermute(given, "section", [(0, 1), (1, 0)])
    layer_routes = (jnp.where(first, kept, taken), jnp.where(first, taken, kept))
    tables = [slot_tables(r, n_exp) for r in layer_routes]

    def forward(x, layer):
        w_qkv, w_out, gain_one, gain_two, table, router, w_in, w_back = weights[layer]
        route_hot, slot_hot = tables[layer]
        middle, normed, proj, attended = attend(x, gain_one, w_qkv, w_out, table, kind)
        mixed = norm(middle, gain_two)
        logits = mm(mixed, router)
        chosen = [jnp.sum(h * logits, -1, keepdims=True) for h in route_hot]
        peak = jnp.maximum(chosen[0], chosen[1])
        raised = [jnp.exp(c - peak) for c in chosen]
        gates = [r / (raised[0] + raised[1]) for r in raised]
        placing = slot_hot[0] + slot_hot[1]
        outgoing = mm_tn(placing, mixed).astype(BF16).reshape(n_exp, PAD, width)
        returned, entering, pre = experts_forward(outgoing, sel, w_in, w_back)
        returned = returned.reshape(slots, width)
        picked = [mm(h, returned) for h in slot_hot]
        y = middle + gates[0] * picked[0] + gates[1] * picked[1]
        keep = (x, normed, proj, attended, middle, mixed, gates, picked, entering, pre)
        return y, keep

    def backward(g, keep, layer):
        x, normed, proj, attended, middle, mixed, gates, picked, entering, pre = keep
        w_qkv, w_out, gain_one, gain_two, table, router, w_in, w_back = weights[layer]
        route_hot, slot_hot = tables[layer]
        dreturned = mm_tn(slot_hot[0], (gates[0] * g).astype(BF16)) + mm_tn(
            slot_hot[1], (gates[1] * g).astype(BF16)
        )
        dreturned = dreturned.astype(BF16).reshape(n_exp, PAD, width)
        dleft, d_in, d_back, e_in, e_back = experts_backward(dreturned, sel, w_in, w_back, entering, pre)
        dleft = dleft.reshape(slots, width)
        dgates = [jnp.sum(g * p, -1, keepdims=True) for p in picked]
        mean = gates[0] * dgates[0] + gates[1] * dgates[1]
        dchosen = [a * (b - mean) for a, b in zip(gates, dgates)]
        dlogits = route_hot[0] * dchosen[0] + route_hot[1] * dchosen[1]
        dlogits = dlogits.astype(BF16)
        d_router = mm_tn(mixed, dlogits)
        dmixed = mm(slot_hot[0] + slot_hot[1], dleft) + mm_nt(dlogits, router)
        dnorm, d_gain_two = norm_back(middle, gain_two, dmixed)
        dmiddle = g + dnorm
        dnormed, pq, po, d_table, g_in, g_back, gq, go = attend_back(
            dmiddle, normed, proj, attended, w_qkv, w_out, table, kind, e_in, e_back, perm, perm_out
        )
        dnorm, d_gain_one = norm_back(x, gain_one, dnormed)
        d_table = jnp.repeat(jnp.sum(d_table, -1).T, 2, axis=0)
        owner = jnp.arange(n_ctx * n_exp)[:, None]
        d_table = jnp.where(owner % 2 == ctx // 2, d_table, 0.0)
        even = ctx % 2 == 0
        d_table = [jnp.where(even, d_table, 0.0), jnp.where(even, 0.0, d_table)]
        owners = (n_ctx * n_exp, -1)
        d_small = jnp.concatenate(
            [d_gain_one.reshape(owners), d_gain_two.reshape(owners), *d_table,
             d_router.reshape(owners)],
            1,
        )
        d_small = jnp.pad(d_small, ((0, 0), (0, 256 - n_small)))
        return dmiddle + dnorm, (pq, gq, po, go, d_small, d_in, g_in, d_back, g_back)

    def swap(x):
        return lax.ppermute(x, "section", [(0, 1), (1, 0)])

    x = jnp.where(first, inputs[0, 0], inputs[1, 0]).astype(F32)
    cot = jnp.where(first, cotangent[0, 0], cotangent[1, 0]).astype(F32)
    y0, keep0 = forward(x, 0)
    h = y0.astype(BF16)
    y1, keep1 = forward(h.astype(F32), 1)
    top = y1.astype(BF16)
    dh, grads1 = backward(cot, keep1, 1)
    dh = dh.astype(BF16)
    dx, grads0 = backward(dh.astype(F32), keep0, 0)
    pq, gq, po, go, d_small, d_in, g_in, d_back, g_back = zip(grads0, grads1)
    pieces, out_grad, d_in, d_back = sum_at_owners(
        pq, gq, po, go, jnp.stack(d_small), place, d_in, g_in, d_back, g_back, n_exp
    )
    qkv_grad = pieces[:, :own_rows].reshape(n_ctx, own_rows, 3, part)
    qkv_grad = qkv_grad.transpose(1, 2, 0, 3).reshape(own_rows, 3 * width)
    out_grad = out_grad[:own_rows]
    small = jnp.sum(pieces[:, own_rows, :n_small], 0)

    other = swap(jnp.where(first, top, h))
    layer_out = jnp.where(
        first, jnp.stack([h, other]), jnp.stack([other, top])
    ).reshape(1, 2, 1, rows, width)
    dh = dh.astype(F32)
    other = swap(jnp.where(first, dh, dx))
    input_grad = jnp.where(
        first, jnp.stack([dx, other]), jnp.stack([other, dh])
    ).reshape(1, 2, 1, rows, width)
    return (
        layer_out,
        input_grad,
        small[:own_rows][None],
        qkv_grad[None],
        out_grad[None],
        small[2 * own_rows : 2 * own_rows + n_bias][None],
        small[own_rows : 2 * own_rows][None],
        small[2 * own_rows + n_bias :].reshape(1, own_rows, n_exp),
        d_in[None, None],
        d_back[None, None],
    )


def solution(mesh):
    return jax.shard_map(
        on_device,
        mesh=mesh,
        in_specs=(
            P(None, "exp", "ctx", None),
            P(None, "exp", "ctx", None),
            P("section", None, "exp", "ctx", None),
            P(),
            P("section", ("ctx", "exp")),
            P("section", ("ctx", "exp"), None),
            P("section", ("ctx", "exp"), None),
            P("section", ("ctx", "exp")),
            P("section", ("ctx", "exp")),
            P("section", ("ctx", "exp"), None),
            P("section", "exp", None, "ctx"),
            P("section", "exp", None, "ctx"),
        ),
        out_specs=(
            P("section", None, "exp", "ctx", None),
            P("section", None, "exp", "ctx", None),
            P("section", ("ctx", "exp")),
            P("section", ("ctx", "exp"), None),
            P("section", ("ctx", "exp"), None),
            P("section", ("ctx", "exp")),
            P("section", ("ctx", "exp")),
            P("section", ("ctx", "exp"), None),
            P("section", "exp", None, "ctx"),
            P("section", "exp", None, "ctx"),
        ),
        check_vma=False,
    )
```

```python
import functools
import math

import jax
import jax.numpy as jnp
import numpy as np
from jax import lax
from jax.experimental import pallas as pl
from jax.experimental.pallas import tpu as pltpu
from jax.sharding import PartitionSpec as P

HEADS = 12
HEAD_DIM = 64
BUCKETS = 32
REACH = 128
TOP = 2
EPS = 1e-06
NEG = -1e30
SPAN = 64
KINDS = 4
MESH = pl.DeviceIdType.MESH
BF16 = jnp.bfloat16
F32 = jnp.float32
GELU_C = math.sqrt(2.0 / math.pi)


def dot(a, b, dims):
    return lax.dot_general(a, b, (dims, ((), ())), preferred_element_type=F32)


def mm(a, b):
    return dot(a, b, ((1,), (0,)))


def mm_nt(a, b):
    return dot(a, b, ((1,), (1,)))


def mm_tn(a, b):
    return dot(a, b, ((0,), (0,)))


def meet_neighbours(axis, count):
    me = lax.axis_index(axis)
    right, left = lax.rem(me + 1, count), lax.rem(me + count - 1, count)
    barrier = pltpu.get_barrier_semaphore()
    for neighbour in (left, right):
        pl.semaphore_signal(barrier, inc=1, device_id={axis: neighbour}, device_id_type=MESH)
    pl.semaphore_wait(barrier, 2)
    return me, right, left


def remote(src, dst, send, recv, k, axis, to):
    return pltpu.make_async_remote_copy(
        src_ref=src,
        dst_ref=dst,
        send_sem=send.at[k],
        recv_sem=recv.at[k],
        device_id={axis: to},
        device_id_type=MESH,
    )


def halves(rows):
    first = (rows // 2 + 15) // 16 * 16
    return (pl.ds(0, first), pl.ds(first, rows - first))


def ring_copy(send, recv, k, src, dst, to):
    return remote(src, dst, send, recv, k, "ctx", to)


class RingGather:
    def __init__(self, all_ref, rows, ids, send, recv):
        me, right, left = ids
        low, high = halves(rows)

        def pass_on(k, slot, half, to):
            at = all_ref.at[slot, half]
            return ring_copy(send, recv, k, at, at, to)

        self.first = (
            pass_on(0, me, low, right),
            pass_on(1, me, high, left),
            pass_on(2, me, high, right),
            pass_on(3, me, low, left),
        )
        self.second = (pass_on(4, left, low, right), pass_on(5, right, high, left))

    def start(self):
        for c in self.first:
            c.start()

    def forward(self):
        self.first[0].wait_recv()
        self.second[0].start()
        self.first[1].wait_recv()
        self.second[1].start()

    def wait_left(self):
        self.first[2].wait_recv()

    def wait_right(self):
        self.first[3].wait_recv()

    def wait_far(self):
        for c in self.second:
            c.wait_recv()

    def wait_send(self):
        for c in self.first + self.second:
            c.wait_send()


class RingScatter:
    def __init__(self, part, rows, ids, bufs, send, recv):
        me, right, left = ids
        far = lax.rem(me + 2, 4)
        low, high = halves(rows)
        far_l, far_r, sum_l, sum_r, in_l, in_r = bufs
        self.part, self.ids, self.n_low, self.bufs = part, ids, low.size, bufs
        copy = functools.partial(ring_copy, send, recv)
        self.far = (
            copy(0, part.at[far, low], far_l, right),
            copy(1, part.at[far, high], far_r, left),
        )
        self.right = copy(2, part.at[right, high], in_l.at[high], right)
        self.left = copy(3, part.at[left, low], in_r.at[low], left)
        self.sums = (
            copy(4, sum_r, in_l.at[low], right),
            copy(5, sum_l, in_r.at[high], left),
        )

    def send_far(self):
        for c in self.far:
            c.start()

    def send_left(self):
        self.left.start()

    def send_right(self):
        self.right.start()

    def send_sums(self):
        me, right, left = self.ids
        far_l, far_r, sum_l, sum_r, in_l, in_r = self.bufs
        n = self.n_low
        self.far[0].wait_recv()
        sum_r[...] = (self.part[right, :n, :].astype(F32) + far_l[...].astype(F32)).astype(BF16)
        self.sums[0].start()
        self.far[1].wait_recv()
        sum_l[...] = (self.part[left, n:, :].astype(F32) + far_r[...].astype(F32)).astype(BF16)
        self.sums[1].start()

    def total(self):
        for c in (self.right, self.left, *self.sums):
            c.wait_recv()
        in_l, in_r = self.bufs[4:]
        return self.part[self.ids[0]].astype(F32) + in_l[...].astype(F32) + in_r[...].astype(F32)

    def wait_send(self):
        for c in (*self.far, self.right, self.left, *self.sums):
            c.wait_send()


def scatter_buffers(rows, width):
    low, high = halves(rows)
    sizes = (low.size, high.size, high.size, low.size, rows, rows)
    return [pltpu.VMEM((n, width), BF16) for n in sizes]


PAD = 32


class Exchange:
    def __init__(self, src, dst, send, recv):
        self.src, self.dst, self.send, self.recv = src, dst, send, recv
        self.me, self.count = lax.axis_index("exp"), lax.axis_size("exp")

    def copy(self, k):
        peer = lax.rem(self.me + k, self.count)
        return remote(
            self.src.at[peer], self.dst.at[self.me], self.send, self.recv, k, "exp", peer
        )

    def each(self, act):
        def body(k, carry):
            act(self.copy(k))
            return carry

        lax.fori_loop(1, self.count, body, 0)

    def start(self):
        self.each(lambda c: c.start())
        self.dst[self.me] = self.src[self.me]

    def wait_recv(self):
        self.each(lambda c: c.wait_recv())

    def wait_send(self):
        self.each(lambda c: c.wait_send())


def meet_all(partner=None):
    barrier = pltpu.get_barrier_semaphore()
    me, count = lax.axis_index("exp"), lax.axis_size("exp")

    def greet(k, carry):
        peer = lax.rem(me + k, count)
        pl.semaphore_signal(barrier, inc=1, device_id={"exp": peer}, device_id_type=MESH)
        return carry

    lax.fori_loop(1, count, greet, 0)
    ctx = lax.axis_index("ctx")
    right, left = lax.rem(ctx + 1, 4), lax.rem(ctx + 3, 4)
    for neighbour in (left, right):
        pl.semaphore_signal(barrier, inc=1, device_id={"ctx": neighbour}, device_id_type=MESH)
    if partner is not None:
        pl.semaphore_signal(barrier, inc=1, device_id={"section": partner}, device_id_type=MESH)
    pl.semaphore_wait(barrier, count + (1 if partner is None else 2))
    return ctx, right, left


def run_experts(
    ids, rows, out_ref, sel_ref, all_ref, ret_ref, block, beside, scratch
):
    inbox, part, res = scratch[:3]
    bufs = scratch[3:9]
    s_in, r_in, s_out, r_out, s_ag, r_ag, s_rs, r_rs = scratch[9:]
    me, right, left = ids
    far = lax.rem(me + 2, 4)
    flat = inbox.shape[0] * inbox.shape[1]
    width = inbox.shape[2]

    arriving = Exchange(out_ref, inbox, s_in, r_in)
    arriving.start()
    beside[0]()
    arriving.wait_recv()
    all_ref[me] = mm(sel_ref[...], inbox[...].reshape(flat, width)).astype(BF16)
    gather = RingGather(all_ref, rows, ids, s_ag, r_ag)
    scatter = RingScatter(part, rows, ids, bufs, s_rs, r_rs)
    gather.start()
    block(me, part)
    gather.forward()
    gather.wait_left()
    block(left, part)
    scatter.send_left()
    gather.wait_right()
    block(right, part)
    scatter.send_right()
    gather.wait_far()
    block(far, part)
    scatter.send_far()
    beside[1]()
    scatter.send_sums()
    beside[2]()
    padded = mm_tn(sel_ref[...], scatter.total().astype(BF16)).astype(BF16)
    res[...] = padded.reshape(res.shape)
    leaving = Exchange(res, ret_ref, s_out, r_out)
    leaving.start()
    beside[3]()
    leaving.wait_recv()
    gather.wait_send()
    scatter.wait_send()
    arriving.wait_send()
    leaving.wait_send()


def expert_scratch(experts, rows, width):
    v = lambda *shape: pltpu.VMEM((*shape, width), BF16)
    return [
        v(experts, PAD),
        v(4, rows),
        v(experts, PAD),
        *scatter_buffers(rows, width),
        *[pltpu.SemaphoreType.DMA((experts,))] * 4,
        *[pltpu.SemaphoreType.DMA((6,))] * 4,
    ]


def route_tables(routes_ref, experts):
    rows = routes_ref.shape[0]
    routes = routes_ref[...]
    lanes = lax.broadcasted_iota(jnp.int32, (rows, experts), 1)
    hot = [jnp.where(routes[:, c : c + 1] == lanes, 1.0, 0.0) for c in range(TOP)]
    row = lax.broadcasted_iota(jnp.int32, (rows, rows), 0)
    col = lax.broadcasted_iota(jnp.int32, (rows, rows), 1)
    before = jnp.where(row > col, 1.0, 0.0).astype(BF16)
    earlier = mm(before, (hot[0] + hot[1]).astype(BF16))
    wide = lax.broadcasted_iota(jnp.int32, (rows, experts * PAD), 1).astype(F32)
    slots = []
    for c in range(TOP):
        slot = jnp.sum(hot[c] * earlier, -1, keepdims=True)
        target = routes[:, c : c + 1].astype(F32) * PAD + slot
        slots.append(jnp.where(wide == target, 1.0, 0.0).astype(BF16))
    return hot, slots


def gates_of(logits, hot):
    chosen = [jnp.sum(h * logits, -1, keepdims=True) for h in hot]
    peak = jnp.maximum(chosen[0], chosen[1])
    raised = [jnp.exp(c - peak) for c in chosen]
    total = 1.0 / (raised[0] + raised[1])
    return [r * total for r in raised]


def selection(experts, capacity):
    sel = np.zeros((experts * capacity, experts, PAD), np.float32)
    for e in range(experts):
        for s in range(capacity):
            sel[e * capacity + s, e, s] = 1
    return jnp.asarray(sel.reshape(experts * capacity, experts * PAD), BF16)


def experts_forward(outgoing, sel, w_in, w_back):
    experts, _, width = outgoing.shape
    rows = sel.shape[0]
    vm = pl.BlockSpec(memory_space=pltpu.VMEM)
    return pl.pallas_call(
        functools.partial(experts_kernel, rows),
        out_shape=(
            jax.ShapeDtypeStruct(outgoing.shape, BF16),
            jax.ShapeDtypeStruct((4, rows, width), BF16),
            jax.ShapeDtypeStruct((4, rows, w_in.shape[1]), F32),
        ),
        in_specs=[vm] * 4,
        out_specs=(vm,) * 3,
        scratch_shapes=expert_scratch(experts, rows, width),
        compiler_params=pltpu.CompilerParams(
            collective_id=2, has_side_effects=True, vmem_limit_bytes=48 << 20
        ),
    )(outgoing, sel, w_in, w_back)


def experts_backward(outgoing, sel, w_in, w_back, entering, pre):
    experts, _, width = outgoing.shape
    rows, hid = sel.shape[0], w_in.shape[1]
    vm = pl.BlockSpec(memory_space=pltpu.VMEM)
    return pl.pallas_call(
        functools.partial(experts_back_kernel, rows),
        out_shape=(
            jax.ShapeDtypeStruct(outgoing.shape, BF16),
            jax.ShapeDtypeStruct(w_in.shape, F32),
            jax.ShapeDtypeStruct(w_back.shape, F32),
            jax.ShapeDtypeStruct(w_in.shape, BF16),
            jax.ShapeDtypeStruct(w_back.shape, BF16),
        ),
        in_specs=[vm] * 6,
        out_specs=(vm,) * 5,
        scratch_shapes=[
            pltpu.VMEM((4, rows, width), BF16),
            pltpu.VMEM((4, rows, hid), BF16),
            pltpu.VMEM((4, rows, hid), BF16),
            *expert_scratch(experts, rows, width),
        ],
        compiler_params=pltpu.CompilerParams(
            collective_id=3, has_side_effects=True, vmem_limit_bytes=48 << 20
        ),
    )(outgoing, sel, w_in, w_back, entering, pre)


def bucket_bounds():
    half = BUCKETS // 2
    powers = np.arange(1, BUCKETS - half) / (BUCKETS - half)
    return [int(m) for m in np.ceil(half * (REACH / half) ** powers)]


def tile_buckets(kind):
    row = lax.broadcasted_iota(jnp.int32, (SPAN, 2 * SPAN), 0)
    col = lax.broadcasted_iota(jnp.int32, (SPAN, 2 * SPAN), 1)
    ahead = kind * SPAN + row - lax.rem(col, SPAN)
    n = jnp.maximum(ahead, 0)
    bucket = jnp.minimum(n, BUCKETS // 2)
    for bound in bucket_bounds():
        bucket += (n >= bound).astype(jnp.int32)
    return ahead, bucket


def tile_range(kind):
    half = BUCKETS // 2
    ends = [max(kind * SPAN + r - c, 0) for r, c in ((0, SPAN - 1), (SPAN - 1, 0))]
    first, last = (min(n, half) + sum(n >= m for m in bucket_bounds()) for n in ends)
    return range(first, last + 1)


def make_tiles(table_ref, tiles_ref, heads):
    repeat = tiles_ref.shape[3] // (2 * SPAN)
    for k in range(KINDS - 1):
        ahead, bucket = tile_buckets(k)
        for h in range(heads):
            tile = jnp.full(bucket.shape, NEG, F32)
            for b in tile_range(k):
                tile = jnp.where(bucket == b, table_ref[b : b + 1, h : h + 1], tile)
            tile = jnp.where(ahead < 0, NEG, tile)
            tiles_ref[h, k] = jnp.concatenate([tile] * repeat, 1)


def bias_rows(tiles_ref, table_ref, kind_ref, head, block):
    kind = kind_ref[block : block + 1, :]
    last = table_ref[BUCKETS - 1 : BUCKETS, head : head + 1]
    rows = jnp.where(kind == 3, last, NEG)
    for k in (2, 1, 0):
        rows = jnp.where(kind == k, tiles_ref[head, k], rows)
    return rows


def head_columns(ref, group, head, heads):
    at = (group * heads + head) * HEAD_DIM
    return ref[:, at : at + HEAD_DIM]


def attend(
    ids, x, gain_ref, w_qkv, w_out, table_ref, kind_ref, all_ref, proj_ref, att_ref,
    tiles_ref, s_ref, p_ref, part, scratch
):
    bufs, (s_ag, r_ag, s_rs, r_rs) = scratch[:6], scratch[6:]
    me, right, left = ids
    far = lax.rem(me + 2, 4)
    rows, width = x.shape
    seq = 4 * rows
    heads = w_out.shape[0] // HEAD_DIM
    all_ref[me] = norm(x, gain_ref[...])
    gather = RingGather(all_ref, rows, ids, s_ag, r_ag)
    gather.start()
    make_tiles(table_ref, tiles_ref, heads)
    gather.forward()
    gather.wait_left()
    gather.wait_right()
    gather.wait_far()
    proj_ref[...] = mm(all_ref[...].reshape(seq, width), w_qkv[...]).astype(BF16)
    parts = []
    for h in range(heads):
        q, k, v = (head_columns(proj_ref, g, h, heads) for g in range(3))
        s_ref[...] = mm_nt(q, k)
        for b in range(seq // SPAN):
            at = slice(b * SPAN, (b + 1) * SPAN)
            s = s_ref[at, :] * HEAD_DIM**-0.5 + bias_rows(tiles_ref, table_ref, kind_ref, h, b)
            e = jnp.exp(s - jnp.max(s, -1, keepdims=True))
            p_ref[at, :] = (e * (1.0 / jnp.sum(e, -1, keepdims=True))).astype(BF16)
        parts.append(mm(p_ref[...], v).astype(BF16))
    att_ref[...] = jnp.concatenate(parts, 1).reshape(att_ref.shape)
    scatter = RingScatter(part, rows, ids, bufs, s_rs, r_rs)
    part[far] = mm(att_ref[far], w_out[...]).astype(BF16)
    scatter.send_far()
    part[right] = mm(att_ref[right], w_out[...]).astype(BF16)
    scatter.send_right()
    part[left] = mm(att_ref[left], w_out[...]).astype(BF16)
    scatter.send_left()
    part[me] = mm(att_ref[me], w_out[...]).astype(BF16)
    scatter.send_sums()
    total = scatter.total()
    gather.wait_send()
    scatter.wait_send()
    return total


def attend_back(
    ids, dmiddle, all_ref, proj_ref, att_ref, w_qkv, w_out, table_ref, kind_ref,
    perm_ref, perm_out_ref, pq_ref, po_ref, dtable_ref, ready,
    tiles_ref, dtiles_ref, s_ref, dp_ref, p_ref, ds_ref, da_ref, dproj_ref, db_ref, part, scratch
):
    bufs, (s_ag, r_ag, s_rs, r_rs) = scratch[:6], scratch[6:]
    me, right, left = ids
    far = lax.rem(me + 2, 4)
    rows, width = dmiddle.shape
    seq = 4 * rows
    heads = w_out.shape[0] // HEAD_DIM
    scale = HEAD_DIM**-0.5
    db_ref[me] = dmiddle.astype(BF16)
    gather = RingGather(db_ref, rows, ids, s_ag, r_ag)
    gather.start()
    make_tiles(table_ref, tiles_ref, heads)
    gather.forward()
    gather.wait_left()
    gather.wait_right()
    gather.wait_far()
    da_ref[...] = mm_nt(db_ref[...].reshape(seq, width), w_out[...]).astype(BF16)
    dq, dk, dv = [], [], []
    for h in range(heads):
        q, k, v = (head_columns(proj_ref, g, h, heads) for g in range(3))
        da = head_columns(da_ref, 0, h, heads)
        s_ref[...] = mm_nt(q, k)
        dp_ref[...] = mm_nt(da, v)
        dtiles_ref[...] = jnp.zeros(dtiles_ref.shape, F32)
        for b in range(seq // SPAN):
            at = slice(b * SPAN, (b + 1) * SPAN)
            s = s_ref[at, :] * scale + bias_rows(tiles_ref, table_ref, kind_ref, h, b)
            e = jnp.exp(s - jnp.max(s, -1, keepdims=True))
            p = e * (1.0 / jnp.sum(e, -1, keepdims=True))
            dp = dp_ref[at, :]
            ds = p * (dp - jnp.sum(p * dp, -1, keepdims=True))
            p_ref[at, :] = p.astype(BF16)
            ds_ref[at, :] = ds.astype(BF16)
            kind = kind_ref[b : b + 1, :]
            for n in range(KINDS):
                dtiles_ref[n] += jnp.where(kind == n, ds, 0.0)
        for n in range(KINDS):
            folded = dtiles_ref[n, :, : 2 * SPAN]
            for m in range(1, seq // (2 * SPAN)):
                folded = folded + dtiles_ref[n, :, m * 2 * SPAN : (m + 1) * 2 * SPAN]
            dtiles_ref[n, :, : 2 * SPAN] = folded
        sums = [jnp.zeros((1, 2 * SPAN), F32)] * BUCKETS
        for n in range(KINDS - 1):
            bucket = tile_buckets(n)[1]
            folded = dtiles_ref[n, :, : 2 * SPAN]
            for b in tile_range(n):
                hit = jnp.where(bucket == b, folded, 0.0)
                sums[b] = sums[b] + jnp.sum(hit, 0, keepdims=True)
        rest = dtiles_ref[KINDS - 1, :, : 2 * SPAN]
        sums[-1] = sums[-1] + jnp.sum(rest, 0, keepdims=True)
        dtable_ref[h] = jnp.concatenate(sums, 0)
        p = p_ref[...]
        ds = ds_ref[...]
        dq.append((mm(ds, k) * scale).astype(BF16))
        dk.append((mm_tn(ds, q) * scale).astype(BF16))
        dv.append(mm_tn(p, da).astype(BF16))
    dproj_ref[...] = jnp.concatenate(dq + dk + dv, 1).reshape(dproj_ref.shape)
    scatter = RingScatter(part, rows, ids, bufs, s_rs, r_rs)
    part[far] = mm_nt(dproj_ref[far], w_qkv[...]).astype(BF16)
    scatter.send_far()
    part[right] = mm_nt(dproj_ref[right], w_qkv[...]).astype(BF16)
    scatter.send_right()
    part[left] = mm_nt(dproj_ref[left], w_qkv[...]).astype(BF16)
    scatter.send_left()
    part[me] = mm_nt(dproj_ref[me], w_qkv[...]).astype(BF16)
    dproj = dproj_ref[...].reshape(seq, dproj_ref.shape[2])
    d_qkv = mm_tn(all_ref[...].reshape(seq, width), dproj).astype(BF16)
    pq_ref[...] = mm(perm_ref[...], d_qkv).astype(BF16)
    ready(0)
    scatter.send_sums()
    d_out = mm_tn(att_ref[...].reshape(seq, att_ref.shape[2]), db_ref[...].reshape(seq, width))
    po_ref[...] = mm(perm_out_ref[...], d_out.astype(BF16)).astype(BF16)
    ready(1)
    total = scatter.total()
    gather.wait_send()
    scatter.wait_send()
    return total


def layer_kernel(
    x_ref, gain_one, gain_two, w_qkv, w_out, table_ref, kind_ref, router_ref, routes_ref,
    sel_ref, w_in, w_back,
    h_ref, all_ref, proj_ref, att_ref, middle_ref, mixed_ref, logits_ref, picked_ref,
    ent_ref, pre_ref, *scratch
):
    tiles_ref, s_ref, p_ref, part, out_ref, ret_ref = scratch[:6]
    ids = meet_all()
    rows, width = x_ref.shape
    x = x_ref[...].astype(F32)
    branch = attend(
        ids, x, gain_one, w_qkv, w_out, table_ref, kind_ref, all_ref, proj_ref, att_ref,
        tiles_ref, s_ref, p_ref, part, scratch[6:16]
    )
    middle = x + branch
    middle_ref[...] = middle
    mixed = norm(middle, gain_two[...])
    mixed_ref[...] = mixed
    hot, slots = route_tables(routes_ref, out_ref.shape[0])
    out_ref[...] = mm_tn(slots[0] + slots[1], mixed).astype(BF16).reshape(out_ref.shape)

    def block(j, part):
        pre = mm(ent_ref[j], w_in[...])
        pre_ref[j] = pre
        hidden = gelu_parts(pre)[0].astype(BF16)
        part[j] = mm_nt(hidden, w_back[...]).astype(BF16)

    def find_logits():
        logits_ref[...] = mm(mixed_ref[...], router_ref[...])

    nothing = lambda: None
    run_experts(
        ids, sel_ref.shape[0], out_ref, sel_ref, ent_ref, ret_ref, block,
        (find_logits, nothing, nothing, nothing), scratch[16:]
    )
    gates = gates_of(logits_ref[...], hot)
    returned = ret_ref[...].reshape(slots[0].shape[1], width)
    y = middle_ref[...]
    for c in range(TOP):
        picked = mm(slots[c], returned)
        picked_ref[c] = picked.astype(BF16)
        y = y + gates[c] * picked
    h_ref[...] = y.astype(BF16)


def layer_forward(x, weights, kind, routes, sel):
    w_qkv, w_out, gain_one, gain_two, table, router, w_in, w_back = weights
    rows, width = x.shape
    seq, part, experts = 4 * rows, w_out.shape[0], router.shape[1]
    heads, slots = part // HEAD_DIM, sel.shape[0]
    vm = pl.BlockSpec(memory_space=pltpu.VMEM)
    shape = jax.ShapeDtypeStruct
    return pl.pallas_call(
        layer_kernel,
        out_shape=(
            shape(x.shape, BF16),
            shape((4, rows, width), BF16),
            shape((seq, 3 * part), BF16),
            shape((4, rows, part), BF16),
            shape(x.shape, F32),
            shape(x.shape, BF16),
            shape((rows, experts), F32),
            shape((TOP, rows, width), BF16),
            shape((4, slots, width), BF16),
            shape((4, slots, w_in.shape[1]), F32),
        ),
        in_specs=[vm] * 12,
        out_specs=(vm,) * 10,
        scratch_shapes=[
            pltpu.VMEM((heads, KINDS - 1, SPAN, seq), F32),
            pltpu.VMEM((seq, seq), F32),
            pltpu.VMEM((seq, seq), BF16),
            pltpu.VMEM((4, rows, width), BF16),
            pltpu.VMEM((experts, PAD, width), BF16),
            pltpu.VMEM((experts, PAD, width), BF16),
            *scatter_buffers(rows, width),
            *[pltpu.SemaphoreType.DMA((6,))] * 4,
            *expert_scratch(experts, slots, width),
        ],
        compiler_params=pltpu.CompilerParams(
            collective_id=0, has_side_effects=True, vmem_limit_bytes=56 << 20
        ),
    )(x, gain_one, gain_two, w_qkv, w_out, table, kind, router, routes, sel, w_in, w_back)


def layer_back_kernel(
    g_ref, x_ref, gain_one, gain_two, w_qkv, w_out, table_ref, kind_ref, router_ref, routes_ref,
    sel_ref, w_in, w_back, perm_ref, perm_out_ref,
    all_ref, proj_ref, att_ref, middle_ref, mixed_ref, logits_ref, picked_ref, ent_ref, pre_ref,
    dx_ref, dxb_ref, dgain_one, dgain_two, drouter_ref, pq_ref, po_ref, dtable_ref,
    d_in, d_back, got_in, got_back, got_pq, got_po, *scratch
):
    (
        tiles_ref, dtiles_ref, s_ref, dp_ref, p_ref, ds_ref, da_ref, dproj_ref, db_ref, part,
        out_ref, ret_ref, darr_ref, hid_ref, dpre_ref, e_in, e_back, s_x, r_x
    ) = scratch[:19]
    partner = 1 - lax.axis_index("section")
    ids = meet_all(partner)
    rows, width = x_ref.shape

    def across(k, src, dst):
        return remote(src, dst, s_x, r_x, k, "section", partner)

    crossing = [
        across(0, e_back, got_back),
        across(1, e_in, got_in),
        across(2, pq_ref, got_pq),
        across(3, po_ref, got_po),
    ]
    g = g_ref[...].astype(F32)
    hot, slots = route_tables(routes_ref, out_ref.shape[0])
    gates = gates_of(logits_ref[...], hot)
    dreturned = mm_tn(slots[0], (gates[0] * g).astype(BF16)) + mm_tn(
        slots[1], (gates[1] * g).astype(BF16)
    )
    out_ref[...] = dreturned.astype(BF16).reshape(out_ref.shape)

    def logits_back():
        g = g_ref[...].astype(F32)
        dgates = [
            jnp.sum(g * picked_ref[c].astype(F32), -1, keepdims=True) for c in range(TOP)
        ]
        mean = gates[0] * dgates[0] + gates[1] * dgates[1]
        dchosen = [a * (b - mean) for a, b in zip(gates, dgates)]
        dlogits = (hot[0] * dchosen[0] + hot[1] * dchosen[1]).astype(BF16)
        drouter_ref[...] = mm_tn(mixed_ref[...], dlogits)
        dx_ref[...] = mm_nt(dlogits, router_ref[...])

    def block(j, part):
        hidden, slope = gelu_parts(pre_ref[j])
        hid_ref[j] = hidden.astype(BF16)
        dpre = (mm(darr_ref[j], w_back[...]) * slope).astype(BF16)
        dpre_ref[j] = dpre
        part[j] = mm_nt(dpre, w_in[...]).astype(BF16)

    def flat(ref):
        return ref[...].reshape(ref.shape[0] * ref.shape[1], ref.shape[2])

    def back_grad():
        grad = mm_tn(flat(darr_ref), flat(hid_ref))
        d_back[...] = grad
        e_back[...] = grad.astype(BF16)
        crossing[0].start()

    def in_grad():
        grad = mm_tn(flat(ent_ref), flat(dpre_ref))
        d_in[...] = grad
        e_in[...] = grad.astype(BF16)
        crossing[1].start()

    run_experts(
        ids, sel_ref.shape[0], out_ref, sel_ref, darr_ref, ret_ref, block,
        (logits_back, back_grad, lambda: None, in_grad), scratch[29:]
    )
    dleft = ret_ref[...].reshape(slots[0].shape[1], width)
    dmixed = mm(slots[0] + slots[1], dleft) + dx_ref[...]
    dnorm, dgain = norm_back(middle_ref[...], gain_two[...], dmixed)
    dgain_two[...] = dgain
    dmiddle = g_ref[...].astype(F32) + dnorm
    dx_ref[...] = dmiddle
    dnormed = attend_back(
        ids, dmiddle, all_ref, proj_ref, att_ref, w_qkv, w_out, table_ref, kind_ref,
        perm_ref, perm_out_ref, pq_ref, po_ref, dtable_ref, lambda k: crossing[2 + k].start(),
        tiles_ref, dtiles_ref, s_ref, dp_ref, p_ref, ds_ref, da_ref, dproj_ref, db_ref, part,
        scratch[19:29]
    )
    dnorm, dgain = norm_back(x_ref[...].astype(F32), gain_one[...], dnormed)
    dgain_one[...] = dgain
    dx = dx_ref[...] + dnorm
    dx_ref[...] = dx
    dxb_ref[...] = dx.astype(BF16)
    for c in crossing:
        c.wait()


def layer_backward(g, keep, weights, kind, routes, sel, perm, perm_out):
    x, *saved = keep
    w_qkv, w_out, gain_one, gain_two, table, router, w_in, w_back = weights
    rows, width = x.shape
    seq, part, experts = 4 * rows, w_out.shape[0], router.shape[1]
    heads, slots, hid = part // HEAD_DIM, sel.shape[0], w_in.shape[1]
    vm = pl.BlockSpec(memory_space=pltpu.VMEM)
    shape = jax.ShapeDtypeStruct
    pq = shape((perm.shape[0], 3 * part), BF16)
    po = shape((perm_out.shape[0], width), BF16)
    return pl.pallas_call(
        layer_back_kernel,
        out_shape=(
            shape(x.shape, F32),
            shape(x.shape, BF16),
            shape((1, width), F32),
            shape((1, width), F32),
            shape((width, experts), F32),
            pq,
            po,
            shape((heads, BUCKETS, 2 * SPAN), F32),
            shape(w_in.shape, F32),
            shape(w_back.shape, F32),
            shape(w_in.shape, BF16),
            shape(w_back.shape, BF16),
            pq,
            po,
        ),
        in_specs=[vm] * 24,
        out_specs=(vm,) * 14,
        scratch_shapes=[
            pltpu.VMEM((heads, KINDS - 1, SPAN, seq), F32),
            pltpu.VMEM((KINDS, SPAN, seq), F32),
            pltpu.VMEM((seq, seq), F32),
            pltpu.VMEM((seq, seq), F32),
            pltpu.VMEM((seq, seq), BF16),
            pltpu.VMEM((seq, seq), BF16),
            pltpu.VMEM((seq, part), BF16),
            pltpu.VMEM((4, rows, 3 * part), BF16),
            pltpu.VMEM((4, rows, width), BF16),
            pltpu.VMEM((4, rows, width), BF16),
            pltpu.VMEM((experts, PAD, width), BF16),
            pltpu.VMEM((experts, PAD, width), BF16),
            pltpu.VMEM((4, slots, width), BF16),
            pltpu.VMEM((4, slots, hid), BF16),
            pltpu.VMEM((4, slots, hid), BF16),
            pltpu.VMEM(w_in.shape, BF16),
            pltpu.VMEM(w_back.shape, BF16),
            *[pltpu.SemaphoreType.DMA((4,))] * 2,
            *scatter_buffers(rows, width),
            *[pltpu.SemaphoreType.DMA((6,))] * 4,
            *expert_scratch(experts, slots, width),
        ],
        compiler_params=pltpu.CompilerParams(
            collective_id=1, has_side_effects=True, vmem_limit_bytes=60 << 20
        ),
    )(
        g, x, gain_one, gain_two, w_qkv, w_out, table, kind, router, routes, sel, w_in, w_back,
        perm, perm_out, *saved
    )


def meet_everyone():
    barrier = pltpu.get_barrier_semaphore()
    peers = [("exp", 16), ("ctx", 4), ("section", 2)]
    for axis, count in peers:
        me = lax.axis_index(axis)

        def greet(k, carry, axis=axis, me=me, count=count):
            peer = lax.rem(me + k, count)
            pl.semaphore_signal(barrier, inc=1, device_id={axis: peer}, device_id_type=MESH)
            return carry

        lax.fori_loop(1, count, greet, 0)
    pl.semaphore_wait(barrier, sum(count - 1 for _, count in peers))


def ctx_exchange(src, dst, send, recv):
    me = lax.axis_index("ctx")
    copies = []
    for k in (1, 3, 2):
        peer = lax.rem(me + k, 4)
        copies.append(remote(src.at[peer], dst.at[me], send, recv, k, "ctx", peer))
    return copies


def weights_kernel(
    cols_ref, outp_ref, w_in, w_back, perm_ref, perm_out_ref, pick_ref,
    w_qkv, w_out, small_ref, both_in, both_back,
    zin, grid, grid_out, s_z, r_z, s_q, r_q, s_o, r_o, s_fq, r_fq, s_fo, r_fo, s_x, r_x, s_own
):
    meet_everyone()
    section, ctx, exp = (lax.axis_index(a) for a in ("section", "ctx", "exp"))
    partner = 1 - section
    count = grid.shape[1]
    turn = ctx_exchange(cols_ref, zin, s_z, r_z)
    for c in turn:
        c.start()
    zin[ctx] = cols_ref[ctx]
    grid_out[section, exp] = outp_ref[...]

    def spread(ref, send, recv, k):
        peer = lax.rem(exp + k, count)
        at = ref.at[section, exp]
        return remote(at, at, send, recv, k, "exp", peer)

    def forward(ref, send, recv, k):
        at = ref.at[section, lax.rem(exp + count - k, count)]
        return remote(at, at, send, recv, k, "section", partner)

    def each(act, first=1):
        def body(k, carry):
            act(k)
            return carry

        lax.fori_loop(first, count, body, 0)

    each(lambda k: spread(grid_out, s_o, r_o, k).start())
    for c in turn:
        c.wait_recv()
    grid[section, exp] = zin[...].reshape(grid.shape[2:])
    each(lambda k: spread(grid, s_q, r_q, k).start())
    forward(grid, s_fq, r_fq, 0).start()
    forward(grid_out, s_fo, r_fo, 0).start()
    own_in = pltpu.make_async_copy(w_in, both_in.at[section], s_own.at[0])
    own_back = pltpu.make_async_copy(w_back, both_back.at[section], s_own.at[1])
    own_in.start()
    own_back.start()
    cross_in = remote(w_in, both_in.at[section], s_x, r_x, 0, "section", partner)
    cross_back = remote(w_back, both_back.at[section], s_x, r_x, 1, "section", partner)

    def relay(ref, s, r, sf, rf, k):
        spread(ref, s, r, k).wait_recv()
        forward(ref, sf, rf, k).start()

    each(lambda k: relay(grid_out, s_o, r_o, s_fo, r_fo, k))
    each(lambda k: relay(grid, s_q, r_q, s_fq, r_fq, k))
    cross_in.start()
    cross_back.start()

    def unpack(layer):
        flat = grid[layer].reshape(perm_ref.shape[0], grid.shape[3])
        w_qkv[layer] = mm_tn(perm_ref[...], flat).astype(BF16)
        small_ref[layer] = mm(pick_ref[...], flat)
        flat = grid_out[layer].reshape(perm_out_ref.shape[0], grid_out.shape[3])
        w_out[layer] = mm_tn(perm_out_ref[...], flat).astype(BF16)

    unpack(section)
    each(lambda k: forward(grid_out, s_fo, r_fo, k).wait_recv(), 0)
    each(lambda k: forward(grid, s_fq, r_fq, k).wait_recv(), 0)
    unpack(partner)
    each(lambda k: spread(grid_out, s_o, r_o, k).wait_send())
    each(lambda k: spread(grid, s_q, r_q, k).wait_send())
    each(lambda k: forward(grid_out, s_fo, r_fo, k).wait_send(), 0)
    each(lambda k: forward(grid, s_fq, r_fq, k).wait_send(), 0)
    for c in turn:
        c.wait_send()
    own_in.wait()
    own_back.wait()
    cross_in.wait()
    cross_back.wait()


def gather_weights(cols, outp, w_in, w_back, perm, perm_out, pick):
    width, part = outp.shape[1], cols.shape[2]
    count = perm_out.shape[0] // 16
    vm = pl.BlockSpec(memory_space=pltpu.VMEM)
    dma = lambda n: pltpu.SemaphoreType.DMA((n,))
    return pl.pallas_call(
        weights_kernel,
        out_shape=(
            jax.ShapeDtypeStruct((2, width, part), BF16),
            jax.ShapeDtypeStruct((2, perm_out.shape[1], width), BF16),
            jax.ShapeDtypeStruct((2, pick.shape[0], part), F32),
            jax.ShapeDtypeStruct((2, *w_in.shape), BF16),
            jax.ShapeDtypeStruct((2, *w_back.shape), BF16),
        ),
        in_specs=[vm] * 7,
        out_specs=(vm,) * 5,
        scratch_shapes=[
            pltpu.VMEM(cols.shape, BF16),
            pltpu.VMEM((2, count, 64, part), BF16),
            pltpu.VMEM((2, count, 16, width), BF16),
            dma(4), dma(4), *[dma(count)] * 8, dma(2), dma(2), dma(2),
        ],
        compiler_params=pltpu.CompilerParams(
            collective_id=4, has_side_effects=True, vmem_limit_bytes=48 << 20
        ),
    )(cols, outp, w_in, w_back, perm, perm_out, pick)


def owners_kernel(
    pq0, pq1, gq0, gq1, po0, po1, go0, go1, small_ref, spread_ref,
    in0, in1, gin0, gin1, back0, back1, gback0, gback1,
    turned, out_grad, d_in, d_back,
    got_small, pieces, box, pieces_out, box_out, summed, s_s, r_s, s_q, r_q, s_o, r_o, s_z, r_z
):
    meet_everyone()
    section, ctx, exp = (lax.axis_index(a) for a in ("section", "ctx", "exp"))
    partner = 1 - section
    first = section == 0
    cross = remote(small_ref.at[partner], got_small, s_s, r_s, 0, "section", partner)
    cross.start()

    def chosen(a, b, c, d):
        return jnp.where(first, a[...], b[...]).astype(F32) + jnp.where(
            first, c[...], d[...]
        ).astype(F32)

    pieces_out[...] = chosen(po0, po1, go0, go1).astype(BF16).reshape(pieces_out.shape)
    swap_out = Exchange(pieces_out, box_out, s_o, r_o)
    swap_out.start()
    dense = chosen(pq0, pq1, gq0, gq1)
    cross.wait_recv()
    small = small_ref[section] + got_small[...]
    wide = mm(spread_ref[...], small.astype(BF16))
    n = wide.shape[1]
    dense = jnp.concatenate([dense[:, :n] + wide, dense[:, n:]], 1)
    pieces[...] = dense.astype(BF16).reshape(pieces.shape)
    swap = Exchange(pieces, box, s_q, r_q)
    swap.start()
    d_in[...] = chosen(in0, in1, gin0, gin1)
    d_back[...] = chosen(back0, back1, gback0, gback1)
    swap_out.wait_recv()
    total = box_out[0].astype(F32)
    for k in range(1, box_out.shape[0]):
        total = total + box_out[k].astype(F32)
    out_grad[...] = total
    swap.wait_recv()
    total = box[0].astype(F32)
    for k in range(1, box.shape[0]):
        total = total + box[k].astype(F32)
    summed[...] = total.reshape(summed.shape)
    turn = ctx_exchange(summed, turned, s_z, r_z)
    for c in turn:
        c.start()
    turned[ctx] = summed[ctx]
    for c in turn:
        c.wait()
    cross.wait_send()
    swap.wait_send()
    swap_out.wait_send()


def sum_at_owners(pq, gq, po, go, small, spread, d_in, g_in, d_back, g_back, count):
    rows, part = pq[0].shape
    out_rows, width = po[0].shape
    vm = pl.BlockSpec(memory_space=pltpu.VMEM)
    dma = lambda n: pltpu.SemaphoreType.DMA((n,))
    own = (rows // count, part)
    own_out = (out_rows // count, width)
    quarter = (4, rows // count // 4, part)
    return pl.pallas_call(
        owners_kernel,
        out_shape=(
            jax.ShapeDtypeStruct(quarter, F32),
            jax.ShapeDtypeStruct(own_out, F32),
            jax.ShapeDtypeStruct(d_in[0].shape, F32),
            jax.ShapeDtypeStruct(d_back[0].shape, F32),
        ),
        in_specs=[vm] * 18,
        out_specs=(vm,) * 4,
        scratch_shapes=[
            pltpu.VMEM(small.shape[1:], F32),
            pltpu.VMEM((count, *own), BF16),
            pltpu.VMEM((count, *own), BF16),
            pltpu.VMEM((count, *own_out), BF16),
            pltpu.VMEM((count, *own_out), BF16),
            pltpu.VMEM(quarter, F32),
            dma(1), dma(1), *[dma(count)] * 4, dma(4), dma(4),
        ],
        compiler_params=pltpu.CompilerParams(
            collective_id=5, has_side_effects=True, vmem_limit_bytes=52 << 20
        ),
    )(*pq, *gq, *po, *go, small, spread, *d_in, *g_in, *d_back, *g_back)


def packing(n_ctx, n_exp, own_rows):
    blocks = n_ctx * n_exp
    perm = np.zeros((blocks, 16, blocks, own_rows), np.float32)
    pick = np.zeros((blocks, blocks, 16), np.float32)
    perm_out = np.zeros((n_exp, 16, n_exp, own_rows), np.float32)
    for e in range(n_exp):
        for i in range(own_rows):
            perm_out[e, i, e, i] = 1
        for c in range(n_ctx):
            for i in range(own_rows):
                perm[e * n_ctx + c, i, c * n_exp + e, i] = 1
            pick[c * n_exp + e, e * n_ctx + c, own_rows] = 1
    perm = perm.reshape(blocks * 16, blocks * own_rows)
    pick = pick.reshape(blocks, blocks * 16)
    perm_out = perm_out.reshape(n_exp * 16, n_exp * own_rows)
    return tuple(jnp.asarray(m, BF16) for m in (perm, pick, pick.T.copy(), perm_out))


def norm_scale(v):
    return lax.rsqrt(jnp.mean(v * v, -1, keepdims=True) + EPS)


def norm(v, gain):
    return (v * norm_scale(v) * gain).astype(BF16)


def norm_back(v, gain, du):
    r = norm_scale(v)
    dug = du * gain
    dv = r * dug - v * (r * r * r) * jnp.mean(dug * v, -1, keepdims=True)
    return dv, jnp.sum(du * v * r, 0, keepdims=True)


def gelu_parts(v):
    t = jnp.tanh(GELU_C * (v + 0.044715 * v * v * v))
    value = 0.5 * v * (1.0 + t)
    slope = 0.5 * (1.0 + t) + 0.5 * v * (1.0 - t * t) * GELU_C * (1.0 + 3 * 0.044715 * v * v)
    return value, slope


def on_device(
    inputs,
    cotangent,
    routes,
    block_order,
    attn_gain,
    qkv_weight,
    out_weight,
    rel_bias,
    moe_gain,
    router_weight,
    expert_in,
    expert_out,
):
    rows, width = inputs.shape[2:]
    n_ctx, n_exp = lax.axis_size("ctx"), lax.axis_size("exp")
    seq = rows * n_ctx
    own_rows = qkv_weight.shape[1]
    heads = HEADS // n_ctx
    part = heads * HEAD_DIM
    capacity = rows * TOP // n_exp + max(1, rows * TOP // (16 * n_exp))
    sel = selection(n_exp, capacity)
    section = lax.axis_index("section")
    ctx = lax.axis_index("ctx")
    first = section == 0

    perm, pick, place, perm_out = packing(n_ctx, n_exp, own_rows)
    small = jnp.concatenate(
        [attn_gain[0], moe_gain[0], rel_bias[0], router_weight[0].reshape(-1)]
    )
    n_small = small.shape[0]
    columns = qkv_weight[0].reshape(own_rows, 3, n_ctx, part).transpose(2, 0, 1, 3)
    columns = columns.reshape(n_ctx, own_rows, 3 * part)
    small_row = jnp.pad(small, (0, 3 * part - n_small))
    small_rows = jnp.broadcast_to(small_row, (n_ctx, 1, 3 * part))
    columns = jnp.concatenate([columns, small_rows], 1)
    columns = jnp.pad(columns, ((0, 0), (0, 15 - own_rows), (0, 0)))
    out_rows = jnp.pad(out_weight[0], ((0, 16 - own_rows), (0, 0)))
    w_qkv_both, w_out_both, small_both, w_in_both, w_back_both = gather_weights(
        columns, out_rows, expert_in[0, 0], expert_out[0, 0], perm, perm_out, pick
    )
    n_bias = BUCKETS * HEADS // (n_ctx * n_exp)

    def dense(layer):
        small = small_both[layer]
        gain_one = small[:, :own_rows].reshape(1, width)
        gain_two = small[:, own_rows : 2 * own_rows].reshape(1, width)
        table = small[:, 2 * own_rows : 2 * own_rows + n_bias].reshape(BUCKETS, HEADS)
        table = lax.dynamic_slice_in_dim(table, ctx * heads, heads, 1)
        router = small[:, 2 * own_rows + n_bias : n_small].reshape(width, n_exp).astype(BF16)
        return (
            w_qkv_both[layer], w_out_both[layer], gain_one, gain_two, table, router,
            w_in_both[layer], w_back_both[layer],
        )

    weights = [dense(0), dense(1)]
    ahead = block_order[:, None] - block_order[None, :]
    kind = jnp.repeat(jnp.where(ahead < 0, -1, jnp.minimum(ahead, 3)), SPAN, 1)

    own_routes = routes[0, :, 0]
    kept = jnp.where(first, own_routes[0], own_routes[1])
    given = jnp.where(first, own_routes[1], own_routes[0])
    taken = lax.ppermute(given, "section", [(0, 1), (1, 0)])
    layer_routes = (jnp.where(first, kept, taken), jnp.where(first, taken, kept))
    def forward(x, layer):
        h, *saved = layer_forward(x, weights[layer], kind, layer_routes[layer], sel)
        return h, (x, *saved)

    def backward(g, keep, layer):
        (
            dx, dxb, d_gain_one, d_gain_two, d_router, pq, po, d_table,
            d_in, d_back, g_in, g_back, gq, go
        ) = layer_backward(
            g, keep, weights[layer], kind, layer_routes[layer], sel, perm, perm_out
        )
        d_table = jnp.repeat(jnp.sum(d_table, -1).T, 2, axis=0)
        owner = jnp.arange(n_ctx * n_exp)[:, None]
        d_table = jnp.where(owner % 2 == ctx // 2, d_table, 0.0)
        even = ctx % 2 == 0
        d_table = [jnp.where(even, d_table, 0.0), jnp.where(even, 0.0, d_table)]
        owners = (n_ctx * n_exp, -1)
        d_small = jnp.concatenate(
            [d_gain_one.reshape(owners), d_gain_two.reshape(owners), *d_table,
             d_router.reshape(owners)],
            1,
        )
        d_small = jnp.pad(d_small, ((0, 0), (0, 256 - n_small)))
        return dx, dxb, (pq, gq, po, go, d_small, d_in, g_in, d_back, g_back)

    def swap(x):
        return lax.ppermute(x, "section", [(0, 1), (1, 0)])

    x = jnp.where(first, inputs[0, 0], inputs[1, 0])
    cot = jnp.where(first, cotangent[0, 0], cotangent[1, 0])
    h, keep0 = forward(x, 0)
    top, keep1 = forward(h, 1)
    _, dh, grads1 = backward(cot, keep1, 1)
    dx, _, grads0 = backward(dh, keep0, 0)
    pq, gq, po, go, d_small, d_in, g_in, d_back, g_back = zip(grads0, grads1)
    pieces, out_grad, d_in, d_back = sum_at_owners(
        pq, gq, po, go, jnp.stack(d_small), place, d_in, g_in, d_back, g_back, n_exp
    )
    qkv_grad = pieces[:, :own_rows].reshape(n_ctx, own_rows, 3, part)
    qkv_grad = qkv_grad.transpose(1, 2, 0, 3).reshape(own_rows, 3 * width)
    out_grad = out_grad[:own_rows]
    small = jnp.sum(pieces[:, own_rows, :n_small], 0)

    other = swap(jnp.where(first, top, h))
    layer_out = jnp.where(
        first, jnp.stack([h, other]), jnp.stack([other, top])
    ).reshape(1, 2, 1, rows, width)
    dh = dh.astype(F32)
    other = swap(jnp.where(first, dh, dx))
    input_grad = jnp.where(
        first, jnp.stack([dx, other]), jnp.stack([other, dh])
    ).reshape(1, 2, 1, rows, width)
    return (
        layer_out,
        input_grad,
        small[:own_rows][None],
        qkv_grad[None],
        out_grad[None],
        small[2 * own_rows : 2 * own_rows + n_bias][None],
        small[own_rows : 2 * own_rows][None],
        small[2 * own_rows + n_bias :].reshape(1, own_rows, n_exp),
        d_in[None, None],
        d_back[None, None],
    )


def solution(mesh):
    return jax.shard_map(
        on_device,
        mesh=mesh,
        in_specs=(
            P(None, "exp", "ctx", None),
            P(None, "exp", "ctx", None),
            P("section", None, "exp", "ctx", None),
            P(),
            P("section", ("ctx", "exp")),
            P("section", ("ctx", "exp"), None),
            P("section", ("ctx", "exp"), None),
            P("section", ("ctx", "exp")),
            P("section", ("ctx", "exp")),
            P("section", ("ctx", "exp"), None),
            P("section", "exp", None, "ctx"),
            P("section", "exp", None, "ctx"),
        ),
        out_specs=(
            P("section", None, "exp", "ctx", None),
            P("section", None, "exp", "ctx", None),
            P("section", ("ctx", "exp")),
            P("section", ("ctx", "exp"), None),
            P("section", ("ctx", "exp"), None),
            P("section", ("ctx", "exp")),
            P("section", ("ctx", "exp")),
            P("section", ("ctx", "exp"), None),
            P("section", "exp", None, "ctx"),
            P("section", "exp", None, "ctx"),
        ),
        check_vma=False,
    )
```

```python
import functools
import math

import jax
import jax.numpy as jnp
import numpy as np
from jax import lax
from jax.experimental import pallas as pl
from jax.experimental.pallas import tpu as pltpu
from jax.sharding import PartitionSpec as P

HEADS = 12
HEAD_DIM = 64
BUCKETS = 32
REACH = 128
TOP = 2
EPS = 1e-06
NEG = -1e30
SPAN = 64
KINDS = 4
MESH = pl.DeviceIdType.MESH
BF16 = jnp.bfloat16
F32 = jnp.float32
GELU_C = math.sqrt(2.0 / math.pi)


def dot(a, b, dims):
    return lax.dot_general(a, b, (dims, ((), ())), preferred_element_type=F32)


def mm(a, b):
    return dot(a, b, ((1,), (0,)))


def mm_nt(a, b):
    return dot(a, b, ((1,), (1,)))


def mm_tn(a, b):
    return dot(a, b, ((0,), (0,)))


def meet_neighbours(axis, count):
    me = lax.axis_index(axis)
    right, left = lax.rem(me + 1, count), lax.rem(me + count - 1, count)
    barrier = pltpu.get_barrier_semaphore()
    for neighbour in (left, right):
        pl.semaphore_signal(barrier, inc=1, device_id={axis: neighbour}, device_id_type=MESH)
    pl.semaphore_wait(barrier, 2)
    return me, right, left


def remote(src, dst, send, recv, k, axis, to):
    return pltpu.make_async_remote_copy(
        src_ref=src,
        dst_ref=dst,
        send_sem=send.at[k],
        recv_sem=recv.at[k],
        device_id={axis: to},
        device_id_type=MESH,
    )


def halves(rows):
    first = (rows // 2 + 15) // 16 * 16
    return (pl.ds(0, first), pl.ds(first, rows - first))


def ring_copy(send, recv, k, src, dst, to):
    return remote(src, dst, send, recv, k, "ctx", to)


class RingGather:
    def __init__(self, all_ref, rows, ids, send, recv):
        me, right, left = ids
        low, high = halves(rows)

        def pass_on(k, slot, half, to):
            at = all_ref.at[slot, half]
            return ring_copy(send, recv, k, at, at, to)

        self.first = (
            pass_on(0, me, low, right),
            pass_on(1, me, high, left),
            pass_on(2, me, high, right),
            pass_on(3, me, low, left),
        )
        self.second = (pass_on(4, left, low, right), pass_on(5, right, high, left))

    def start(self):
        for c in self.first:
            c.start()

    def forward(self):
        self.first[0].wait_recv()
        self.second[0].start()
        self.first[1].wait_recv()
        self.second[1].start()

    def wait_left(self):
        self.first[2].wait_recv()

    def wait_right(self):
        self.first[3].wait_recv()

    def wait_far(self):
        for c in self.second:
            c.wait_recv()

    def wait_send(self):
        for c in self.first + self.second:
            c.wait_send()


class RingScatter:
    def __init__(self, part, rows, ids, bufs, send, recv):
        me, right, left = ids
        far = lax.rem(me + 2, 4)
        low, high = halves(rows)
        far_l, far_r, sum_l, sum_r, in_l, in_r = bufs
        self.part, self.ids, self.n_low, self.bufs = part, ids, low.size, bufs
        copy = functools.partial(ring_copy, send, recv)
        self.far = (
            copy(0, part.at[far, low], far_l, right),
            copy(1, part.at[far, high], far_r, left),
        )
        self.right = copy(2, part.at[right, high], in_l.at[high], right)
        self.left = copy(3, part.at[left, low], in_r.at[low], left)
        self.sums = (
            copy(4, sum_r, in_l.at[low], right),
            copy(5, sum_l, in_r.at[high], left),
        )

    def send_far(self):
        for c in self.far:
            c.start()

    def send_left(self):
        self.left.start()

    def send_right(self):
        self.right.start()

    def send_sums(self):
        me, right, left = self.ids
        far_l, far_r, sum_l, sum_r, in_l, in_r = self.bufs
        n = self.n_low
        self.far[0].wait_recv()
        sum_r[...] = (self.part[right, :n, :].astype(F32) + far_l[...].astype(F32)).astype(BF16)
        self.sums[0].start()
        self.far[1].wait_recv()
        sum_l[...] = (self.part[left, n:, :].astype(F32) + far_r[...].astype(F32)).astype(BF16)
        self.sums[1].start()

    def total(self):
        for c in (self.right, self.left, *self.sums):
            c.wait_recv()
        in_l, in_r = self.bufs[4:]
        return self.part[self.ids[0]].astype(F32) + in_l[...].astype(F32) + in_r[...].astype(F32)

    def wait_send(self):
        for c in (*self.far, self.right, self.left, *self.sums):
            c.wait_send()


def scatter_buffers(rows, width):
    low, high = halves(rows)
    sizes = (low.size, high.size, high.size, low.size, rows, rows)
    return [pltpu.VMEM((n, width), BF16) for n in sizes]


TILE = 16
PARTS = 2


class Loads:
    def __init__(self, sems):
        self.sems, self.copies = sems, []

    def start(self, src, dst):
        copy = pltpu.make_async_copy(src, dst, self.sems.at[len(self.copies)])
        copy.start()
        self.copies.append(copy)

    def wait(self, *which):
        for k in which:
            self.copies[k].wait()

    def wait_all(self):
        self.wait(*range(len(self.copies)))


def set_slots(main, extra, values):
    count = extra.shape[0]
    main[...] = values[: count * TILE].astype(BF16).reshape(main.shape)
    for e in range(count):
        extra[e] = values[count * TILE + e : count * TILE + e + 1]


def get_slots(main, extra):
    count = extra.shape[0]
    rows = [extra[e] for e in range(count)]
    first = main[...].reshape(count * TILE, main.shape[2])
    return jnp.concatenate([first, jnp.concatenate(rows, 0).astype(BF16)], 0)


class Exchange:
    def __init__(self, copy, send, recv):
        self.copy, self.send, self.recv = copy, send, recv
        self.me, self.count = lax.axis_index("exp"), lax.axis_size("exp")

    def each(self, act, first=1, last=None):
        def body(k, carry):
            act(self.copy(self, k))
            return carry

        lax.fori_loop(first, self.count if last is None else last, body, 0)

    def start(self, *span):
        self.each(lambda c: c.start(), *span)

    def wait_recv(self, *span):
        self.each(lambda c: c.wait_recv(), *span)

    def wait_send(self):
        self.each(lambda c: c.wait_send())

    def to(self, src, dst, k, peer):
        return remote(src, dst, self.send, self.recv, k, "exp", peer)


def exchange_out(src, dst, send, recv):
    def copy(x, k):
        peer = lax.rem(x.me + k, x.count)
        return x.to(src.at[peer], dst.at[k], k, peer)

    return Exchange(copy, send, recv)


def exchange_home(src, dst, send, recv):
    def copy(x, k):
        peer = lax.rem(x.me + x.count - k, x.count)
        return x.to(src.at[k], dst.at[x.me], k, peer)

    return Exchange(copy, send, recv)


def meet_all(partner=None):
    barrier = pltpu.get_barrier_semaphore()
    me, count = lax.axis_index("exp"), lax.axis_size("exp")

    def greet(k, carry):
        peer = lax.rem(me + k, count)
        pl.semaphore_signal(barrier, inc=1, device_id={"exp": peer}, device_id_type=MESH)
        return carry

    lax.fori_loop(1, count, greet, 0)
    ctx = lax.axis_index("ctx")
    right, left = lax.rem(ctx + 1, 4), lax.rem(ctx + 3, 4)
    for neighbour in (left, right):
        pl.semaphore_signal(barrier, inc=1, device_id={"ctx": neighbour}, device_id_type=MESH)
    if partner is not None:
        pl.semaphore_signal(barrier, inc=1, device_id={"section": partner}, device_id_type=MESH)
    pl.semaphore_wait(barrier, count + (1 if partner is None else 2))
    return ctx, right, left


def run_experts(ids, outs, all_ref, rets, block, done, beside, scratch):
    part = scratch[0]
    inbox, res = scratch[1:3], scratch[3:5]
    s_in, r_in, s_out, r_out = scratch[5:7], scratch[7:9], scratch[9:11], scratch[11:13]
    rest = scratch[13:]
    me, right, left = ids
    far = lax.rem(me + 2, 4)
    parts, _, rows, width = all_ref.shape
    near = inbox[0].shape[0] // parts
    filled = near * TILE
    exp = lax.axis_index("exp")
    arriving = [exchange_out(outs[m], inbox[m], s_in[m], r_in[m]) for m in range(2)]
    leaving = [exchange_home(res[m], rets[m], s_out[m], r_out[m]) for m in range(2)]
    gathers = [RingGather(all_ref.at[n], rows, ids, *rest[10 * n : 10 * n + 2]) for n in range(parts)]
    scatters = [
        RingScatter(
            part.at[n], rows, ids, rest[10 * n + 4 : 10 * n + 10], *rest[10 * n + 2 : 10 * n + 4]
        )
        for n in range(parts)
    ]
    for n in range(parts):
        for x in arriving:
            x.start(max(1, n * near), (n + 1) * near)
    for m in range(2):
        inbox[m][0] = outs[m][exp]
    beside[0]()
    for n in range(parts):
        for x in arriving:
            x.wait_recv(max(1, n * near), (n + 1) * near)
        all_ref[n, me, :filled] = inbox[0][n * near : (n + 1) * near].reshape(filled, width)
        last = [inbox[1][n * near + k] for k in range(near)]
        last.append(jnp.zeros((rows - filled - near, width), F32))
        all_ref[n, me, filled:] = jnp.concatenate(last, 0).astype(BF16)
        gathers[n].start()
    for n in range(parts):
        block(n, me, part)
    for g in gathers:
        g.forward()
    for n in range(parts):
        gathers[n].wait_left()
        block(n, left, part)
        scatters[n].send_left()
        gathers[n].wait_right()
        block(n, right, part)
        scatters[n].send_right()
        gathers[n].wait_far()
        block(n, far, part)
        scatters[n].send_far()
        done(n)
    beside[1]()
    for n in range(parts):
        scatters[n].send_sums()
    beside[2]()
    for n in range(parts):
        total = scatters[n].total().astype(BF16)
        res[0][n * near : (n + 1) * near] = total[:filled].reshape(near, TILE, width)
        last = total[filled:].astype(F32)
        for k in range(near):
            res[1][n * near + k] = last[k : k + 1]
        for x in leaving:
            x.start(max(1, n * near), (n + 1) * near)
    for m in range(2):
        rets[m][exp] = res[m][0]
    beside[3]()
    for x in leaving:
        x.wait_recv()
    for x in (*gathers, *scatters, *arriving, *leaving):
        x.wait_send()


def slot_buffers(experts, width):
    return [pltpu.VMEM((experts, TILE, width), BF16), pltpu.VMEM((experts, 1, width), F32)]


def expert_scratch(experts, rows, width):
    ring = [*[pltpu.SemaphoreType.DMA((6,))] * 4, *scatter_buffers(rows, width)]
    return [
        pltpu.VMEM((PARTS, 4, rows, width), BF16),
        *slot_buffers(experts, width) * 2,
        *[pltpu.SemaphoreType.DMA((experts,))] * 8,
        *ring * PARTS,
    ]


def route_tables(routes_ref, experts):
    rows = routes_ref.shape[0]
    routes = routes_ref[...]
    lanes = lax.broadcasted_iota(jnp.int32, (rows, experts), 1)
    hot = [jnp.where(routes[:, c : c + 1] == lanes, 1.0, 0.0) for c in range(TOP)]
    row = lax.broadcasted_iota(jnp.int32, (rows, rows), 0)
    col = lax.broadcasted_iota(jnp.int32, (rows, rows), 1)
    before = jnp.where(row > col, 1.0, 0.0).astype(BF16)
    earlier = mm(before, (hot[0] + hot[1]).astype(BF16))
    wide = lax.broadcasted_iota(jnp.int32, (rows, experts * (TILE + 1)), 1).astype(F32)
    slots = []
    for c in range(TOP):
        slot = jnp.sum(hot[c] * earlier, -1, keepdims=True)
        expert = routes[:, c : c + 1].astype(F32)
        target = jnp.where(slot < TILE, expert * TILE + slot, experts * TILE + expert)
        slots.append(jnp.where(wide == target, 1.0, 0.0).astype(BF16))
    return hot, slots


def gates_of(logits, hot):
    chosen = [jnp.sum(h * logits, -1, keepdims=True) for h in hot]
    peak = jnp.maximum(chosen[0], chosen[1])
    raised = [jnp.exp(c - peak) for c in chosen]
    total = 1.0 / (raised[0] + raised[1])
    return [r * total for r in raised]


def part_rows(experts, capacity):
    return -(-(experts // PARTS) * capacity // TILE) * TILE


def bucket_bounds():
    half = BUCKETS // 2
    powers = np.arange(1, BUCKETS - half) / (BUCKETS - half)
    return [int(m) for m in np.ceil(half * (REACH / half) ** powers)]


def tile_buckets(kind):
    row = lax.broadcasted_iota(jnp.int32, (SPAN, 2 * SPAN), 0)
    col = lax.broadcasted_iota(jnp.int32, (SPAN, 2 * SPAN), 1)
    ahead = kind * SPAN + row - lax.rem(col, SPAN)
    n = jnp.maximum(ahead, 0)
    bucket = jnp.minimum(n, BUCKETS // 2)
    for bound in bucket_bounds():
        bucket += (n >= bound).astype(jnp.int32)
    return ahead, bucket


def tile_range(kind):
    half = BUCKETS // 2
    ends = [max(kind * SPAN + r - c, 0) for r, c in ((0, SPAN - 1), (SPAN - 1, 0))]
    first, last = (min(n, half) + sum(n >= m for m in bucket_bounds()) for n in ends)
    return range(first, last + 1)


def make_tiles(table_ref, tiles_ref, heads):
    repeat = tiles_ref.shape[3] // (2 * SPAN)
    for k in range(KINDS - 1):
        ahead, bucket = tile_buckets(k)
        for h in range(heads):
            tile = jnp.full(bucket.shape, NEG, F32)
            for b in tile_range(k):
                tile = jnp.where(bucket == b, table_ref[b : b + 1, h : h + 1], tile)
            tile = jnp.where(ahead < 0, NEG, tile)
            tiles_ref[h, k] = jnp.concatenate([tile] * repeat, 1)


def bias_rows(tiles_ref, table_ref, kind_ref, head, block):
    kind = kind_ref[block : block + 1, :]
    last = table_ref[BUCKETS - 1 : BUCKETS, head : head + 1]
    rows = jnp.where(kind == 3, last, NEG)
    for k in (2, 1, 0):
        rows = jnp.where(kind == k, tiles_ref[head, k], rows)
    return rows


def head_columns(ref, group, head, heads):
    at = (group * heads + head) * HEAD_DIM
    return ref[:, at : at + HEAD_DIM]


def attend(
    ids, x, gain_ref, w_qkv, w_out, table_ref, kind_ref, all_ref, proj_ref, att_ref,
    tiles_ref, s_ref, p_ref, part, scratch
):
    bufs, (s_ag, r_ag, s_rs, r_rs) = scratch[:6], scratch[6:]
    me, right, left = ids
    far = lax.rem(me + 2, 4)
    rows, width = x.shape
    seq = 4 * rows
    heads = w_out.shape[0] // HEAD_DIM
    all_ref[me] = norm(x, gain_ref[...])
    gather = RingGather(all_ref, rows, ids, s_ag, r_ag)
    gather.start()
    make_tiles(table_ref, tiles_ref, heads)
    gather.forward()
    gather.wait_left()
    gather.wait_right()
    gather.wait_far()
    proj_ref[...] = mm(all_ref[...].reshape(seq, width), w_qkv[...]).astype(BF16)
    parts = []
    for h in range(heads):
        q, k, v = (head_columns(proj_ref, g, h, heads) for g in range(3))
        s_ref[...] = mm_nt(q, k)
        for b in range(seq // SPAN):
            at = slice(b * SPAN, (b + 1) * SPAN)
            s = s_ref[at, :] * HEAD_DIM**-0.5 + bias_rows(tiles_ref, table_ref, kind_ref, h, b)
            e = jnp.exp(s - jnp.max(s, -1, keepdims=True))
            p_ref[at, :] = (e * (1.0 / jnp.sum(e, -1, keepdims=True))).astype(BF16)
        parts.append(mm(p_ref[...], v).astype(BF16))
    att_ref[...] = jnp.concatenate(parts, 1).reshape(att_ref.shape)
    scatter = RingScatter(part, rows, ids, bufs, s_rs, r_rs)
    part[far] = mm(att_ref[far], w_out[...]).astype(BF16)
    scatter.send_far()
    part[right] = mm(att_ref[right], w_out[...]).astype(BF16)
    scatter.send_right()
    part[left] = mm(att_ref[left], w_out[...]).astype(BF16)
    scatter.send_left()
    part[me] = mm(att_ref[me], w_out[...]).astype(BF16)
    scatter.send_sums()
    total = scatter.total()
    gather.wait_send()
    scatter.wait_send()
    return total


def attend_back(
    ids, dmiddle, all_ref, proj_ref, att_ref, w_qkv, w_out, table_ref, kind_ref,
    perm_ref, perm_out_ref, pq_ref, po_ref, dtable_ref, ready,
    tiles_ref, dtiles_ref, s_ref, dp_ref, p_ref, ds_ref, da_ref, dproj_ref, db_ref, part, scratch
):
    bufs, (s_ag, r_ag, s_rs, r_rs) = scratch[:6], scratch[6:]
    me, right, left = ids
    far = lax.rem(me + 2, 4)
    rows, width = dmiddle.shape
    seq = 4 * rows
    heads = w_out.shape[0] // HEAD_DIM
    scale = HEAD_DIM**-0.5
    db_ref[me] = dmiddle.astype(BF16)
    gather = RingGather(db_ref, rows, ids, s_ag, r_ag)
    gather.start()
    make_tiles(table_ref, tiles_ref, heads)
    gather.forward()
    gather.wait_left()
    gather.wait_right()
    gather.wait_far()
    da_ref[...] = mm_nt(db_ref[...].reshape(seq, width), w_out[...]).astype(BF16)
    dq, dk, dv = [], [], []
    for h in range(heads):
        q, k, v = (head_columns(proj_ref, g, h, heads) for g in range(3))
        da = head_columns(da_ref, 0, h, heads)
        s_ref[...] = mm_nt(q, k)
        dp_ref[...] = mm_nt(da, v)
        dtiles_ref[...] = jnp.zeros(dtiles_ref.shape, F32)
        for b in range(seq // SPAN):
            at = slice(b * SPAN, (b + 1) * SPAN)
            s = s_ref[at, :] * scale + bias_rows(tiles_ref, table_ref, kind_ref, h, b)
            e = jnp.exp(s - jnp.max(s, -1, keepdims=True))
            p = e * (1.0 / jnp.sum(e, -1, keepdims=True))
            dp = dp_ref[at, :]
            ds = p * (dp - jnp.sum(p * dp, -1, keepdims=True))
            p_ref[at, :] = p.astype(BF16)
            ds_ref[at, :] = ds.astype(BF16)
            kind = kind_ref[b : b + 1, :]
            for n in range(KINDS):
                dtiles_ref[n] += jnp.where(kind == n, ds, 0.0)
        for n in range(KINDS):
            folded = dtiles_ref[n, :, : 2 * SPAN]
            for m in range(1, seq // (2 * SPAN)):
                folded = folded + dtiles_ref[n, :, m * 2 * SPAN : (m + 1) * 2 * SPAN]
            dtiles_ref[n, :, : 2 * SPAN] = folded
        sums = [jnp.zeros((1, 2 * SPAN), F32)] * BUCKETS
        for n in range(KINDS - 1):
            bucket = tile_buckets(n)[1]
            folded = dtiles_ref[n, :, : 2 * SPAN]
            for b in tile_range(n):
                hit = jnp.where(bucket == b, folded, 0.0)
                sums[b] = sums[b] + jnp.sum(hit, 0, keepdims=True)
        rest = dtiles_ref[KINDS - 1, :, : 2 * SPAN]
        sums[-1] = sums[-1] + jnp.sum(rest, 0, keepdims=True)
        dtable_ref[h] = jnp.concatenate(sums, 0)
        p = p_ref[...]
        ds = ds_ref[...]
        dq.append((mm(ds, k) * scale).astype(BF16))
        dk.append((mm_tn(ds, q) * scale).astype(BF16))
        dv.append(mm_tn(p, da).astype(BF16))
    dproj_ref[...] = jnp.concatenate(dq + dk + dv, 1).reshape(dproj_ref.shape)
    scatter = RingScatter(part, rows, ids, bufs, s_rs, r_rs)
    part[far] = mm_nt(dproj_ref[far], w_qkv[...]).astype(BF16)
    scatter.send_far()
    part[right] = mm_nt(dproj_ref[right], w_qkv[...]).astype(BF16)
    scatter.send_right()
    part[left] = mm_nt(dproj_ref[left], w_qkv[...]).astype(BF16)
    scatter.send_left()
    part[me] = mm_nt(dproj_ref[me], w_qkv[...]).astype(BF16)
    dproj = dproj_ref[...].reshape(seq, dproj_ref.shape[2])
    d_qkv = mm_tn(all_ref[...].reshape(seq, width), dproj).astype(BF16)
    pq_ref[...] = mm(perm_ref[...], d_qkv).astype(BF16)
    ready(0)
    scatter.send_sums()
    d_out = mm_tn(att_ref[...].reshape(seq, att_ref.shape[2]), db_ref[...].reshape(seq, width))
    po_ref[...] = mm(perm_out_ref[...], d_out.astype(BF16)).astype(BF16)
    ready(1)
    total = scatter.total()
    gather.wait_send()
    scatter.wait_send()
    return total


def layer_kernel(
    layer, x_ref, gains, w_qkv_both, w_out_both, tables, kind_ref, routers, routes_ref,
    w_in_both, w_back_both,
    h_ref, all_ref, proj_ref, att_ref, middle_ref, mixed_ref, logits_ref, picked_ref,
    ent_out, pre_out, *scratch
):
    tiles_ref, s_ref, p_ref, part, w_in, w_back, ent_ref, pre_ref, sems, save_sems = scratch[:10]
    outs, rets = scratch[10:12], scratch[12:14]
    loads, saves = Loads(sems), Loads(save_sems)
    loads.start(w_in_both.at[layer], w_in)
    loads.start(w_back_both.at[layer], w_back)
    gain_one, gain_two = gains.at[2 * layer], gains.at[2 * layer + 1]
    w_qkv, w_out = w_qkv_both.at[layer], w_out_both.at[layer]
    table_ref, router_ref = tables.at[layer], routers.at[layer]
    ids = meet_all()
    rows, width = x_ref.shape
    x = x_ref[...].astype(F32)
    branch = attend(
        ids, x, gain_one, w_qkv, w_out, table_ref, kind_ref, all_ref, proj_ref, att_ref,
        tiles_ref, s_ref, p_ref, part, scratch[14:24]
    )
    middle = x + branch
    middle_ref[...] = middle
    mixed = norm(middle, gain_two[...])
    mixed_ref[...] = mixed
    hot, slots = route_tables(routes_ref, logits_ref.shape[1])
    set_slots(*outs, mm_tn(slots[0] + slots[1], mixed))

    def block(n, j, part):
        pre = mm(ent_ref[n, j], w_in[...])
        pre_ref[n, j] = pre
        hidden = gelu_parts(pre)[0].astype(BF16)
        part[n, j] = mm_nt(hidden, w_back[...]).astype(BF16)

    def find_logits():
        logits_ref[...] = mm(mixed_ref[...], router_ref[...])
        loads.wait_all()

    def save(n):
        saves.start(ent_ref.at[n], ent_out.at[n])
        saves.start(pre_ref.at[n], pre_out.at[n])

    nothing = lambda: None
    run_experts(
        ids, outs, ent_ref, rets, block, save,
        (find_logits, nothing, nothing, nothing), scratch[24:]
    )
    gates = gates_of(logits_ref[...], hot)
    returned = get_slots(*rets)
    y = middle_ref[...]
    for c in range(TOP):
        picked = mm(slots[c], returned)
        picked_ref[c] = picked.astype(BF16)
        y = y + gates[c] * picked
    h_ref[...] = y.astype(BF16)
    saves.wait_all()


def layer_forward(x, layer, weights, kind, routes, slots):
    gains, w_qkv, w_out, table, router, w_in, w_back = weights
    rows, width = x.shape
    seq, part, experts = 4 * rows, w_out.shape[1], router.shape[2]
    heads = part // HEAD_DIM
    vm, far = pl.BlockSpec(memory_space=pltpu.VMEM), pl.BlockSpec(memory_space=pl.ANY)
    shape = jax.ShapeDtypeStruct
    return pl.pallas_call(
        functools.partial(layer_kernel, layer),
        out_shape=(
            shape(x.shape, BF16),
            shape((4, rows, width), BF16),
            shape((seq, 3 * part), BF16),
            shape((4, rows, part), BF16),
            shape(x.shape, F32),
            shape(x.shape, BF16),
            shape((rows, experts), F32),
            shape((TOP, rows, width), BF16),
            shape((PARTS, 4, slots, width), BF16),
            shape((PARTS, 4, slots, w_in.shape[2]), F32),
        ),
        in_specs=[vm] * 8 + [far] * 2,
        out_specs=(vm,) * 8 + (far,) * 2,
        scratch_shapes=[
            pltpu.VMEM((heads, KINDS - 1, SPAN, seq), F32),
            pltpu.VMEM((seq, seq), F32),
            pltpu.VMEM((seq, seq), BF16),
            pltpu.VMEM((4, rows, width), BF16),
            pltpu.VMEM(w_in.shape[1:], BF16),
            pltpu.VMEM(w_back.shape[1:], BF16),
            pltpu.VMEM((PARTS, 4, slots, width), BF16),
            pltpu.VMEM((PARTS, 4, slots, w_in.shape[2]), F32),
            pltpu.SemaphoreType.DMA((2,)),
            pltpu.SemaphoreType.DMA((2 * PARTS,)),
            *slot_buffers(experts, width) * 2,
            *scatter_buffers(rows, width),
            *[pltpu.SemaphoreType.DMA((6,))] * 4,
            *expert_scratch(experts, slots, width),
        ],
        compiler_params=pltpu.CompilerParams(
            collective_id=layer, has_side_effects=True, vmem_limit_bytes=56 << 20
        ),
    )(x, gains, w_qkv, w_out, table, kind, router, routes, w_in, w_back)


def layer_back_kernel(
    layer, g_ref, x_ref, gains, w_qkv_both, w_out_both, tables, kind_ref, routers, routes_ref,
    middle_ref, mixed_ref, logits_ref, picked_ref,
    w_in_both, w_back_both, perm_in, perm_out_in, all_in, proj_in, att_in, ent_in, pre_in,
    dx_ref, dxb_ref, small_ref, pq_ref, po_ref,
    d_in_out, d_back_out, got_in, got_back, got_pq, got_po, *scratch
):
    (
        tiles_ref, dtiles_ref, s_ref, dp_ref, p_ref, ds_ref, da_ref, dproj_ref, db_ref, part,
        darr_ref, hid_ref, dpre_ref, e_in, e_back, drouter_ref, dtable_ref, s_x, r_x,
        d_in, d_back, w_in, w_back, perm_ref, perm_out_ref, all_ref, proj_ref, att_ref,
        ent_ref, pre_ref, sems, save_sems
    ) = scratch[:32]
    outs, rets = scratch[32:34], scratch[34:36]
    loads, saves = Loads(sems), Loads(save_sems)
    loads.start(w_back_both.at[layer], w_back)
    loads.start(w_in_both.at[layer], w_in)
    loads.start(pre_in, pre_ref)
    loads.start(ent_in, ent_ref)
    loads.start(all_in, all_ref)
    loads.start(proj_in, proj_ref)
    loads.start(att_in, att_ref)
    loads.start(perm_in, perm_ref)
    loads.start(perm_out_in, perm_out_ref)
    gain_one, gain_two = gains.at[2 * layer], gains.at[2 * layer + 1]
    w_qkv, w_out = w_qkv_both.at[layer], w_out_both.at[layer]
    table_ref, router_ref = tables.at[layer], routers.at[layer]
    partner = 1 - lax.axis_index("section")
    ids = meet_all(partner)
    rows, width = x_ref.shape

    def across(k, src, dst):
        return remote(src, dst, s_x, r_x, k, "section", partner)

    crossing = [
        across(0, e_back, got_back),
        across(1, e_in, got_in),
        across(2, pq_ref, got_pq),
        across(3, po_ref, got_po),
    ]
    g = g_ref[...].astype(F32)
    hot, slots = route_tables(routes_ref, logits_ref.shape[1])
    gates = gates_of(logits_ref[...], hot)
    dreturned = mm_tn(slots[0], (gates[0] * g).astype(BF16)) + mm_tn(
        slots[1], (gates[1] * g).astype(BF16)
    )
    set_slots(*outs, dreturned)

    def logits_back():
        g = g_ref[...].astype(F32)
        dgates = [
            jnp.sum(g * picked_ref[c].astype(F32), -1, keepdims=True) for c in range(TOP)
        ]
        mean = gates[0] * dgates[0] + gates[1] * dgates[1]
        dchosen = [a * (b - mean) for a, b in zip(gates, dgates)]
        dlogits = (hot[0] * dchosen[0] + hot[1] * dchosen[1]).astype(BF16)
        drouter_ref[...] = mm_tn(mixed_ref[...], dlogits)
        dx_ref[...] = mm_nt(dlogits, router_ref[...])
        loads.wait(0, 1, 2)

    def block(n, j, expert_part):
        hidden, slope = gelu_parts(pre_ref[n, j])
        hid_ref[n, j] = hidden.astype(BF16)
        dpre = (mm(darr_ref[n, j], w_back[...]) * slope).astype(BF16)
        dpre_ref[n, j] = dpre
        expert_part[n, j] = mm_nt(dpre, w_in[...]).astype(BF16)

    def flat(ref):
        return ref[...].reshape(math.prod(ref.shape[:3]), ref.shape[3])

    def back_grad():
        grad = mm_tn(flat(darr_ref), flat(hid_ref))
        d_back[...] = grad
        saves.start(d_back, d_back_out)
        e_back[...] = grad.astype(BF16)
        crossing[0].start()

    def in_grad():
        loads.wait(3)
        grad = mm_tn(flat(ent_ref), flat(dpre_ref))
        d_in[...] = grad
        saves.start(d_in, d_in_out)
        e_in[...] = grad.astype(BF16)
        crossing[1].start()

    run_experts(
        ids, outs, darr_ref, rets, block, lambda n: None,
        (logits_back, back_grad, lambda: None, in_grad), scratch[46:]
    )
    dleft = get_slots(*rets)
    loads.wait(*range(4, 9))
    dmixed = mm(slots[0] + slots[1], dleft) + dx_ref[...]
    dnorm, dgain = norm_back(middle_ref[...], gain_two[...], dmixed)
    small_ref[...] = pack_gain(dgain, 1, small_ref.shape) + pack_router(
        drouter_ref[...], small_ref.shape
    )
    dmiddle = g_ref[...].astype(F32) + dnorm
    dx_ref[...] = dmiddle
    dnormed = attend_back(
        ids, dmiddle, all_ref, proj_ref, att_ref, w_qkv, w_out, table_ref, kind_ref,
        perm_ref, perm_out_ref, pq_ref, po_ref, dtable_ref, lambda k: crossing[2 + k].start(),
        tiles_ref, dtiles_ref, s_ref, dp_ref, p_ref, ds_ref, da_ref, dproj_ref, db_ref, part,
        scratch[36:46]
    )
    dnorm, dgain = norm_back(x_ref[...].astype(F32), gain_one[...], dnormed)
    small_ref[...] += pack_gain(dgain, 0, small_ref.shape) + pack_table(
        dtable_ref, small_ref.shape
    )
    dx = dx_ref[...] + dnorm
    dx_ref[...] = dx
    dxb_ref[...] = dx.astype(BF16)
    saves.wait_all()
    for c in crossing:
        c.wait()


def layer_backward(g, keep, layer, weights, kind, routes, slots, perm, perm_out):
    x, normed, proj, attended, middle, mixed, logits, picked, entering, pre = keep
    gains, w_qkv, w_out, table, router, w_in, w_back = weights
    rows, width = x.shape
    seq, part, experts = 4 * rows, w_out.shape[1], router.shape[2]
    heads, hid = part // HEAD_DIM, w_in.shape[2]
    w_shape = w_in.shape[1:]
    vm, far = pl.BlockSpec(memory_space=pltpu.VMEM), pl.BlockSpec(memory_space=pl.ANY)
    shape = jax.ShapeDtypeStruct
    pq = shape((perm.shape[0], 3 * part), BF16)
    po = shape((perm_out.shape[0], width), BF16)
    loaded = (normed, proj, attended, entering, pre)
    return pl.pallas_call(
        functools.partial(layer_back_kernel, layer),
        out_shape=(
            shape(x.shape, F32),
            shape(x.shape, BF16),
            shape((perm.shape[0] // 16, SMALL), F32),
            pq,
            po,
            shape(w_shape, F32),
            shape(w_shape, F32),
            shape(w_shape, BF16),
            shape(w_shape, BF16),
            pq,
            po,
        ),
        in_specs=[vm] * 13 + [far] * 9,
        out_specs=(vm,) * 5 + (far,) * 6,
        scratch_shapes=[
            pltpu.VMEM((heads, KINDS - 1, SPAN, seq), F32),
            pltpu.VMEM((KINDS, SPAN, seq), F32),
            pltpu.VMEM((seq, seq), F32),
            pltpu.VMEM((seq, seq), F32),
            pltpu.VMEM((seq, seq), BF16),
            pltpu.VMEM((seq, seq), BF16),
            pltpu.VMEM((seq, part), BF16),
            pltpu.VMEM((4, rows, 3 * part), BF16),
            pltpu.VMEM((4, rows, width), BF16),
            pltpu.VMEM((4, rows, width), BF16),
            pltpu.VMEM((PARTS, 4, slots, width), BF16),
            pltpu.VMEM((PARTS, 4, slots, hid), BF16),
            pltpu.VMEM((PARTS, 4, slots, hid), BF16),
            pltpu.VMEM(w_shape, BF16),
            pltpu.VMEM(w_shape, BF16),
            pltpu.VMEM((width, experts), F32),
            pltpu.VMEM((heads, BUCKETS, 2 * SPAN), F32),
            *[pltpu.SemaphoreType.DMA((4,))] * 2,
            *[pltpu.VMEM(w_shape, F32)] * 2,
            *[pltpu.VMEM(w_shape, BF16)] * 2,
            *[pltpu.VMEM(a.shape, a.dtype) for a in (perm, perm_out, *loaded)],
            pltpu.SemaphoreType.DMA((9,)),
            pltpu.SemaphoreType.DMA((2,)),
            *slot_buffers(experts, width) * 2,
            *scatter_buffers(rows, width),
            *[pltpu.SemaphoreType.DMA((6,))] * 4,
            *expert_scratch(experts, slots, width),
        ],
        compiler_params=pltpu.CompilerParams(
            collective_id=2 + layer, has_side_effects=True, vmem_limit_bytes=60 << 20
        ),
    )(
        g, x, gains, w_qkv, w_out, table, kind, router, routes, middle, mixed, logits, picked,
        w_in, w_back, perm, perm_out, *loaded
    )


SMALL = 256
OWN = 12
AT_TABLE = 2 * OWN


def grid_of(shape):
    return tuple(lax.broadcasted_iota(jnp.int32, shape, d) for d in (0, 1))


def one_hot(where):
    return jnp.where(where, 1.0, 0.0).astype(BF16)


def owner_rows(owners, width):
    row, col = grid_of((owners, width))
    return one_hot((col >= OWN * row) & (col < OWN * row + OWN))


def table_rows(owners):
    row, col = grid_of((BUCKETS, owners))
    return one_hot(col == 2 * row + lax.axis_index("ctx") // 2)


def table_column(head):
    return AT_TABLE + HEADS // 4 * lax.rem(lax.axis_index("ctx"), 2) + head


def at_router(experts):
    return AT_TABLE + BUCKETS * HEADS // 64


def router_mask(width, experts):
    row, col = grid_of((width, SMALL))
    first = at_router(experts) + experts * lax.rem(row, OWN)
    return (col >= first) & (col < first + experts)


def unpack_small(small, width, experts, heads):
    owners = small.shape[0]
    small = small.astype(BF16)
    own = owner_rows(owners, width)
    spread = mm_tn(small[:, :128], own)
    row, col = grid_of(spread.shape)
    gains = [
        jnp.sum(jnp.where(row == lax.rem(col, OWN) + n * OWN, spread, 0.0), 0, keepdims=True)
        for n in range(2)
    ]
    wide = mm_tn(own, small)
    wide = jnp.where(router_mask(width, experts), wide, 0.0).astype(BF16)
    row, col = grid_of((SMALL, experts))
    first = at_router(experts)
    inside = (row >= first) & (row < first + OWN * experts)
    router = mm(wide, one_hot(inside & (lax.rem(row + experts - first % experts, experts) == col)))
    table = mm(table_rows(owners), small[:, :128]).astype(BF16)
    row, col = grid_of((128, heads))
    table = mm(table, one_hot(row == table_column(col)))
    return gains, router.astype(BF16), table


def pack_gain(dgain, n, shape):
    width = dgain.shape[1]
    row, col = grid_of((width, shape[1]))
    own = owner_rows(shape[0], width).astype(F32) * dgain
    return mm(own.astype(BF16), one_hot(col == lax.rem(row, OWN) + n * OWN))


def pack_router(drouter, shape):
    width, experts = drouter.shape
    row, col = grid_of((experts, shape[1]))
    first = at_router(experts)
    wide = mm(
        drouter.astype(BF16), one_hot(lax.rem(col + experts - first % experts, experts) == row)
    )
    wide = jnp.where(router_mask(width, experts), wide, 0.0).astype(BF16)
    return mm(owner_rows(shape[0], width), wide)


def pack_table(dtable_ref, shape):
    total = jnp.zeros((BUCKETS, shape[1]), F32)
    col = grid_of(total.shape)[1]
    for h in range(dtable_ref.shape[0]):
        column = jnp.sum(dtable_ref[h], -1, keepdims=True)
        total = total + jnp.where(col == table_column(h), column, 0.0)
    return mm_tn(table_rows(shape[0]), total.astype(BF16))


def meet_everyone():
    barrier = pltpu.get_barrier_semaphore()
    peers = [("exp", 16), ("ctx", 4), ("section", 2)]
    for axis, count in peers:
        me = lax.axis_index(axis)

        def greet(k, carry, axis=axis, me=me, count=count):
            peer = lax.rem(me + k, count)
            pl.semaphore_signal(barrier, inc=1, device_id={axis: peer}, device_id_type=MESH)
            return carry

        lax.fori_loop(1, count, greet, 0)
    pl.semaphore_wait(barrier, sum(count - 1 for _, count in peers))


def ctx_exchange(src, dst, send, recv):
    me = lax.axis_index("ctx")
    copies = []
    for k in (1, 3, 2):
        peer = lax.rem(me + k, 4)
        copies.append(remote(src.at[peer], dst.at[me], send, recv, k, "ctx", peer))
    return copies


def weights_kernel(
    cols_ref, outp_ref, w_in, w_back, perm_ref, perm_out_ref, pick_ref,
    w_qkv, w_out, gains, routers, tables, both_in, both_back,
    zin, grid, grid_out, s_z, r_z, s_q, r_q, s_o, r_o, s_fq, r_fq, s_fo, r_fo, s_x, r_x, s_own
):
    meet_everyone()
    section, ctx, exp = (lax.axis_index(a) for a in ("section", "ctx", "exp"))
    partner = 1 - section
    count = grid.shape[1]
    turn = ctx_exchange(cols_ref, zin, s_z, r_z)
    for c in turn:
        c.start()
    cross_in = remote(w_in, both_in.at[section], s_x, r_x, 0, "section", partner)
    cross_back = remote(w_back, both_back.at[section], s_x, r_x, 1, "section", partner)
    cross_in.start()
    cross_back.start()
    zin[ctx] = cols_ref[ctx]
    grid_out[section, exp] = outp_ref[...]

    def spread(ref, send, recv, k):
        peer = lax.rem(exp + k, count)
        at = ref.at[section, exp]
        return remote(at, at, send, recv, k, "exp", peer)

    def forward(ref, send, recv, k):
        at = ref.at[section, lax.rem(exp + count - k, count)]
        return remote(at, at, send, recv, k, "section", partner)

    def each(act, first=1):
        def body(k, carry):
            act(k)
            return carry

        lax.fori_loop(first, count, body, 0)

    each(lambda k: spread(grid_out, s_o, r_o, k).start())
    for c in turn:
        c.wait_recv()
    grid[section, exp] = zin[...].reshape(grid.shape[2:])
    each(lambda k: spread(grid, s_q, r_q, k).start())
    forward(grid, s_fq, r_fq, 0).start()
    forward(grid_out, s_fo, r_fo, 0).start()
    own_in = pltpu.make_async_copy(w_in, both_in.at[section], s_own.at[0])
    own_back = pltpu.make_async_copy(w_back, both_back.at[section], s_own.at[1])
    own_in.start()
    own_back.start()

    def relay(ref, s, r, sf, rf, k):
        spread(ref, s, r, k).wait_recv()
        forward(ref, sf, rf, k).start()

    each(lambda k: relay(grid_out, s_o, r_o, s_fo, r_fo, k))
    each(lambda k: relay(grid, s_q, r_q, s_fq, r_fq, k))

    def unpack(layer):
        flat = grid[layer].reshape(perm_ref.shape[0], grid.shape[3])
        w_qkv[layer] = mm_tn(perm_ref[...], flat).astype(BF16)
        small = mm(pick_ref[...], flat[:, :SMALL])
        two, routers[layer], tables[layer] = unpack_small(
            small, routers.shape[1], routers.shape[2], tables.shape[2]
        )
        gains[2 * layer], gains[2 * layer + 1] = two
        flat = grid_out[layer].reshape(perm_out_ref.shape[0], grid_out.shape[3])
        w_out[layer] = mm_tn(perm_out_ref[...], flat).astype(BF16)

    unpack(section)
    each(lambda k: forward(grid_out, s_fo, r_fo, k).wait_recv(), 0)
    each(lambda k: forward(grid, s_fq, r_fq, k).wait_recv(), 0)
    unpack(partner)
    each(lambda k: spread(grid_out, s_o, r_o, k).wait_send())
    each(lambda k: spread(grid, s_q, r_q, k).wait_send())
    each(lambda k: forward(grid_out, s_fo, r_fo, k).wait_send(), 0)
    each(lambda k: forward(grid, s_fq, r_fq, k).wait_send(), 0)
    for c in turn:
        c.wait_send()
    own_in.wait()
    own_back.wait()
    cross_in.wait()
    cross_back.wait()


def gather_weights(cols, outp, w_in, w_back, perm, perm_out, pick):
    width, part = outp.shape[1], cols.shape[2]
    count = perm_out.shape[0] // 16
    vm, far = pl.BlockSpec(memory_space=pltpu.VMEM), pl.BlockSpec(memory_space=pl.ANY)
    dma = lambda n: pltpu.SemaphoreType.DMA((n,))
    return pl.pallas_call(
        weights_kernel,
        out_shape=(
            jax.ShapeDtypeStruct((2, width, part), BF16),
            jax.ShapeDtypeStruct((2, perm_out.shape[1], width), BF16),
            jax.ShapeDtypeStruct((4, 1, width), F32),
            jax.ShapeDtypeStruct((2, width, count), BF16),
            jax.ShapeDtypeStruct((2, BUCKETS, part // (3 * HEAD_DIM)), F32),
            jax.ShapeDtypeStruct((2, *w_in.shape), BF16),
            jax.ShapeDtypeStruct((2, *w_back.shape), BF16),
        ),
        in_specs=[vm] * 2 + [far] * 2 + [vm] * 3,
        out_specs=(vm,) * 5 + (far,) * 2,
        scratch_shapes=[
            pltpu.VMEM(cols.shape, BF16),
            pltpu.VMEM((2, count, 64, part), BF16),
            pltpu.VMEM((2, count, 16, width), BF16),
            dma(4), dma(4), *[dma(count)] * 8, dma(2), dma(2), dma(2),
        ],
        compiler_params=pltpu.CompilerParams(
            collective_id=4, has_side_effects=True, vmem_limit_bytes=48 << 20
        ),
    )(cols, outp, w_in, w_back, perm, perm_out, pick)


def owners_kernel(
    small0, small1, spread_ref, y0, y1, dx0, dx1,
    pq0, pq1, gq0, gq1, po0, po1, go0, go1, in0, in1, gin0, gin1, back0, back1, gback0, gback1,
    turned, out_grad, d_in_out, d_back_out, layer_out, input_grad,
    pq, gq, po, go, d_in, gin, d_back, gback,
    sent_small, got_small, sent_y, sent_dx, pieces, box, pieces_out, box_out, summed,
    s_s, r_s, s_q, r_q, s_o, r_o, s_z, r_z, sems, save_sems
):
    section, ctx, exp = (lax.axis_index(a) for a in ("section", "ctx", "exp"))
    partner = 1 - section
    first = section == 0
    of_first = (po0, go0, pq0, gq0, in0, gin0, back0, gback0)
    of_second = (po1, go1, pq1, gq1, in1, gin1, back1, gback1)
    held = (po, go, pq, gq, d_in, gin, d_back, gback)

    def load(sources):
        for k, (src, dst) in enumerate(zip(sources, held)):
            pltpu.make_async_copy(src, dst, sems.at[k]).start()

    @pl.when(first)
    def _():
        load(of_first)

    @pl.when(jnp.logical_not(first))
    def _():
        load(of_second)

    def loaded(*which):
        for k in which:
            pltpu.make_async_copy(of_first[k], held[k], sems.at[k]).wait()

    meet_everyone()
    sent_small[...] = jnp.where(first, small1[...], small0[...])
    cross = [
        remote(sent_small, got_small, s_s, r_s, 0, "section", partner),
        remote(sent_y, layer_out.at[section], s_s, r_s, 1, "section", partner),
        remote(sent_dx, input_grad.at[section], s_s, r_s, 2, "section", partner),
    ]
    cross[0].start()

    def both(a, b):
        return a[...].astype(F32) + b[...].astype(F32)

    loaded(2, 3)
    dense = both(pq, gq)
    cross[0].wait_recv()
    small = jnp.where(first, small0[...], small1[...]) + got_small[...]
    wide = mm(spread_ref[...], small.astype(BF16))
    n = wide.shape[1]
    dense = jnp.concatenate([dense[:, :n] + wide, dense[:, n:]], 1)
    pieces[...] = dense.astype(BF16).reshape(pieces.shape)
    swap = exchange_out(pieces, box, s_q, r_q)
    swap.start()
    loaded(0, 1)
    pieces_out[...] = both(po, go).astype(BF16).reshape(pieces_out.shape)
    swap_out = exchange_out(pieces_out, box_out, s_o, r_o)
    swap_out.start()
    box[0] = pieces[exp]
    box_out[0] = pieces_out[exp]
    sent_y[...] = jnp.where(first, y1[...], y0[...])
    cross[1].start()
    sent_dx[...] = jnp.where(first, dx1[...], dx0[...])
    cross[2].start()
    layer_out[section] = jnp.where(first, y0[...], y1[...])
    input_grad[section] = jnp.where(first, dx0[...], dx1[...])
    saves = Loads(save_sems)
    loaded(4, 5)
    d_in[...] += gin[...].astype(F32)
    saves.start(d_in, d_in_out)
    loaded(6, 7)
    d_back[...] += gback[...].astype(F32)
    saves.start(d_back, d_back_out)
    swap.wait_recv()
    total = box[0].astype(F32)
    for k in range(1, box.shape[0]):
        total = total + box[k].astype(F32)
    summed[...] = total.reshape(summed.shape)
    turn = ctx_exchange(summed, turned, s_z, r_z)
    for c in turn:
        c.start()
    turned[ctx] = summed[ctx]
    swap_out.wait_recv()
    total = box_out[0].astype(F32)
    for k in range(1, box_out.shape[0]):
        total = total + box_out[k].astype(F32)
    out_grad[...] = total
    for c in turn:
        c.wait()
    cross[0].wait_send()
    cross[1].wait()
    cross[2].wait()
    swap.wait_send()
    swap_out.wait_send()
    saves.wait_all()


def sum_at_owners(pq, gq, po, go, small, spread, d_in, g_in, d_back, g_back, y, dx, count):
    rows, part = pq[0].shape
    out_rows, width = po[0].shape
    vm, far = pl.BlockSpec(memory_space=pltpu.VMEM), pl.BlockSpec(memory_space=pl.ANY)
    dma = lambda n: pltpu.SemaphoreType.DMA((n,))
    own = (rows // count, part)
    own_out = (out_rows // count, width)
    quarter = (4, rows // count // 4, part)
    held = [a[0] for a in (pq, gq, po, go, d_in, g_in, d_back, g_back)]
    return pl.pallas_call(
        owners_kernel,
        out_shape=(
            jax.ShapeDtypeStruct(quarter, F32),
            jax.ShapeDtypeStruct(own_out, F32),
            jax.ShapeDtypeStruct(d_in[0].shape, F32),
            jax.ShapeDtypeStruct(d_back[0].shape, F32),
            jax.ShapeDtypeStruct((2, *y[0].shape), BF16),
            jax.ShapeDtypeStruct((2, *dx[0].shape), F32),
        ),
        in_specs=[vm] * 7 + [far] * 16,
        out_specs=(vm, vm, far, far, vm, vm),
        scratch_shapes=[
            *[pltpu.VMEM(a.shape, a.dtype) for a in held],
            pltpu.VMEM(small[0].shape, F32),
            pltpu.VMEM(small[0].shape, F32),
            pltpu.VMEM(y[0].shape, BF16),
            pltpu.VMEM(dx[0].shape, F32),
            pltpu.VMEM((count, *own), BF16),
            pltpu.VMEM((count, *own), BF16),
            pltpu.VMEM((count, *own_out), BF16),
            pltpu.VMEM((count, *own_out), BF16),
            pltpu.VMEM(quarter, F32),
            dma(3), dma(3), *[dma(count)] * 4, dma(4), dma(4), dma(8), dma(2),
        ],
        compiler_params=pltpu.CompilerParams(
            collective_id=5, has_side_effects=True, vmem_limit_bytes=52 << 20
        ),
    )(*small, spread, *y, *dx, *pq, *gq, *po, *go, *d_in, *g_in, *d_back, *g_back)


def packing(n_ctx, n_exp, own_rows):
    blocks = n_ctx * n_exp
    perm = np.zeros((blocks, 16, blocks, own_rows), np.float32)
    pick = np.zeros((blocks, blocks, 16), np.float32)
    perm_out = np.zeros((n_exp, 16, n_exp, own_rows), np.float32)
    for e in range(n_exp):
        for i in range(own_rows):
            perm_out[e, i, e, i] = 1
        for c in range(n_ctx):
            for i in range(own_rows):
                perm[e * n_ctx + c, i, c * n_exp + e, i] = 1
            pick[c * n_exp + e, e * n_ctx + c, own_rows] = 1
    perm = perm.reshape(blocks * 16, blocks * own_rows)
    pick = pick.reshape(blocks, blocks * 16)
    perm_out = perm_out.reshape(n_exp * 16, n_exp * own_rows)
    return tuple(jnp.asarray(m, BF16) for m in (perm, pick, pick.T.copy(), perm_out))


def norm_scale(v):
    return lax.rsqrt(jnp.mean(v * v, -1, keepdims=True) + EPS)


def norm(v, gain):
    return (v * norm_scale(v) * gain).astype(BF16)


def norm_back(v, gain, du):
    r = norm_scale(v)
    dug = du * gain
    dv = r * dug - v * (r * r * r) * jnp.mean(dug * v, -1, keepdims=True)
    return dv, jnp.sum(du * v * r, 0, keepdims=True)


def gelu_parts(v):
    t = jnp.tanh(GELU_C * (v + 0.044715 * v * v * v))
    value = 0.5 * v * (1.0 + t)
    slope = 0.5 * (1.0 + t) + 0.5 * v * (1.0 - t * t) * GELU_C * (1.0 + 3 * 0.044715 * v * v)
    return value, slope


def on_device(
    inputs,
    cotangent,
    routes,
    block_order,
    attn_gain,
    qkv_weight,
    out_weight,
    rel_bias,
    moe_gain,
    router_weight,
    expert_in,
    expert_out,
):
    rows, width = inputs.shape[2:]
    n_ctx, n_exp = lax.axis_size("ctx"), lax.axis_size("exp")
    seq = rows * n_ctx
    own_rows = qkv_weight.shape[1]
    heads = HEADS // n_ctx
    part = heads * HEAD_DIM
    capacity = rows * TOP // n_exp + max(1, rows * TOP // (16 * n_exp))
    slots = part_rows(n_exp, capacity)
    section = lax.axis_index("section")
    ctx = lax.axis_index("ctx")
    first = section == 0

    perm, pick, place, perm_out = packing(n_ctx, n_exp, own_rows)
    small = jnp.concatenate(
        [attn_gain[0], moe_gain[0], rel_bias[0], router_weight[0].reshape(-1)]
    )
    n_small = small.shape[0]
    columns = qkv_weight[0].reshape(own_rows, 3, n_ctx, part).transpose(2, 0, 1, 3)
    columns = columns.reshape(n_ctx, own_rows, 3 * part)
    small_row = jnp.pad(small, (0, 3 * part - n_small))
    small_rows = jnp.broadcast_to(small_row, (n_ctx, 1, 3 * part))
    columns = jnp.concatenate([columns, small_rows], 1)
    columns = jnp.pad(columns, ((0, 0), (0, 15 - own_rows), (0, 0)))
    out_rows = jnp.pad(out_weight[0], ((0, 16 - own_rows), (0, 0)))
    w_qkv, w_out, gains, routers, tables, w_in, w_back = gather_weights(
        columns, out_rows, expert_in[0, 0], expert_out[0, 0], perm, perm_out, pick
    )
    weights = (gains, w_qkv, w_out, tables, routers, w_in, w_back)
    n_bias = BUCKETS * HEADS // (n_ctx * n_exp)
    ahead = block_order[:, None] - block_order[None, :]
    kind = jnp.repeat(jnp.where(ahead < 0, -1, jnp.minimum(ahead, 3)), SPAN, 1)

    own_routes = routes[0, :, 0]
    kept = jnp.where(first, own_routes[0], own_routes[1])
    given = jnp.where(first, own_routes[1], own_routes[0])
    taken = lax.ppermute(given, "section", [(0, 1), (1, 0)])
    layer_routes = (jnp.where(first, kept, taken), jnp.where(first, taken, kept))
    def forward(x, layer):
        h, *saved = layer_forward(x, layer, weights, kind, layer_routes[layer], slots)
        return h, (x, *saved)

    def backward(g, keep, layer):
        dx, dxb, d_small, pq, po, d_in, d_back, g_in, g_back, gq, go = layer_backward(
            g, keep, layer, weights, kind, layer_routes[layer], slots, perm, perm_out
        )
        return dx, dxb, (pq, gq, po, go, d_small, d_in, g_in, d_back, g_back)

    x = jnp.where(first, inputs[0, 0], inputs[1, 0])
    cot = jnp.where(first, cotangent[0, 0], cotangent[1, 0])
    h, keep0 = forward(x, 0)
    top, keep1 = forward(h, 1)
    _, dh, grads1 = backward(cot, keep1, 1)
    dx, _, grads0 = backward(dh, keep0, 0)
    pq, gq, po, go, d_small, d_in, g_in, d_back, g_back = zip(grads0, grads1)
    pieces, out_grad, d_in, d_back, layer_out, input_grad = sum_at_owners(
        pq, gq, po, go, d_small, place, d_in, g_in, d_back, g_back,
        (h, top), (dx, dh.astype(F32)), n_exp
    )
    qkv_grad = pieces[:, :own_rows].reshape(n_ctx, own_rows, 3, part)
    qkv_grad = qkv_grad.transpose(1, 2, 0, 3).reshape(own_rows, 3 * width)
    out_grad = out_grad[:own_rows]
    small = jnp.sum(pieces[:, own_rows, :n_small], 0)

    layer_out = layer_out.reshape(1, 2, 1, rows, width)
    input_grad = input_grad.reshape(1, 2, 1, rows, width)
    return (
        layer_out,
        input_grad,
        small[:own_rows][None],
        qkv_grad[None],
        out_grad[None],
        small[2 * own_rows : 2 * own_rows + n_bias][None],
        small[own_rows : 2 * own_rows][None],
        small[2 * own_rows + n_bias :].reshape(1, own_rows, n_exp),
        d_in[None, None],
        d_back[None, None],
    )


def solution(mesh):
    return jax.shard_map(
        on_device,
        mesh=mesh,
        in_specs=(
            P(None, "exp", "ctx", None),
            P(None, "exp", "ctx", None),
            P("section", None, "exp", "ctx", None),
            P(),
            P("section", ("ctx", "exp")),
            P("section", ("ctx", "exp"), None),
            P("section", ("ctx", "exp"), None),
            P("section", ("ctx", "exp")),
            P("section", ("ctx", "exp")),
            P("section", ("ctx", "exp"), None),
            P("section", "exp", None, "ctx"),
            P("section", "exp", None, "ctx"),
        ),
        out_specs=(
            P("section", None, "exp", "ctx", None),
            P("section", None, "exp", "ctx", None),
            P("section", ("ctx", "exp")),
            P("section", ("ctx", "exp"), None),
            P("section", ("ctx", "exp"), None),
            P("section", ("ctx", "exp")),
            P("section", ("ctx", "exp")),
            P("section", ("ctx", "exp"), None),
            P("section", "exp", None, "ctx"),
            P("section", "exp", None, "ctx"),
        ),
        check_vma=False,
    )
```

```python
import functools
import math

import jax
import jax.numpy as jnp
import numpy as np
from jax import lax
from jax.experimental import pallas as pl
from jax.experimental.pallas import tpu as pltpu
from jax.sharding import PartitionSpec as P

HEADS = 12
HEAD_DIM = 64
BUCKETS = 32
REACH = 128
TOP = 2
EPS = 1e-06
NEG = -1e30
SPAN = 64
KINDS = 4
MESH = pl.DeviceIdType.MESH
BF16 = jnp.bfloat16
F32 = jnp.float32
GELU_C = math.sqrt(2.0 / math.pi)


def dot(a, b, dims):
    return lax.dot_general(a, b, (dims, ((), ())), preferred_element_type=F32)


def mm(a, b):
    return dot(a, b, ((1,), (0,)))


def mm_nt(a, b):
    return dot(a, b, ((1,), (1,)))


def mm_tn(a, b):
    return dot(a, b, ((0,), (0,)))


def meet_neighbours(axis, count):
    me = lax.axis_index(axis)
    right, left = lax.rem(me + 1, count), lax.rem(me + count - 1, count)
    barrier = pltpu.get_barrier_semaphore()
    for neighbour in (left, right):
        pl.semaphore_signal(barrier, inc=1, device_id={axis: neighbour}, device_id_type=MESH)
    pl.semaphore_wait(barrier, 2)
    return me, right, left


def remote(src, dst, send, recv, k, axis, to):
    return pltpu.make_async_remote_copy(
        src_ref=src,
        dst_ref=dst,
        send_sem=send.at[k],
        recv_sem=recv.at[k],
        device_id={axis: to},
        device_id_type=MESH,
    )


def halves(rows):
    first = (rows // 2 + 15) // 16 * 16
    return (pl.ds(0, first), pl.ds(first, rows - first))


def ring_copy(send, recv, k, src, dst, to):
    return remote(src, dst, send, recv, k, "ctx", to)


class RingGather:
    def __init__(self, all_ref, rows, ids, send, recv):
        me, right, left = ids
        low, high = halves(rows)

        def pass_on(k, slot, half, to):
            at = all_ref.at[slot, half]
            return ring_copy(send, recv, k, at, at, to)

        self.first = (
            pass_on(0, me, low, right),
            pass_on(1, me, high, left),
            pass_on(2, me, high, right),
            pass_on(3, me, low, left),
        )
        self.second = (pass_on(4, left, low, right), pass_on(5, right, high, left))

    def start(self):
        for c in self.first:
            c.start()

    def forward(self):
        self.first[0].wait_recv()
        self.second[0].start()
        self.first[1].wait_recv()
        self.second[1].start()

    def wait_left(self):
        self.first[2].wait_recv()

    def wait_right(self):
        self.first[3].wait_recv()

    def wait_far(self):
        for c in self.second:
            c.wait_recv()

    def wait_send(self):
        for c in self.first + self.second:
            c.wait_send()


class RingScatter:
    def __init__(self, part, rows, ids, bufs, send, recv):
        me, right, left = ids
        far = lax.rem(me + 2, 4)
        low, high = halves(rows)
        far_l, far_r, sum_l, sum_r, in_l, in_r = bufs
        self.part, self.ids, self.n_low, self.bufs = part, ids, low.size, bufs
        copy = functools.partial(ring_copy, send, recv)
        self.far = (
            copy(0, part.at[far, low], far_l, right),
            copy(1, part.at[far, high], far_r, left),
        )
        self.right = copy(2, part.at[right, high], in_l.at[high], right)
        self.left = copy(3, part.at[left, low], in_r.at[low], left)
        self.sums = (
            copy(4, sum_r, in_l.at[low], right),
            copy(5, sum_l, in_r.at[high], left),
        )

    def send_far(self):
        for c in self.far:
            c.start()

    def send_left(self):
        self.left.start()

    def send_right(self):
        self.right.start()

    def send_sums(self):
        me, right, left = self.ids
        far_l, far_r, sum_l, sum_r, in_l, in_r = self.bufs
        n = self.n_low
        self.far[0].wait_recv()
        sum_r[...] = (self.part[right, :n, :].astype(F32) + far_l[...].astype(F32)).astype(BF16)
        self.sums[0].start()
        self.far[1].wait_recv()
        sum_l[...] = (self.part[left, n:, :].astype(F32) + far_r[...].astype(F32)).astype(BF16)
        self.sums[1].start()

    def total(self):
        for c in (self.right, self.left, *self.sums):
            c.wait_recv()
        in_l, in_r = self.bufs[4:]
        return self.part[self.ids[0]].astype(F32) + in_l[...].astype(F32) + in_r[...].astype(F32)

    def wait_send(self):
        for c in (*self.far, self.right, self.left, *self.sums):
            c.wait_send()


def scatter_buffers(rows, width):
    low, high = halves(rows)
    sizes = (low.size, high.size, high.size, low.size, rows, rows)
    return [pltpu.VMEM((n, width), BF16) for n in sizes]


TILE = 16
PARTS = 2


class Loads:
    def __init__(self, sems):
        self.sems, self.copies = sems, []

    def start(self, src, dst):
        copy = pltpu.make_async_copy(src, dst, self.sems.at[len(self.copies)])
        copy.start()
        self.copies.append(copy)

    def wait(self, *which):
        for k in which:
            self.copies[k].wait()

    def wait_all(self):
        self.wait(*range(len(self.copies)))


def set_slots(main, extra, values):
    count = extra.shape[0]
    main[...] = values[: count * TILE].astype(BF16).reshape(main.shape)
    for e in range(count):
        extra[e] = values[count * TILE + e : count * TILE + e + 1]


def get_slots(main, extra):
    count = extra.shape[0]
    rows = [extra[e] for e in range(count)]
    first = main[...].reshape(count * TILE, main.shape[2])
    return jnp.concatenate([first, jnp.concatenate(rows, 0).astype(BF16)], 0)


class Exchange:
    def __init__(self, copy, send, recv):
        self.copy, self.send, self.recv = copy, send, recv
        self.me, self.count = lax.axis_index("exp"), lax.axis_size("exp")

    def each(self, act, first=1, last=None):
        def body(k, carry):
            act(self.copy(self, k))
            return carry

        lax.fori_loop(first, self.count if last is None else last, body, 0)

    def start(self, *span):
        self.each(lambda c: c.start(), *span)

    def wait_recv(self, *span):
        self.each(lambda c: c.wait_recv(), *span)

    def wait_send(self):
        self.each(lambda c: c.wait_send())

    def to(self, src, dst, k, peer):
        return remote(src, dst, self.send, self.recv, k, "exp", peer)


def exchange_out(src, dst, send, recv):
    def copy(x, k):
        peer = lax.rem(x.me + k, x.count)
        return x.to(src.at[peer], dst.at[k], k, peer)

    return Exchange(copy, send, recv)


def exchange_home(src, dst, send, recv):
    def copy(x, k):
        peer = lax.rem(x.me + x.count - k, x.count)
        return x.to(src.at[k], dst.at[x.me], k, peer)

    return Exchange(copy, send, recv)


def meet_all(partner=None):
    barrier = pltpu.get_barrier_semaphore()
    me, count = lax.axis_index("exp"), lax.axis_size("exp")

    def greet(k, carry):
        peer = lax.rem(me + k, count)
        pl.semaphore_signal(barrier, inc=1, device_id={"exp": peer}, device_id_type=MESH)
        return carry

    lax.fori_loop(1, count, greet, 0)
    ctx = lax.axis_index("ctx")
    right, left = lax.rem(ctx + 1, 4), lax.rem(ctx + 3, 4)
    for neighbour in (left, right):
        pl.semaphore_signal(barrier, inc=1, device_id={"ctx": neighbour}, device_id_type=MESH)
    if partner is not None:
        pl.semaphore_signal(barrier, inc=1, device_id={"section": partner}, device_id_type=MESH)
    greeted = count + (1 if partner is None else 2)
    return (ctx, right, left), lambda: pl.semaphore_wait(barrier, greeted)


def run_experts(ids, outs, all_ref, rets, block, done, beside, scratch):
    part = scratch[0]
    inbox, res = scratch[1:3], scratch[3:5]
    s_in, r_in, s_out, r_out = scratch[5:7], scratch[7:9], scratch[9:11], scratch[11:13]
    rest = scratch[13:]
    me, right, left = ids
    far = lax.rem(me + 2, 4)
    parts, _, rows, width = all_ref.shape
    near = inbox[0].shape[0] // parts
    filled = near * TILE
    exp = lax.axis_index("exp")
    arriving = [exchange_out(outs[m], inbox[m], s_in[m], r_in[m]) for m in range(2)]
    leaving = [exchange_home(res[m], rets[m], s_out[m], r_out[m]) for m in range(2)]
    gathers = [RingGather(all_ref.at[n], rows, ids, *rest[10 * n : 10 * n + 2]) for n in range(parts)]
    scatters = [
        RingScatter(
            part.at[n], rows, ids, rest[10 * n + 4 : 10 * n + 10], *rest[10 * n + 2 : 10 * n + 4]
        )
        for n in range(parts)
    ]
    for n in range(parts):
        for x in arriving:
            x.start(max(1, n * near), (n + 1) * near)
    for m in range(2):
        inbox[m][0] = outs[m][exp]
    beside[0]()
    for n in range(parts):
        for x in arriving:
            x.wait_recv(max(1, n * near), (n + 1) * near)
        all_ref[n, me, :filled] = inbox[0][n * near : (n + 1) * near].reshape(filled, width)
        last = [inbox[1][n * near + k] for k in range(near)]
        last.append(jnp.zeros((rows - filled - near, width), F32))
        all_ref[n, me, filled:] = jnp.concatenate(last, 0).astype(BF16)
        gathers[n].start()
    for n in range(parts):
        block(n, me, part)
    for g in gathers:
        g.forward()
    for n in range(parts):
        gathers[n].wait_left()
        block(n, left, part)
        scatters[n].send_left()
        gathers[n].wait_right()
        block(n, right, part)
        scatters[n].send_right()
        gathers[n].wait_far()
        block(n, far, part)
        scatters[n].send_far()
        done(n)
    beside[1]()
    for n in range(parts):
        scatters[n].send_sums()
    beside[2]()
    for n in range(parts):
        total = scatters[n].total().astype(BF16)
        res[0][n * near : (n + 1) * near] = total[:filled].reshape(near, TILE, width)
        last = total[filled:].astype(F32)
        for k in range(near):
            res[1][n * near + k] = last[k : k + 1]
        for x in leaving:
            x.start(max(1, n * near), (n + 1) * near)
    for m in range(2):
        rets[m][exp] = res[m][0]
    beside[3]()
    for x in leaving:
        x.wait_recv()
    for x in (*gathers, *scatters, *arriving, *leaving):
        x.wait_send()


def slot_buffers(experts, width):
    return [pltpu.VMEM((experts, TILE, width), BF16), pltpu.VMEM((experts, 1, width), F32)]


def expert_scratch(experts, rows, width):
    ring = [*[pltpu.SemaphoreType.DMA((6,))] * 4, *scatter_buffers(rows, width)]
    return [
        pltpu.VMEM((PARTS, 4, rows, width), BF16),
        *slot_buffers(experts, width) * 2,
        *[pltpu.SemaphoreType.DMA((experts,))] * 8,
        *ring * PARTS,
    ]


def route_tables(routes_ref, experts):
    rows = routes_ref.shape[0]
    routes = routes_ref[...]
    lanes = lax.broadcasted_iota(jnp.int32, (rows, experts), 1)
    hot = [jnp.where(routes[:, c : c + 1] == lanes, 1.0, 0.0) for c in range(TOP)]
    row = lax.broadcasted_iota(jnp.int32, (rows, rows), 0)
    col = lax.broadcasted_iota(jnp.int32, (rows, rows), 1)
    before = jnp.where(row > col, 1.0, 0.0).astype(BF16)
    earlier = mm(before, (hot[0] + hot[1]).astype(BF16))
    wide = lax.broadcasted_iota(jnp.int32, (rows, experts * (TILE + 1)), 1).astype(F32)
    slots = []
    for c in range(TOP):
        slot = jnp.sum(hot[c] * earlier, -1, keepdims=True)
        expert = routes[:, c : c + 1].astype(F32)
        target = jnp.where(slot < TILE, expert * TILE + slot, experts * TILE + expert)
        slots.append(jnp.where(wide == target, 1.0, 0.0).astype(BF16))
    return hot, slots


def gates_of(logits, hot):
    chosen = [jnp.sum(h * logits, -1, keepdims=True) for h in hot]
    peak = jnp.maximum(chosen[0], chosen[1])
    raised = [jnp.exp(c - peak) for c in chosen]
    total = 1.0 / (raised[0] + raised[1])
    return [r * total for r in raised]


def part_rows(experts, capacity):
    return -(-(experts // PARTS) * capacity // TILE) * TILE


def bucket_bounds():
    half = BUCKETS // 2
    powers = np.arange(1, BUCKETS - half) / (BUCKETS - half)
    return [int(m) for m in np.ceil(half * (REACH / half) ** powers)]


def tile_buckets(kind):
    row = lax.broadcasted_iota(jnp.int32, (SPAN, 2 * SPAN), 0)
    col = lax.broadcasted_iota(jnp.int32, (SPAN, 2 * SPAN), 1)
    ahead = kind * SPAN + row - lax.rem(col, SPAN)
    n = jnp.maximum(ahead, 0)
    bucket = jnp.minimum(n, BUCKETS // 2)
    for bound in bucket_bounds():
        bucket += (n >= bound).astype(jnp.int32)
    return ahead, bucket


def tile_range(kind):
    half = BUCKETS // 2
    ends = [max(kind * SPAN + r - c, 0) for r, c in ((0, SPAN - 1), (SPAN - 1, 0))]
    first, last = (min(n, half) + sum(n >= m for m in bucket_bounds()) for n in ends)
    return range(first, last + 1)


def make_tiles(table_ref, tiles_ref, heads):
    repeat = tiles_ref.shape[3] // (2 * SPAN)
    for k in range(KINDS - 1):
        ahead, bucket = tile_buckets(k)
        for h in range(heads):
            tile = jnp.full(bucket.shape, NEG, F32)
            for b in tile_range(k):
                tile = jnp.where(bucket == b, table_ref[b : b + 1, h : h + 1], tile)
            tile = jnp.where(ahead < 0, NEG, tile)
            tiles_ref[h, k] = jnp.concatenate([tile] * repeat, 1)


def bias_rows(tiles_ref, table_ref, kind_ref, head, block):
    kind = kind_ref[block : block + 1, :]
    last = table_ref[BUCKETS - 1 : BUCKETS, head : head + 1]
    rows = jnp.where(kind == 3, last, NEG)
    for k in (2, 1, 0):
        rows = jnp.where(kind == k, tiles_ref[head, k], rows)
    return rows


def head_columns(ref, group, head, heads):
    at = (group * heads + head) * HEAD_DIM
    return ref[:, at : at + HEAD_DIM]


def attend(
    ids, wait_all_here, x, gain_ref, w_qkv, w_out, table_ref, kind_ref, all_ref, proj_ref, att_ref,
    tiles_ref, s_ref, p_ref, part, scratch
):
    bufs, (s_ag, r_ag, s_rs, r_rs) = scratch[:6], scratch[6:]
    me, right, left = ids
    far = lax.rem(me + 2, 4)
    rows, width = x.shape
    seq = 4 * rows
    heads = w_out.shape[0] // HEAD_DIM
    all_ref[me] = norm(x, gain_ref[...])
    gather = RingGather(all_ref, rows, ids, s_ag, r_ag)
    wait_all_here()
    gather.start()
    make_tiles(table_ref, tiles_ref, heads)
    gather.forward()
    gather.wait_left()
    gather.wait_right()
    gather.wait_far()
    proj_ref[...] = mm(all_ref[...].reshape(seq, width), w_qkv[...]).astype(BF16)
    parts = []
    for h in range(heads):
        q, k, v = (head_columns(proj_ref, g, h, heads) for g in range(3))
        s_ref[...] = mm_nt(q, k)
        for b in range(seq // SPAN):
            at = slice(b * SPAN, (b + 1) * SPAN)
            s = s_ref[at, :] * HEAD_DIM**-0.5 + bias_rows(tiles_ref, table_ref, kind_ref, h, b)
            e = jnp.exp(s - jnp.max(s, -1, keepdims=True))
            p_ref[at, :] = (e * (1.0 / jnp.sum(e, -1, keepdims=True))).astype(BF16)
        parts.append(mm(p_ref[...], v).astype(BF16))
    att_ref[...] = jnp.concatenate(parts, 1).reshape(att_ref.shape)
    scatter = RingScatter(part, rows, ids, bufs, s_rs, r_rs)
    part[far] = mm(att_ref[far], w_out[...]).astype(BF16)
    scatter.send_far()
    part[right] = mm(att_ref[right], w_out[...]).astype(BF16)
    scatter.send_right()
    part[left] = mm(att_ref[left], w_out[...]).astype(BF16)
    scatter.send_left()
    part[me] = mm(att_ref[me], w_out[...]).astype(BF16)
    scatter.send_sums()
    total = scatter.total()
    gather.wait_send()
    scatter.wait_send()
    return total


def attend_back(
    ids, dmiddle, all_ref, proj_ref, att_ref, w_qkv, w_out, table_ref, kind_ref,
    perm_ref, perm_out_ref, pq_ref, po_ref, dtable_ref, ready,
    tiles_ref, dtiles_ref, s_ref, dp_ref, p_ref, ds_ref, da_ref, dproj_ref, db_ref, part, scratch
):
    bufs, (s_ag, r_ag, s_rs, r_rs) = scratch[:6], scratch[6:]
    me, right, left = ids
    far = lax.rem(me + 2, 4)
    rows, width = dmiddle.shape
    seq = 4 * rows
    heads = w_out.shape[0] // HEAD_DIM
    scale = HEAD_DIM**-0.5
    db_ref[me] = dmiddle.astype(BF16)
    gather = RingGather(db_ref, rows, ids, s_ag, r_ag)
    gather.start()
    make_tiles(table_ref, tiles_ref, heads)
    gather.forward()
    gather.wait_left()
    gather.wait_right()
    gather.wait_far()
    da_ref[...] = mm_nt(db_ref[...].reshape(seq, width), w_out[...]).astype(BF16)
    dq, dk, dv = [], [], []
    for h in range(heads):
        q, k, v = (head_columns(proj_ref, g, h, heads) for g in range(3))
        da = head_columns(da_ref, 0, h, heads)
        s_ref[...] = mm_nt(q, k)
        dp_ref[...] = mm_nt(da, v)
        dtiles_ref[...] = jnp.zeros(dtiles_ref.shape, F32)
        for b in range(seq // SPAN):
            at = slice(b * SPAN, (b + 1) * SPAN)
            s = s_ref[at, :] * scale + bias_rows(tiles_ref, table_ref, kind_ref, h, b)
            e = jnp.exp(s - jnp.max(s, -1, keepdims=True))
            p = e * (1.0 / jnp.sum(e, -1, keepdims=True))
            dp = dp_ref[at, :]
            ds = p * (dp - jnp.sum(p * dp, -1, keepdims=True))
            p_ref[at, :] = p.astype(BF16)
            ds_ref[at, :] = ds.astype(BF16)
            kind = kind_ref[b : b + 1, :]
            for n in range(KINDS):
                dtiles_ref[n] += jnp.where(kind == n, ds, 0.0)
        for n in range(KINDS):
            folded = dtiles_ref[n, :, : 2 * SPAN]
            for m in range(1, seq // (2 * SPAN)):
                folded = folded + dtiles_ref[n, :, m * 2 * SPAN : (m + 1) * 2 * SPAN]
            dtiles_ref[n, :, : 2 * SPAN] = folded
        sums = [jnp.zeros((1, 2 * SPAN), F32)] * BUCKETS
        for n in range(KINDS - 1):
            bucket = tile_buckets(n)[1]
            folded = dtiles_ref[n, :, : 2 * SPAN]
            for b in tile_range(n):
                hit = jnp.where(bucket == b, folded, 0.0)
                sums[b] = sums[b] + jnp.sum(hit, 0, keepdims=True)
        rest = dtiles_ref[KINDS - 1, :, : 2 * SPAN]
        sums[-1] = sums[-1] + jnp.sum(rest, 0, keepdims=True)
        dtable_ref[h] = jnp.concatenate(sums, 0)
        p = p_ref[...]
        ds = ds_ref[...]
        dq.append((mm(ds, k) * scale).astype(BF16))
        dk.append((mm_tn(ds, q) * scale).astype(BF16))
        dv.append(mm_tn(p, da).astype(BF16))
    dproj_ref[...] = jnp.concatenate(dq + dk + dv, 1).reshape(dproj_ref.shape)
    scatter = RingScatter(part, rows, ids, bufs, s_rs, r_rs)
    part[far] = mm_nt(dproj_ref[far], w_qkv[...]).astype(BF16)
    scatter.send_far()
    part[right] = mm_nt(dproj_ref[right], w_qkv[...]).astype(BF16)
    scatter.send_right()
    part[left] = mm_nt(dproj_ref[left], w_qkv[...]).astype(BF16)
    scatter.send_left()
    part[me] = mm_nt(dproj_ref[me], w_qkv[...]).astype(BF16)
    dproj = dproj_ref[...].reshape(seq, dproj_ref.shape[2])
    d_qkv = mm_tn(all_ref[...].reshape(seq, width), dproj).astype(BF16)
    pq_ref[...] = mm(perm_ref[...], d_qkv).astype(BF16)
    ready(0)
    scatter.send_sums()
    d_out = mm_tn(att_ref[...].reshape(seq, att_ref.shape[2]), db_ref[...].reshape(seq, width))
    po_ref[...] = mm(perm_out_ref[...], d_out.astype(BF16)).astype(BF16)
    ready(1)
    total = scatter.total()
    gather.wait_send()
    scatter.wait_send()
    return total


def layer_kernel(
    layer, x_ref, gains, w_qkv_both, w_out_both, tables, kind_ref, routers, routes_ref,
    w_in_both, w_back_both,
    h_ref, all_ref, proj_ref, att_ref, middle_ref, mixed_ref, logits_ref, picked_ref,
    ent_out, pre_out, *scratch
):
    tiles_ref, s_ref, p_ref, part, w_in, w_back, ent_ref, pre_ref, sems, save_sems = scratch[:10]
    outs, rets = scratch[10:12], scratch[12:14]
    loads, saves = Loads(sems), Loads(save_sems)
    loads.start(w_in_both.at[layer], w_in)
    loads.start(w_back_both.at[layer], w_back)
    gain_one, gain_two = gains.at[2 * layer], gains.at[2 * layer + 1]
    w_qkv, w_out = w_qkv_both.at[layer], w_out_both.at[layer]
    table_ref, router_ref = tables.at[layer], routers.at[layer]
    ids, wait_all_here = meet_all()
    rows, width = x_ref.shape
    x = x_ref[...].astype(F32)
    branch = attend(
        ids, wait_all_here, x, gain_one, w_qkv, w_out, table_ref, kind_ref, all_ref, proj_ref, att_ref,
        tiles_ref, s_ref, p_ref, part, scratch[14:24]
    )
    middle = x + branch
    middle_ref[...] = middle
    mixed = norm(middle, gain_two[...])
    mixed_ref[...] = mixed
    hot, slots = route_tables(routes_ref, logits_ref.shape[1])
    set_slots(*outs, mm_tn(slots[0] + slots[1], mixed))

    def block(n, j, part):
        pre = mm(ent_ref[n, j], w_in[...])
        pre_ref[n, j] = pre
        hidden = gelu_parts(pre)[0].astype(BF16)
        part[n, j] = mm_nt(hidden, w_back[...]).astype(BF16)

    def find_logits():
        logits_ref[...] = mm(mixed_ref[...], router_ref[...])
        loads.wait_all()

    def save(n):
        saves.start(ent_ref.at[n], ent_out.at[n])
        saves.start(pre_ref.at[n], pre_out.at[n])

    nothing = lambda: None
    run_experts(
        ids, outs, ent_ref, rets, block, save,
        (find_logits, nothing, nothing, nothing), scratch[24:]
    )
    gates = gates_of(logits_ref[...], hot)
    returned = get_slots(*rets)
    y = middle_ref[...]
    for c in range(TOP):
        picked = mm(slots[c], returned)
        picked_ref[c] = picked.astype(BF16)
        y = y + gates[c] * picked
    h_ref[...] = y.astype(BF16)
    saves.wait_all()


def layer_forward(x, layer, weights, kind, routes, slots):
    gains, w_qkv, w_out, table, router, w_in, w_back = weights
    rows, width = x.shape
    seq, part, experts = 4 * rows, w_out.shape[1], router.shape[2]
    heads = part // HEAD_DIM
    vm, far = pl.BlockSpec(memory_space=pltpu.VMEM), pl.BlockSpec(memory_space=pl.ANY)
    shape = jax.ShapeDtypeStruct
    return pl.pallas_call(
        functools.partial(layer_kernel, layer),
        out_shape=(
            shape(x.shape, BF16),
            shape((4, rows, width), BF16),
            shape((seq, 3 * part), BF16),
            shape((4, rows, part), BF16),
            shape(x.shape, F32),
            shape(x.shape, BF16),
            shape((rows, experts), F32),
            shape((TOP, rows, width), BF16),
            shape((PARTS, 4, slots, width), BF16),
            shape((PARTS, 4, slots, w_in.shape[2]), F32),
        ),
        in_specs=[vm] * 8 + [far] * 2,
        out_specs=(vm,) * 8 + (far,) * 2,
        scratch_shapes=[
            pltpu.VMEM((heads, KINDS - 1, SPAN, seq), F32),
            pltpu.VMEM((seq, seq), F32),
            pltpu.VMEM((seq, seq), BF16),
            pltpu.VMEM((4, rows, width), BF16),
            pltpu.VMEM(w_in.shape[1:], BF16),
            pltpu.VMEM(w_back.shape[1:], BF16),
            pltpu.VMEM((PARTS, 4, slots, width), BF16),
            pltpu.VMEM((PARTS, 4, slots, w_in.shape[2]), F32),
            pltpu.SemaphoreType.DMA((2,)),
            pltpu.SemaphoreType.DMA((2 * PARTS,)),
            *slot_buffers(experts, width) * 2,
            *scatter_buffers(rows, width),
            *[pltpu.SemaphoreType.DMA((6,))] * 4,
            *expert_scratch(experts, slots, width),
        ],
        compiler_params=pltpu.CompilerParams(
            collective_id=layer, has_side_effects=True, vmem_limit_bytes=56 << 20
        ),
    )(x, gains, w_qkv, w_out, table, kind, router, routes, w_in, w_back)


def layer_back_kernel(
    layer, g_ref, x_ref, gains, w_qkv_both, w_out_both, tables, kind_ref, routers, routes_ref,
    middle_ref, mixed_ref, logits_ref, picked_ref,
    w_in_both, w_back_both, perm_in, perm_out_in, all_in, proj_in, att_in, ent_in, pre_in,
    dx_ref, dxb_ref, small_ref, pq_ref, po_ref,
    d_in_out, d_back_out, got_in, got_back, got_pq, got_po, *scratch
):
    (
        tiles_ref, dtiles_ref, s_ref, dp_ref, p_ref, ds_ref, da_ref, dproj_ref, db_ref, part,
        darr_ref, hid_ref, dpre_ref, e_in, e_back, drouter_ref, dtable_ref, s_x, r_x,
        d_in, d_back, w_in, w_back, perm_ref, perm_out_ref, all_ref, proj_ref, att_ref,
        ent_ref, pre_ref, sems, save_sems
    ) = scratch[:32]
    outs, rets = scratch[32:34], scratch[34:36]
    loads, saves = Loads(sems), Loads(save_sems)
    loads.start(w_back_both.at[layer], w_back)
    loads.start(w_in_both.at[layer], w_in)
    loads.start(pre_in, pre_ref)
    loads.start(ent_in, ent_ref)
    loads.start(all_in, all_ref)
    loads.start(proj_in, proj_ref)
    loads.start(att_in, att_ref)
    loads.start(perm_in, perm_ref)
    loads.start(perm_out_in, perm_out_ref)
    gain_one, gain_two = gains.at[2 * layer], gains.at[2 * layer + 1]
    w_qkv, w_out = w_qkv_both.at[layer], w_out_both.at[layer]
    table_ref, router_ref = tables.at[layer], routers.at[layer]
    partner = 1 - lax.axis_index("section")
    ids, wait_all_here = meet_all(partner)
    rows, width = x_ref.shape

    def across(k, src, dst):
        return remote(src, dst, s_x, r_x, k, "section", partner)

    crossing = [
        across(0, e_back, got_back),
        across(1, e_in, got_in),
        across(2, pq_ref, got_pq),
        across(3, po_ref, got_po),
    ]
    g = g_ref[...].astype(F32)
    hot, slots = route_tables(routes_ref, logits_ref.shape[1])
    gates = gates_of(logits_ref[...], hot)
    dreturned = mm_tn(slots[0], (gates[0] * g).astype(BF16)) + mm_tn(
        slots[1], (gates[1] * g).astype(BF16)
    )
    set_slots(*outs, dreturned)
    wait_all_here()

    def logits_back():
        g = g_ref[...].astype(F32)
        dgates = [
            jnp.sum(g * picked_ref[c].astype(F32), -1, keepdims=True) for c in range(TOP)
        ]
        mean = gates[0] * dgates[0] + gates[1] * dgates[1]
        dchosen = [a * (b - mean) for a, b in zip(gates, dgates)]
        dlogits = (hot[0] * dchosen[0] + hot[1] * dchosen[1]).astype(BF16)
        drouter_ref[...] = mm_tn(mixed_ref[...], dlogits)
        dx_ref[...] = mm_nt(dlogits, router_ref[...])
        loads.wait(0, 1, 2)

    def block(n, j, expert_part):
        hidden, slope = gelu_parts(pre_ref[n, j])
        hid_ref[n, j] = hidden.astype(BF16)
        dpre = (mm(darr_ref[n, j], w_back[...]) * slope).astype(BF16)
        dpre_ref[n, j] = dpre
        expert_part[n, j] = mm_nt(dpre, w_in[...]).astype(BF16)

    def flat(ref):
        return ref[...].reshape(math.prod(ref.shape[:3]), ref.shape[3])

    def back_grad():
        grad = mm_tn(flat(darr_ref), flat(hid_ref))
        d_back[...] = grad
        saves.start(d_back, d_back_out)
        e_back[...] = grad.astype(BF16)
        crossing[0].start()

    def in_grad():
        loads.wait(3)
        grad = mm_tn(flat(ent_ref), flat(dpre_ref))
        d_in[...] = grad
        saves.start(d_in, d_in_out)
        e_in[...] = grad.astype(BF16)
        crossing[1].start()

    run_experts(
        ids, outs, darr_ref, rets, block, lambda n: None,
        (logits_back, back_grad, lambda: None, in_grad), scratch[46:]
    )
    dleft = get_slots(*rets)
    loads.wait(*range(4, 9))
    dmixed = mm(slots[0] + slots[1], dleft) + dx_ref[...]
    dnorm, dgain = norm_back(middle_ref[...], gain_two[...], dmixed)
    small_ref[...] = pack_gain(dgain, 1, small_ref.shape) + pack_router(
        drouter_ref[...], small_ref.shape
    )
    dmiddle = g_ref[...].astype(F32) + dnorm
    dx_ref[...] = dmiddle
    dnormed = attend_back(
        ids, dmiddle, all_ref, proj_ref, att_ref, w_qkv, w_out, table_ref, kind_ref,
        perm_ref, perm_out_ref, pq_ref, po_ref, dtable_ref, lambda k: crossing[2 + k].start(),
        tiles_ref, dtiles_ref, s_ref, dp_ref, p_ref, ds_ref, da_ref, dproj_ref, db_ref, part,
        scratch[36:46]
    )
    dnorm, dgain = norm_back(x_ref[...].astype(F32), gain_one[...], dnormed)
    small_ref[...] += pack_gain(dgain, 0, small_ref.shape) + pack_table(
        dtable_ref, small_ref.shape
    )
    dx = dx_ref[...] + dnorm
    dx_ref[...] = dx
    dxb_ref[...] = dx.astype(BF16)
    saves.wait_all()
    for c in crossing:
        c.wait()


def layer_backward(g, keep, layer, weights, kind, routes, slots, perm, perm_out):
    x, normed, proj, attended, middle, mixed, logits, picked, entering, pre = keep
    gains, w_qkv, w_out, table, router, w_in, w_back = weights
    rows, width = x.shape
    seq, part, experts = 4 * rows, w_out.shape[1], router.shape[2]
    heads, hid = part // HEAD_DIM, w_in.shape[2]
    w_shape = w_in.shape[1:]
    vm, far = pl.BlockSpec(memory_space=pltpu.VMEM), pl.BlockSpec(memory_space=pl.ANY)
    shape = jax.ShapeDtypeStruct
    pq = shape((perm.shape[0], 3 * part), BF16)
    po = shape((perm_out.shape[0], width), BF16)
    loaded = (normed, proj, attended, entering, pre)
    return pl.pallas_call(
        functools.partial(layer_back_kernel, layer),
        out_shape=(
            shape(x.shape, F32),
            shape(x.shape, BF16),
            shape((perm.shape[0] // OWN, SMALL), F32),
            pq,
            po,
            shape(w_shape, F32),
            shape(w_shape, F32),
            shape(w_shape, BF16),
            shape(w_shape, BF16),
            pq,
            po,
        ),
        in_specs=[vm] * 13 + [far] * 9,
        out_specs=(vm,) * 5 + (far,) * 6,
        scratch_shapes=[
            pltpu.VMEM((heads, KINDS - 1, SPAN, seq), F32),
            pltpu.VMEM((KINDS, SPAN, seq), F32),
            pltpu.VMEM((seq, seq), F32),
            pltpu.VMEM((seq, seq), F32),
            pltpu.VMEM((seq, seq), BF16),
            pltpu.VMEM((seq, seq), BF16),
            pltpu.VMEM((seq, part), BF16),
            pltpu.VMEM((4, rows, 3 * part), BF16),
            pltpu.VMEM((4, rows, width), BF16),
            pltpu.VMEM((4, rows, width), BF16),
            pltpu.VMEM((PARTS, 4, slots, width), BF16),
            pltpu.VMEM((PARTS, 4, slots, hid), BF16),
            pltpu.VMEM((PARTS, 4, slots, hid), BF16),
            pltpu.VMEM(w_shape, BF16),
            pltpu.VMEM(w_shape, BF16),
            pltpu.VMEM((width, experts), F32),
            pltpu.VMEM((heads, BUCKETS, 2 * SPAN), F32),
            *[pltpu.SemaphoreType.DMA((4,))] * 2,
            *[pltpu.VMEM(w_shape, F32)] * 2,
            *[pltpu.VMEM(w_shape, BF16)] * 2,
            *[pltpu.VMEM(a.shape, a.dtype) for a in (perm, perm_out, *loaded)],
            pltpu.SemaphoreType.DMA((9,)),
            pltpu.SemaphoreType.DMA((2,)),
            *slot_buffers(experts, width) * 2,
            *scatter_buffers(rows, width),
            *[pltpu.SemaphoreType.DMA((6,))] * 4,
            *expert_scratch(experts, slots, width),
        ],
        compiler_params=pltpu.CompilerParams(
            collective_id=2 + layer, has_side_effects=True, vmem_limit_bytes=60 << 20
        ),
    )(
        g, x, gains, w_qkv, w_out, table, kind, router, routes, middle, mixed, logits, picked,
        w_in, w_back, perm, perm_out, *loaded
    )


SMALL = 256
OWN = 12
AT_TABLE = 2 * OWN


def grid_of(shape):
    return tuple(lax.broadcasted_iota(jnp.int32, shape, d) for d in (0, 1))


def one_hot(where):
    return jnp.where(where, 1.0, 0.0).astype(BF16)


def owner_rows(owners, width):
    row, col = grid_of((owners, width))
    return one_hot((col >= OWN * row) & (col < OWN * row + OWN))


def table_rows(owners):
    row, col = grid_of((BUCKETS, owners))
    return one_hot(col == 2 * row + lax.axis_index("ctx") // 2)


def table_column(head):
    return AT_TABLE + HEADS // 4 * lax.rem(lax.axis_index("ctx"), 2) + head


def at_router(experts):
    return AT_TABLE + BUCKETS * HEADS // 64


def router_mask(width, experts):
    row, col = grid_of((width, SMALL))
    first = at_router(experts) + experts * lax.rem(row, OWN)
    return (col >= first) & (col < first + experts)


def unpack_small(small, width, experts, heads):
    owners = small.shape[0]
    small = small.astype(BF16)
    own = owner_rows(owners, width)
    spread = mm_tn(small[:, :128], own)
    row, col = grid_of(spread.shape)
    gains = [
        jnp.sum(jnp.where(row == lax.rem(col, OWN) + n * OWN, spread, 0.0), 0, keepdims=True)
        for n in range(2)
    ]
    wide = mm_tn(own, small)
    wide = jnp.where(router_mask(width, experts), wide, 0.0).astype(BF16)
    row, col = grid_of((SMALL, experts))
    first = at_router(experts)
    inside = (row >= first) & (row < first + OWN * experts)
    router = mm(wide, one_hot(inside & (lax.rem(row + experts - first % experts, experts) == col)))
    table = mm(table_rows(owners), small[:, :128]).astype(BF16)
    row, col = grid_of((128, heads))
    table = mm(table, one_hot(row == table_column(col)))
    return gains, router.astype(BF16), table


def pack_gain(dgain, n, shape):
    width = dgain.shape[1]
    row, col = grid_of((width, shape[1]))
    own = owner_rows(shape[0], width).astype(F32) * dgain
    return mm(own.astype(BF16), one_hot(col == lax.rem(row, OWN) + n * OWN))


def pack_router(drouter, shape):
    width, experts = drouter.shape
    row, col = grid_of((experts, shape[1]))
    first = at_router(experts)
    wide = mm(
        drouter.astype(BF16), one_hot(lax.rem(col + experts - first % experts, experts) == row)
    )
    wide = jnp.where(router_mask(width, experts), wide, 0.0).astype(BF16)
    return mm(owner_rows(shape[0], width), wide)


def pack_table(dtable_ref, shape):
    total = jnp.zeros((BUCKETS, shape[1]), F32)
    col = grid_of(total.shape)[1]
    for h in range(dtable_ref.shape[0]):
        column = jnp.sum(dtable_ref[h], -1, keepdims=True)
        total = total + jnp.where(col == table_column(h), column, 0.0)
    return mm_tn(table_rows(shape[0]), total.astype(BF16))


def meet_everyone():
    barrier = pltpu.get_barrier_semaphore()
    peers = [("exp", 16), ("ctx", 4), ("section", 2)]
    for axis, count in peers:
        me = lax.axis_index(axis)

        def greet(k, carry, axis=axis, me=me, count=count):
            peer = lax.rem(me + k, count)
            pl.semaphore_signal(barrier, inc=1, device_id={axis: peer}, device_id_type=MESH)
            return carry

        lax.fori_loop(1, count, greet, 0)
    pl.semaphore_wait(barrier, sum(count - 1 for _, count in peers))


def ctx_exchange(src, dst, send, recv):
    me = lax.axis_index("ctx")
    copies = []
    for k in (1, 3, 2):
        peer = lax.rem(me + k, 4)
        copies.append(remote(src.at[peer], dst.at[me], send, recv, k, "ctx", peer))
    return copies


def weights_kernel(
    cols_ref, outp_ref, w_in, w_back, perm_ref, perm_out_ref, pick_ref, fill_ref, fill_small_ref,
    w_qkv, w_out, gains, routers, tables, both_in, both_back,
    zin, grid, grid_out, s_z, r_z, s_q, r_q, s_o, r_o, s_fq, r_fq, s_fo, r_fo, s_x, r_x, s_own
):
    meet_everyone()
    section, ctx, exp = (lax.axis_index(a) for a in ("section", "ctx", "exp"))
    partner = 1 - section
    count = grid.shape[1]
    turn = ctx_exchange(cols_ref, zin, s_z, r_z)
    for c in turn:
        c.start()
    w_in, w_back = w_in.at[0, 0], w_back.at[0, 0]
    cross_in = remote(w_in, both_in.at[section], s_x, r_x, 0, "section", partner)
    cross_back = remote(w_back, both_back.at[section], s_x, r_x, 1, "section", partner)
    cross_in.start()
    cross_back.start()
    zin[ctx] = cols_ref[ctx]

    def spread(ref, send, recv, k):
        peer = lax.rem(exp + k, count)
        at = ref.at[section, exp]
        return remote(at, at, send, recv, k, "exp", peer)

    def forward(ref, send, recv, k):
        at = ref.at[section, lax.rem(exp + count - k, count)]
        return remote(at, at, send, recv, k, "section", partner)

    def each(act, first=1):
        def body(k, carry):
            act(k)
            return carry

        lax.fori_loop(first, count, body, 0)

    for c in turn:
        c.wait_recv()
    came = zin[...].reshape(zin.shape[0] * zin.shape[1], zin.shape[2])
    small = mm(fill_small_ref[...], came[:, :SMALL]).astype(BF16)
    outp = outp_ref[...]
    grid_out[section, exp] = jnp.concatenate([outp[:, :SMALL] + small, outp[:, SMALL:]], 1)
    each(lambda k: spread(grid_out, s_o, r_o, k).start())
    grid[section, exp] = mm(fill_ref[...], came).astype(BF16)
    each(lambda k: spread(grid, s_q, r_q, k).start())
    forward(grid_out, s_fo, r_fo, 0).start()
    forward(grid, s_fq, r_fq, 0).start()
    own_in = pltpu.make_async_copy(w_in, both_in.at[section], s_own.at[0])
    own_back = pltpu.make_async_copy(w_back, both_back.at[section], s_own.at[1])
    own_in.start()
    own_back.start()

    def relay(ref, s, r, sf, rf, k):
        spread(ref, s, r, k).wait_recv()
        forward(ref, sf, rf, k).start()

    each(lambda k: relay(grid_out, s_o, r_o, s_fo, r_fo, k))
    each(lambda k: relay(grid, s_q, r_q, s_fq, r_fq, k))

    def unpack(layer):
        flat = grid[layer].reshape(perm_ref.shape[1], grid.shape[3])
        w_qkv[layer] = mm(perm_ref[...], flat).astype(BF16)
        flat = grid_out[layer].reshape(perm_out_ref.shape[1], grid_out.shape[3])
        w_out[layer] = mm(perm_out_ref[...], flat).astype(BF16)
        small = mm(pick_ref[...], flat[:, :SMALL])
        two, routers[layer], tables[layer] = unpack_small(
            small, routers.shape[1], routers.shape[2], tables.shape[2]
        )
        gains[2 * layer], gains[2 * layer + 1] = two

    unpack(section)
    each(lambda k: forward(grid_out, s_fo, r_fo, k).wait_recv(), 0)
    each(lambda k: forward(grid, s_fq, r_fq, k).wait_recv(), 0)
    unpack(partner)
    each(lambda k: spread(grid_out, s_o, r_o, k).wait_send())
    each(lambda k: spread(grid, s_q, r_q, k).wait_send())
    each(lambda k: forward(grid_out, s_fo, r_fo, k).wait_send(), 0)
    each(lambda k: forward(grid, s_fq, r_fq, k).wait_send(), 0)
    for c in turn:
        c.wait_send()
    own_in.wait()
    own_back.wait()
    cross_in.wait()
    cross_back.wait()


def gather_weights(cols, outp, w_in, w_back, perm, perm_out, pick, fill, fill_small):
    width, part = outp.shape[1], cols.shape[2]
    count = perm_out.shape[1] // TILE
    vm, far = pl.BlockSpec(memory_space=pltpu.VMEM), pl.BlockSpec(memory_space=pl.ANY)
    dma = lambda n: pltpu.SemaphoreType.DMA((n,))
    return pl.pallas_call(
        weights_kernel,
        out_shape=(
            jax.ShapeDtypeStruct((2, width, part), BF16),
            jax.ShapeDtypeStruct((2, perm_out.shape[0], width), BF16),
            jax.ShapeDtypeStruct((4, 1, width), F32),
            jax.ShapeDtypeStruct((2, width, count), BF16),
            jax.ShapeDtypeStruct((2, BUCKETS, part // (3 * HEAD_DIM)), F32),
            jax.ShapeDtypeStruct((2, *w_in.shape[2:]), BF16),
            jax.ShapeDtypeStruct((2, *w_back.shape[2:]), BF16),
        ),
        in_specs=[vm] * 2 + [far] * 2 + [vm] * 5,
        out_specs=(vm,) * 5 + (far,) * 2,
        scratch_shapes=[
            pltpu.VMEM(cols.shape, BF16),
            pltpu.VMEM((2, count, fill.shape[0], part), BF16),
            pltpu.VMEM((2, count, 16, width), BF16),
            dma(4), dma(4), *[dma(count)] * 8, dma(2), dma(2), dma(2),
        ],
        compiler_params=pltpu.CompilerParams(
            collective_id=4, has_side_effects=True, vmem_limit_bytes=48 << 20
        ),
    )(cols, outp, w_in, w_back, perm, perm_out, pick, fill, fill_small)


def owners_kernel(
    small0, small1, spread_ref, y0, y1, dx0, dx1,
    pq0, pq1, gq0, gq1, po0, po1, go0, go1, in0, in1, gin0, gin1, back0, back1, gback0, gback1,
    turned, out_grad, d_in_out, d_back_out, layer_out, input_grad,
    pq, gq, po, go, d_in, gin, d_back, gback,
    sent_small, got_small, sent_y, sent_dx, pieces, box, pieces_out, box_out, summed,
    s_s, r_s, s_q, r_q, s_o, r_o, s_z, r_z, sems, save_sems
):
    section, ctx, exp = (lax.axis_index(a) for a in ("section", "ctx", "exp"))
    partner = 1 - section
    first = section == 0
    of_first = (po0, go0, pq0, gq0, in0, gin0, back0, gback0)
    of_second = (po1, go1, pq1, gq1, in1, gin1, back1, gback1)
    held = (po, go, pq, gq, d_in, gin, d_back, gback)

    def load(sources):
        for k, (src, dst) in enumerate(zip(sources, held)):
            pltpu.make_async_copy(src, dst, sems.at[k]).start()

    @pl.when(first)
    def _():
        load(of_first)

    @pl.when(jnp.logical_not(first))
    def _():
        load(of_second)

    def loaded(*which):
        for k in which:
            pltpu.make_async_copy(of_first[k], held[k], sems.at[k]).wait()

    meet_everyone()
    sent_small[...] = jnp.where(first, small1[...], small0[...])
    cross = [
        remote(sent_small, got_small, s_s, r_s, 0, "section", partner),
        remote(sent_y, layer_out.at[section], s_s, r_s, 1, "section", partner),
        remote(sent_dx, input_grad.at[section], s_s, r_s, 2, "section", partner),
    ]
    cross[0].start()

    def both(a, b):
        return a[...].astype(F32) + b[...].astype(F32)

    loaded(2, 3)
    pieces[...] = both(pq, gq).astype(BF16).reshape(pieces.shape)
    swap = exchange_out(pieces, box, s_q, r_q)
    swap.start()
    loaded(0, 1)
    dense = both(po, go)
    cross[0].wait_recv()
    small = jnp.where(first, small0[...], small1[...]) + got_small[...]
    wide = mm(spread_ref[...], small.astype(BF16))
    dense = jnp.concatenate([dense[:, :SMALL] + wide, dense[:, SMALL:]], 1)
    pieces_out[...] = dense.astype(BF16).reshape(pieces_out.shape)
    swap_out = exchange_out(pieces_out, box_out, s_o, r_o)
    swap_out.start()
    box[0] = pieces[exp]
    box_out[0] = pieces_out[exp]
    sent_y[...] = jnp.where(first, y1[...], y0[...])
    cross[1].start()
    sent_dx[...] = jnp.where(first, dx1[...], dx0[...])
    cross[2].start()
    layer_out[section] = jnp.where(first, y0[...], y1[...])
    input_grad[section] = jnp.where(first, dx0[...], dx1[...])
    saves = Loads(save_sems)
    loaded(4, 5)
    d_in[...] += gin[...].astype(F32)
    saves.start(d_in, d_in_out.at[0, 0])
    loaded(6, 7)
    d_back[...] += gback[...].astype(F32)
    saves.start(d_back, d_back_out.at[0, 0])
    swap.wait_recv()
    total = box[0].astype(F32)
    for k in range(1, box.shape[0]):
        total = total + box[k].astype(F32)
    summed[...] = jnp.zeros(summed.shape, F32)
    for c in range(4):
        summed[c, :OWN, :] = total[c * OWN : (c + 1) * OWN]
    swap_out.wait_recv()
    total = box_out[0].astype(F32)
    for k in range(1, box_out.shape[0]):
        total = total + box_out[k].astype(F32)
    out_grad[...] = total
    for c in range(4):
        summed[c, OWN : OWN + 1, :SMALL] = total[OWN + c : OWN + c + 1, :SMALL]
    turn = ctx_exchange(summed, turned, s_z, r_z)
    for c in turn:
        c.start()
    turned[ctx] = summed[ctx]
    for c in turn:
        c.wait()
    cross[0].wait_send()
    cross[1].wait()
    cross[2].wait()
    swap.wait_send()
    swap_out.wait_send()
    saves.wait_all()


def sum_at_owners(pq, gq, po, go, small, spread, d_in, g_in, d_back, g_back, y, dx, count):
    rows, part = pq[0].shape
    out_rows, width = po[0].shape
    vm, far = pl.BlockSpec(memory_space=pltpu.VMEM), pl.BlockSpec(memory_space=pl.ANY)
    dma = lambda n: pltpu.SemaphoreType.DMA((n,))
    own = (rows // count, part)
    own_out = (out_rows // count, width)
    quarter = (4, TILE, part)
    held = [a[0] for a in (pq, gq, po, go, d_in, g_in, d_back, g_back)]
    return pl.pallas_call(
        owners_kernel,
        out_shape=(
            jax.ShapeDtypeStruct(quarter, F32),
            jax.ShapeDtypeStruct(own_out, F32),
            jax.ShapeDtypeStruct((1, 1, *d_in[0].shape), F32),
            jax.ShapeDtypeStruct((1, 1, *d_back[0].shape), F32),
            jax.ShapeDtypeStruct((2, *y[0].shape), BF16),
            jax.ShapeDtypeStruct((2, *dx[0].shape), F32),
        ),
        in_specs=[vm] * 7 + [far] * 16,
        out_specs=(vm, vm, far, far, vm, vm),
        scratch_shapes=[
            *[pltpu.VMEM(a.shape, a.dtype) for a in held],
            pltpu.VMEM(small[0].shape, F32),
            pltpu.VMEM(small[0].shape, F32),
            pltpu.VMEM(y[0].shape, BF16),
            pltpu.VMEM(dx[0].shape, F32),
            pltpu.VMEM((count, *own), BF16),
            pltpu.VMEM((count, *own), BF16),
            pltpu.VMEM((count, *own_out), BF16),
            pltpu.VMEM((count, *own_out), BF16),
            pltpu.VMEM(quarter, F32),
            dma(3), dma(3), *[dma(count)] * 4, dma(4), dma(4), dma(8), dma(2),
        ],
        compiler_params=pltpu.CompilerParams(
            collective_id=5, has_side_effects=True, vmem_limit_bytes=52 << 20
        ),
    )(*small, spread, *y, *dx, *pq, *gq, *po, *go, *d_in, *g_in, *d_back, *g_back)


def packing(n_ctx, n_exp, own_rows):
    blocks = n_ctx * n_exp
    perm = np.zeros((blocks, own_rows, blocks, own_rows), np.float32)
    pick = np.zeros((blocks, n_exp, TILE), np.float32)
    perm_out = np.zeros((n_exp, TILE, n_exp, own_rows), np.float32)
    fill = np.zeros((n_ctx, own_rows, n_ctx, TILE), np.float32)
    fill_small = np.zeros((TILE, n_ctx, TILE), np.float32)
    for c in range(n_ctx):
        fill_small[own_rows + c, c, own_rows] = 1
        for i in range(own_rows):
            fill[c, i, c, i] = 1
    for e in range(n_exp):
        for i in range(own_rows):
            perm_out[e, i, e, i] = 1
        for c in range(n_ctx):
            for i in range(own_rows):
                perm[e * n_ctx + c, i, c * n_exp + e, i] = 1
            pick[c * n_exp + e, e, own_rows + c] = 1
    perm = perm.reshape(blocks * own_rows, blocks * own_rows)
    pick = pick.reshape(blocks, n_exp * TILE)
    perm_out = perm_out.reshape(n_exp * TILE, n_exp * own_rows)
    fill = fill.reshape(n_ctx * own_rows, n_ctx * TILE)
    fill_small = fill_small.reshape(TILE, n_ctx * TILE)
    pack = (perm, perm_out, pick.T.copy())
    unpack = (perm.T.copy(), perm_out.T.copy(), pick, fill, fill_small)
    return tuple(tuple(jnp.asarray(m, BF16) for m in ms) for ms in (pack, unpack))


def norm_scale(v):
    return lax.rsqrt(jnp.mean(v * v, -1, keepdims=True) + EPS)


def norm(v, gain):
    return (v * norm_scale(v) * gain).astype(BF16)


def norm_back(v, gain, du):
    r = norm_scale(v)
    dug = du * gain
    dv = r * dug - v * (r * r * r) * jnp.mean(dug * v, -1, keepdims=True)
    return dv, jnp.sum(du * v * r, 0, keepdims=True)


def gelu_parts(v):
    t = jnp.tanh(GELU_C * (v + 0.044715 * v * v * v))
    value = 0.5 * v * (1.0 + t)
    slope = 0.5 * (1.0 + t) + 0.5 * v * (1.0 - t * t) * GELU_C * (1.0 + 3 * 0.044715 * v * v)
    return value, slope


def on_device(
    inputs,
    cotangent,
    routes,
    block_order,
    attn_gain,
    qkv_weight,
    out_weight,
    rel_bias,
    moe_gain,
    router_weight,
    expert_in,
    expert_out,
):
    rows, width = inputs.shape[2:]
    n_ctx, n_exp = lax.axis_size("ctx"), lax.axis_size("exp")
    seq = rows * n_ctx
    own_rows = qkv_weight.shape[1]
    heads = HEADS // n_ctx
    part = heads * HEAD_DIM
    capacity = rows * TOP // n_exp + max(1, rows * TOP // (16 * n_exp))
    slots = part_rows(n_exp, capacity)
    section = lax.axis_index("section")
    ctx = lax.axis_index("ctx")
    first = section == 0

    (perm, perm_out, place), unpack = packing(n_ctx, n_exp, own_rows)
    small = jnp.concatenate(
        [attn_gain[0], moe_gain[0], rel_bias[0], router_weight[0].reshape(-1)]
    )
    n_small = small.shape[0]
    columns = qkv_weight[0].reshape(own_rows, 3, n_ctx, part).transpose(2, 0, 1, 3)
    columns = columns.reshape(n_ctx, own_rows, 3 * part)
    small_row = jnp.pad(small, (0, 3 * part - n_small))
    small_rows = jnp.broadcast_to(small_row, (n_ctx, 1, 3 * part))
    columns = jnp.concatenate([columns, small_rows], 1)
    columns = jnp.pad(columns, ((0, 0), (0, 15 - own_rows), (0, 0)))
    out_rows = jnp.pad(out_weight[0], ((0, 16 - own_rows), (0, 0)))
    w_qkv, w_out, gains, routers, tables, w_in, w_back = gather_weights(
        columns, out_rows, expert_in, expert_out, *unpack
    )
    weights = (gains, w_qkv, w_out, tables, routers, w_in, w_back)
    n_bias = BUCKETS * HEADS // (n_ctx * n_exp)
    ahead = block_order[:, None] - block_order[None, :]
    kind = jnp.repeat(jnp.where(ahead < 0, -1, jnp.minimum(ahead, 3)), SPAN, 1)

    own_routes = routes[0, :, 0]
    kept = jnp.where(first, own_routes[0], own_routes[1])
    given = jnp.where(first, own_routes[1], own_routes[0])
    taken = lax.ppermute(given, "section", [(0, 1), (1, 0)])
    layer_routes = (jnp.where(first, kept, taken), jnp.where(first, taken, kept))
    def forward(x, layer):
        h, *saved = layer_forward(x, layer, weights, kind, layer_routes[layer], slots)
        return h, (x, *saved)

    def backward(g, keep, layer):
        dx, dxb, d_small, pq, po, d_in, d_back, g_in, g_back, gq, go = layer_backward(
            g, keep, layer, weights, kind, layer_routes[layer], slots, perm, perm_out
        )
        return dx, dxb, (pq, gq, po, go, d_small, d_in, g_in, d_back, g_back)

    x = jnp.where(first, inputs[0, 0], inputs[1, 0])
    cot = jnp.where(first, cotangent[0, 0], cotangent[1, 0])
    h, keep0 = forward(x, 0)
    top, keep1 = forward(h, 1)
    _, dh, grads1 = backward(cot, keep1, 1)
    dx, _, grads0 = backward(dh, keep0, 0)
    pq, gq, po, go, d_small, d_in, g_in, d_back, g_back = zip(grads0, grads1)
    pieces, out_grad, d_in, d_back, layer_out, input_grad = sum_at_owners(
        pq, gq, po, go, d_small, place, d_in, g_in, d_back, g_back,
        (h, top), (dx, dh.astype(F32)), n_exp
    )
    qkv_grad = pieces[:, :own_rows].reshape(n_ctx, own_rows, 3, part)
    qkv_grad = qkv_grad.transpose(1, 2, 0, 3).reshape(own_rows, 3 * width)
    out_grad = out_grad[:own_rows]
    small = jnp.sum(pieces[:, own_rows, :n_small], 0)

    layer_out = layer_out.reshape(1, 2, 1, rows, width)
    input_grad = input_grad.reshape(1, 2, 1, rows, width)
    return (
        layer_out,
        input_grad,
        small[:own_rows][None],
        qkv_grad[None],
        out_grad[None],
        small[2 * own_rows : 2 * own_rows + n_bias][None],
        small[own_rows : 2 * own_rows][None],
        small[2 * own_rows + n_bias :].reshape(1, own_rows, n_exp),
        d_in,
        d_back,
    )


def solution(mesh):
    return jax.shard_map(
        on_device,
        mesh=mesh,
        in_specs=(
            P(None, "exp", "ctx", None),
            P(None, "exp", "ctx", None),
            P("section", None, "exp", "ctx", None),
            P(),
            P("section", ("ctx", "exp")),
            P("section", ("ctx", "exp"), None),
            P("section", ("ctx", "exp"), None),
            P("section", ("ctx", "exp")),
            P("section", ("ctx", "exp")),
            P("section", ("ctx", "exp"), None),
            P("section", "exp", None, "ctx"),
            P("section", "exp", None, "ctx"),
        ),
        out_specs=(
            P("section", None, "exp", "ctx", None),
            P("section", None, "exp", "ctx", None),
            P("section", ("ctx", "exp")),
            P("section", ("ctx", "exp"), None),
            P("section", ("ctx", "exp"), None),
            P("section", ("ctx", "exp")),
            P("section", ("ctx", "exp")),
            P("section", ("ctx", "exp"), None),
            P("section", "exp", None, "ctx"),
            P("section", "exp", None, "ctx"),
        ),
        check_vma=False,
    )
```

```python
import functools
import math

import jax
import jax.numpy as jnp
import numpy as np
from jax import lax
from jax.experimental import pallas as pl
from jax.experimental.pallas import tpu as pltpu
from jax.sharding import PartitionSpec as P

HEADS = 12
HEAD_DIM = 64
BUCKETS = 32
REACH = 128
TOP = 2
EPS = 1e-06
NEG = -1e30
SPAN = 64
KINDS = 4
MESH = pl.DeviceIdType.MESH
BF16 = jnp.bfloat16
F32 = jnp.float32
GELU_C = math.sqrt(2.0 / math.pi)


def dot(a, b, dims):
    return lax.dot_general(a, b, (dims, ((), ())), preferred_element_type=F32)


def mm(a, b):
    return dot(a, b, ((1,), (0,)))


def mm_nt(a, b):
    return dot(a, b, ((1,), (1,)))


def mm_tn(a, b):
    return dot(a, b, ((0,), (0,)))


def meet_neighbours(axis, count):
    me = lax.axis_index(axis)
    right, left = lax.rem(me + 1, count), lax.rem(me + count - 1, count)
    barrier = pltpu.get_barrier_semaphore()
    for neighbour in (left, right):
        pl.semaphore_signal(barrier, inc=1, device_id={axis: neighbour}, device_id_type=MESH)
    pl.semaphore_wait(barrier, 2)
    return me, right, left


def remote(src, dst, send, recv, k, axis, to):
    return pltpu.make_async_remote_copy(
        src_ref=src,
        dst_ref=dst,
        send_sem=send.at[k],
        recv_sem=recv.at[k],
        device_id={axis: to},
        device_id_type=MESH,
    )


def halves(rows):
    first = (rows // 2 + 15) // 16 * 16
    return (pl.ds(0, first), pl.ds(first, rows - first))


def ring_copy(send, recv, k, src, dst, to):
    return remote(src, dst, send, recv, k, "ctx", to)


class RingGather:
    def __init__(self, all_ref, rows, ids, send, recv):
        me, right, left = ids
        low, high = halves(rows)

        def pass_on(k, slot, half, to):
            at = all_ref.at[slot, half]
            return ring_copy(send, recv, k, at, at, to)

        self.first = (
            pass_on(0, me, low, right),
            pass_on(1, me, high, left),
            pass_on(2, me, high, right),
            pass_on(3, me, low, left),
        )
        self.second = (pass_on(4, left, low, right), pass_on(5, right, high, left))

    def start(self):
        for c in self.first:
            c.start()

    def forward(self):
        self.first[0].wait_recv()
        self.second[0].start()
        self.first[1].wait_recv()
        self.second[1].start()

    def wait_left(self):
        self.first[2].wait_recv()

    def wait_right(self):
        self.first[3].wait_recv()

    def wait_far(self):
        for c in self.second:
            c.wait_recv()

    def wait_send(self):
        for c in self.first + self.second:
            c.wait_send()


class RingScatter:
    def __init__(self, part, rows, ids, bufs, send, recv):
        me, right, left = ids
        far = lax.rem(me + 2, 4)
        low, high = halves(rows)
        far_l, far_r, sum_l, sum_r, in_l, in_r = bufs
        self.part, self.ids, self.n_low, self.bufs = part, ids, low.size, bufs
        copy = functools.partial(ring_copy, send, recv)
        self.far = (
            copy(0, part.at[far, low], far_l, right),
            copy(1, part.at[far, high], far_r, left),
        )
        self.right = copy(2, part.at[right, high], in_l.at[high], right)
        self.left = copy(3, part.at[left, low], in_r.at[low], left)
        self.sums = (
            copy(4, sum_r, in_l.at[low], right),
            copy(5, sum_l, in_r.at[high], left),
        )

    def send_far(self):
        for c in self.far:
            c.start()

    def send_left(self):
        self.left.start()

    def send_right(self):
        self.right.start()

    def send_sums(self):
        me, right, left = self.ids
        far_l, far_r, sum_l, sum_r, in_l, in_r = self.bufs
        n = self.n_low
        self.far[0].wait_recv()
        sum_r[...] = (self.part[right, :n, :].astype(F32) + far_l[...].astype(F32)).astype(BF16)
        self.sums[0].start()
        self.far[1].wait_recv()
        sum_l[...] = (self.part[left, n:, :].astype(F32) + far_r[...].astype(F32)).astype(BF16)
        self.sums[1].start()

    def total(self):
        for c in (self.right, self.left, *self.sums):
            c.wait_recv()
        in_l, in_r = self.bufs[4:]
        return self.part[self.ids[0]].astype(F32) + in_l[...].astype(F32) + in_r[...].astype(F32)

    def wait_send(self):
        for c in (*self.far, self.right, self.left, *self.sums):
            c.wait_send()


def scatter_buffers(rows, width):
    low, high = halves(rows)
    sizes = (low.size, high.size, high.size, low.size, rows, rows)
    return [pltpu.VMEM((n, width), BF16) for n in sizes]


TILE = 16
PARTS = 2


class Loads:
    def __init__(self, sems):
        self.sems, self.copies = sems, []

    def start(self, src, dst):
        copy = pltpu.make_async_copy(src, dst, self.sems.at[len(self.copies)])
        copy.start()
        self.copies.append(copy)

    def wait(self, *which):
        for k in which:
            self.copies[k].wait()

    def wait_all(self):
        self.wait(*range(len(self.copies)))


def set_slots(main, extra, values):
    count = extra.shape[0]
    main[...] = values[: count * TILE].astype(BF16).reshape(main.shape)
    for e in range(count):
        extra[e] = values[count * TILE + e : count * TILE + e + 1]


def get_slots(main, extra):
    count = extra.shape[0]
    rows = [extra[e] for e in range(count)]
    first = main[...].reshape(count * TILE, main.shape[2])
    return jnp.concatenate([first, jnp.concatenate(rows, 0).astype(BF16)], 0)


class Exchange:
    def __init__(self, copy, send, recv):
        self.copy, self.send, self.recv = copy, send, recv
        self.me, self.count = lax.axis_index("exp"), lax.axis_size("exp")

    def each(self, act, first=1, last=None):
        def body(k, carry):
            act(self.copy(self, k))
            return carry

        lax.fori_loop(first, self.count if last is None else last, body, 0)

    def start(self, *span):
        self.each(lambda c: c.start(), *span)

    def wait_recv(self, *span):
        self.each(lambda c: c.wait_recv(), *span)

    def wait_send(self):
        self.each(lambda c: c.wait_send())

    def to(self, src, dst, k, peer):
        return remote(src, dst, self.send, self.recv, k, "exp", peer)


def exchange_out(src, dst, send, recv):
    def copy(x, k):
        peer = lax.rem(x.me + k, x.count)
        return x.to(src.at[peer], dst.at[k], k, peer)

    return Exchange(copy, send, recv)


def exchange_home(src, dst, send, recv):
    def copy(x, k):
        peer = lax.rem(x.me + x.count - k, x.count)
        return x.to(src.at[k], dst.at[x.me], k, peer)

    return Exchange(copy, send, recv)


def meet_all(partner=None):
    barrier = pltpu.get_barrier_semaphore()
    me, count = lax.axis_index("exp"), lax.axis_size("exp")

    def greet(k, carry):
        peer = lax.rem(me + k, count)
        pl.semaphore_signal(barrier, inc=1, device_id={"exp": peer}, device_id_type=MESH)
        return carry

    lax.fori_loop(1, count, greet, 0)
    ctx = lax.axis_index("ctx")
    right, left = lax.rem(ctx + 1, 4), lax.rem(ctx + 3, 4)
    for neighbour in (left, right):
        pl.semaphore_signal(barrier, inc=1, device_id={"ctx": neighbour}, device_id_type=MESH)
    if partner is not None:
        pl.semaphore_signal(barrier, inc=1, device_id={"section": partner}, device_id_type=MESH)
    greeted = count + (1 if partner is None else 2)
    return (ctx, right, left), lambda: pl.semaphore_wait(barrier, greeted)


def run_experts(ids, outs, all_ref, rets, block, done, beside, scratch):
    part = scratch[0]
    inbox, res = scratch[1:3], scratch[3:5]
    s_in, r_in, s_out, r_out = scratch[5:7], scratch[7:9], scratch[9:11], scratch[11:13]
    rest = scratch[13:]
    me, right, left = ids
    far = lax.rem(me + 2, 4)
    parts, _, rows, width = all_ref.shape
    near = inbox[0].shape[0] // parts
    filled = near * TILE
    exp = lax.axis_index("exp")
    arriving = [exchange_out(outs[m], inbox[m], s_in[m], r_in[m]) for m in range(2)]
    leaving = [exchange_home(res[m], rets[m], s_out[m], r_out[m]) for m in range(2)]
    gathers = [RingGather(all_ref.at[n], rows, ids, *rest[10 * n : 10 * n + 2]) for n in range(parts)]
    scatters = [
        RingScatter(
            part.at[n], rows, ids, rest[10 * n + 4 : 10 * n + 10], *rest[10 * n + 2 : 10 * n + 4]
        )
        for n in range(parts)
    ]
    for n in range(parts):
        for x in arriving:
            x.start(max(1, n * near), (n + 1) * near)
    for m in range(2):
        inbox[m][0] = outs[m][exp]
    beside[0]()
    for n in range(parts):
        for x in arriving:
            x.wait_recv(max(1, n * near), (n + 1) * near)
        all_ref[n, me, :filled] = inbox[0][n * near : (n + 1) * near].reshape(filled, width)
        last = [inbox[1][n * near + k] for k in range(near)]
        last.append(jnp.zeros((rows - filled - near, width), F32))
        all_ref[n, me, filled:] = jnp.concatenate(last, 0).astype(BF16)
        gathers[n].start()
    for n in range(parts):
        block(n, me, part)
    for g in gathers:
        g.forward()
    for n in range(parts):
        gathers[n].wait_left()
        block(n, left, part)
        scatters[n].send_left()
        gathers[n].wait_right()
        block(n, right, part)
        scatters[n].send_right()
        gathers[n].wait_far()
        block(n, far, part)
        scatters[n].send_far()
        done(n)
        if n:
            scatters[n - 1].send_sums()
    beside[1]()
    scatters[-1].send_sums()
    beside[2]()
    for n in range(parts):
        total = scatters[n].total().astype(BF16)
        res[0][n * near : (n + 1) * near] = total[:filled].reshape(near, TILE, width)
        last = total[filled:].astype(F32)
        for k in range(near):
            res[1][n * near + k] = last[k : k + 1]
        for x in leaving:
            x.start(max(1, n * near), (n + 1) * near)
    for m in range(2):
        rets[m][exp] = res[m][0]
    beside[3]()
    for x in leaving:
        x.wait_recv()
    for x in (*gathers, *scatters, *arriving, *leaving):
        x.wait_send()


def slot_buffers(experts, width):
    return [pltpu.VMEM((experts, TILE, width), BF16), pltpu.VMEM((experts, 1, width), F32)]


def expert_scratch(experts, rows, width):
    ring = [*[pltpu.SemaphoreType.DMA((6,))] * 4, *scatter_buffers(rows, width)]
    return [
        pltpu.VMEM((PARTS, 4, rows, width), BF16),
        *slot_buffers(experts, width) * 2,
        *[pltpu.SemaphoreType.DMA((experts,))] * 8,
        *ring * PARTS,
    ]


def route_tables(routes_ref, experts):
    rows = routes_ref.shape[0]
    routes = routes_ref[...]
    lanes = lax.broadcasted_iota(jnp.int32, (rows, experts), 1)
    hot = [jnp.where(routes[:, c : c + 1] == lanes, 1.0, 0.0) for c in range(TOP)]
    row = lax.broadcasted_iota(jnp.int32, (rows, rows), 0)
    col = lax.broadcasted_iota(jnp.int32, (rows, rows), 1)
    before = jnp.where(row > col, 1.0, 0.0).astype(BF16)
    earlier = mm(before, (hot[0] + hot[1]).astype(BF16))
    wide = lax.broadcasted_iota(jnp.int32, (rows, experts * (TILE + 1)), 1).astype(F32)
    slots = []
    for c in range(TOP):
        slot = jnp.sum(hot[c] * earlier, -1, keepdims=True)
        expert = routes[:, c : c + 1].astype(F32)
        target = jnp.where(slot < TILE, expert * TILE + slot, experts * TILE + expert)
        slots.append(jnp.where(wide == target, 1.0, 0.0).astype(BF16))
    return hot, slots


def gates_of(logits, hot):
    chosen = [jnp.sum(h * logits, -1, keepdims=True) for h in hot]
    peak = jnp.maximum(chosen[0], chosen[1])
    raised = [jnp.exp(c - peak) for c in chosen]
    total = 1.0 / (raised[0] + raised[1])
    return [r * total for r in raised]


def part_rows(experts, capacity):
    return -(-(experts // PARTS) * capacity // TILE) * TILE


def bucket_bounds():
    half = BUCKETS // 2
    powers = np.arange(1, BUCKETS - half) / (BUCKETS - half)
    return [int(m) for m in np.ceil(half * (REACH / half) ** powers)]


def tile_buckets(kind):
    row = lax.broadcasted_iota(jnp.int32, (SPAN, 2 * SPAN), 0)
    col = lax.broadcasted_iota(jnp.int32, (SPAN, 2 * SPAN), 1)
    ahead = kind * SPAN + row - lax.rem(col, SPAN)
    n = jnp.maximum(ahead, 0)
    bucket = jnp.minimum(n, BUCKETS // 2)
    for bound in bucket_bounds():
        bucket += (n >= bound).astype(jnp.int32)
    return ahead, bucket


def tile_range(kind):
    half = BUCKETS // 2
    ends = [max(kind * SPAN + r - c, 0) for r, c in ((0, SPAN - 1), (SPAN - 1, 0))]
    first, last = (min(n, half) + sum(n >= m for m in bucket_bounds()) for n in ends)
    return range(first, last + 1)


def make_tiles(table_ref, tiles_ref, heads):
    repeat = tiles_ref.shape[3] // (2 * SPAN)
    for k in range(KINDS - 1):
        ahead, bucket = tile_buckets(k)
        for h in range(heads):
            tile = jnp.full(bucket.shape, NEG, F32)
            for b in tile_range(k):
                tile = jnp.where(bucket == b, table_ref[b : b + 1, h : h + 1], tile)
            tile = jnp.where(ahead < 0, NEG, tile)
            tiles_ref[h, k] = jnp.concatenate([tile] * repeat, 1)


def bias_rows(tiles_ref, table_ref, kind_ref, head, block):
    kind = kind_ref[block : block + 1, :]
    last = table_ref[BUCKETS - 1 : BUCKETS, head : head + 1]
    rows = jnp.where(kind == 3, last, NEG)
    for k in (2, 1, 0):
        rows = jnp.where(kind == k, tiles_ref[head, k], rows)
    return rows


def head_columns(ref, group, head, heads):
    at = (group * heads + head) * HEAD_DIM
    return ref[:, at : at + HEAD_DIM]


def attend(
    ids, wait_all_here, x, gain_ref, w_qkv, w_out, table_ref, kind_ref, all_ref, proj_ref, att_ref,
    tiles_ref, s_ref, p_ref, part, scratch, weights_here
):
    bufs, (s_ag, r_ag, s_rs, r_rs) = scratch[:6], scratch[6:]
    me, right, left = ids
    far = lax.rem(me + 2, 4)
    rows, width = x.shape
    seq = 4 * rows
    heads = w_out.shape[0] // HEAD_DIM
    all_ref[me] = norm(x, gain_ref[...])
    gather = RingGather(all_ref, rows, ids, s_ag, r_ag)
    wait_all_here()
    gather.start()
    make_tiles(table_ref, tiles_ref, heads)
    gather.forward()
    gather.wait_left()
    gather.wait_right()
    gather.wait_far()
    weights_here()
    proj_ref[...] = mm(all_ref[...].reshape(seq, width), w_qkv[...]).astype(BF16)
    parts = []
    for h in range(heads):
        q, k, v = (head_columns(proj_ref, g, h, heads) for g in range(3))
        s_ref[...] = mm_nt(q, k)
        for b in range(seq // SPAN):
            at = slice(b * SPAN, (b + 1) * SPAN)
            s = s_ref[at, :] * HEAD_DIM**-0.5 + bias_rows(tiles_ref, table_ref, kind_ref, h, b)
            e = jnp.exp(s - jnp.max(s, -1, keepdims=True))
            p_ref[at, :] = (e * (1.0 / jnp.sum(e, -1, keepdims=True))).astype(BF16)
        parts.append(mm(p_ref[...], v).astype(BF16))
    att_ref[...] = jnp.concatenate(parts, 1).reshape(att_ref.shape)
    scatter = RingScatter(part, rows, ids, bufs, s_rs, r_rs)
    part[far] = mm(att_ref[far], w_out[...]).astype(BF16)
    scatter.send_far()
    part[right] = mm(att_ref[right], w_out[...]).astype(BF16)
    scatter.send_right()
    part[left] = mm(att_ref[left], w_out[...]).astype(BF16)
    scatter.send_left()
    part[me] = mm(att_ref[me], w_out[...]).astype(BF16)
    scatter.send_sums()
    total = scatter.total()
    gather.wait_send()
    scatter.wait_send()
    return total


def attend_back(
    ids, dmiddle, all_ref, proj_ref, att_ref, w_qkv, w_out, table_ref, kind_ref,
    perm_ref, perm_out_ref, pq_ref, po_ref, dtable_ref, ready,
    tiles_ref, dtiles_ref, s_ref, dp_ref, p_ref, ds_ref, da_ref, dproj_ref, db_ref, part, scratch
):
    bufs, (s_ag, r_ag, s_rs, r_rs) = scratch[:6], scratch[6:]
    me, right, left = ids
    far = lax.rem(me + 2, 4)
    rows, width = dmiddle.shape
    seq = 4 * rows
    heads = w_out.shape[0] // HEAD_DIM
    scale = HEAD_DIM**-0.5
    db_ref[me] = dmiddle.astype(BF16)
    gather = RingGather(db_ref, rows, ids, s_ag, r_ag)
    gather.start()
    make_tiles(table_ref, tiles_ref, heads)
    gather.forward()
    gather.wait_left()
    gather.wait_right()
    gather.wait_far()
    da_ref[...] = mm_nt(db_ref[...].reshape(seq, width), w_out[...]).astype(BF16)
    dq, dk, dv = [], [], []
    for h in range(heads):
        q, k, v = (head_columns(proj_ref, g, h, heads) for g in range(3))
        da = head_columns(da_ref, 0, h, heads)
        s_ref[...] = mm_nt(q, k)
        dp_ref[...] = mm_nt(da, v)
        dtiles_ref[...] = jnp.zeros(dtiles_ref.shape, F32)
        for b in range(seq // SPAN):
            at = slice(b * SPAN, (b + 1) * SPAN)
            s = s_ref[at, :] * scale + bias_rows(tiles_ref, table_ref, kind_ref, h, b)
            e = jnp.exp(s - jnp.max(s, -1, keepdims=True))
            p = e * (1.0 / jnp.sum(e, -1, keepdims=True))
            dp = dp_ref[at, :]
            ds = p * (dp - jnp.sum(p * dp, -1, keepdims=True))
            p_ref[at, :] = p.astype(BF16)
            ds_ref[at, :] = ds.astype(BF16)
            kind = kind_ref[b : b + 1, :]
            for n in range(KINDS):
                dtiles_ref[n] += jnp.where(kind == n, ds, 0.0)
        for n in range(KINDS):
            folded = dtiles_ref[n, :, : 2 * SPAN]
            for m in range(1, seq // (2 * SPAN)):
                folded = folded + dtiles_ref[n, :, m * 2 * SPAN : (m + 1) * 2 * SPAN]
            dtiles_ref[n, :, : 2 * SPAN] = folded
        sums = [jnp.zeros((1, 2 * SPAN), F32)] * BUCKETS
        for n in range(KINDS - 1):
            bucket = tile_buckets(n)[1]
            folded = dtiles_ref[n, :, : 2 * SPAN]
            for b in tile_range(n):
                hit = jnp.where(bucket == b, folded, 0.0)
                sums[b] = sums[b] + jnp.sum(hit, 0, keepdims=True)
        rest = dtiles_ref[KINDS - 1, :, : 2 * SPAN]
        sums[-1] = sums[-1] + jnp.sum(rest, 0, keepdims=True)
        dtable_ref[h] = jnp.concatenate(sums, 0)
        p = p_ref[...]
        ds = ds_ref[...]
        dq.append((mm(ds, k) * scale).astype(BF16))
        dk.append((mm_tn(ds, q) * scale).astype(BF16))
        dv.append(mm_tn(p, da).astype(BF16))
    dproj_ref[...] = jnp.concatenate(dq + dk + dv, 1).reshape(dproj_ref.shape)
    scatter = RingScatter(part, rows, ids, bufs, s_rs, r_rs)
    part[far] = mm_nt(dproj_ref[far], w_qkv[...]).astype(BF16)
    scatter.send_far()
    part[right] = mm_nt(dproj_ref[right], w_qkv[...]).astype(BF16)
    scatter.send_right()
    part[left] = mm_nt(dproj_ref[left], w_qkv[...]).astype(BF16)
    scatter.send_left()
    part[me] = mm_nt(dproj_ref[me], w_qkv[...]).astype(BF16)
    dproj = dproj_ref[...].reshape(seq, dproj_ref.shape[2])
    d_qkv = mm_tn(all_ref[...].reshape(seq, width), dproj).astype(BF16)
    pq_ref[...] = mm(perm_ref[...], d_qkv).astype(BF16)
    ready(0)
    scatter.send_sums()
    d_out = mm_tn(att_ref[...].reshape(seq, att_ref.shape[2]), db_ref[...].reshape(seq, width))
    po_ref[...] = mm(perm_out_ref[...], d_out.astype(BF16)).astype(BF16)
    ready(1)
    total = scatter.total()
    gather.wait_send()
    scatter.wait_send()
    return total


def own_stream(ref):
    return ref.at[lax.axis_index("section"), 0] if len(ref.shape) == 4 else ref


def layer_kernel(
    layer, gains, tables, kind_ref, routers, routes_ref,
    x_in, w_qkv_both, w_out_both, w_in_both, w_back_both,
    h_ref, middle_ref, mixed_ref, logits_ref, picked_ref,
    all_out, proj_out, att_out, ent_out, pre_out, *scratch
):
    tiles_ref, s_ref, p_ref, part, w_in, w_back, ent_ref, pre_ref, sems, save_sems = scratch[:10]
    outs, rets = scratch[10:12], scratch[12:14]
    w_qkv, w_out, all_ref, proj_ref, att_ref, x_ref = scratch[14:20]
    scratch = scratch[:14] + scratch[20:]
    loads, saves = Loads(sems), Loads(save_sems)
    loads.start(own_stream(x_in), x_ref)
    loads.start(w_qkv_both.at[layer], w_qkv)
    loads.start(w_out_both.at[layer], w_out)
    loads.start(w_in_both.at[layer], w_in)
    loads.start(w_back_both.at[layer], w_back)
    gain_one, gain_two = gains.at[2 * layer], gains.at[2 * layer + 1]
    table_ref, router_ref = tables.at[layer], routers.at[layer]
    ids, wait_all_here = meet_all()
    rows, width = x_ref.shape
    loads.wait(0)
    x = x_ref[...].astype(F32)
    branch = attend(
        ids, wait_all_here, x, gain_one, w_qkv, w_out, table_ref, kind_ref, all_ref, proj_ref, att_ref,
        tiles_ref, s_ref, p_ref, part, scratch[14:24], lambda: loads.wait(1, 2)
    )
    saves.start(all_ref, all_out)
    saves.start(proj_ref, proj_out)
    saves.start(att_ref, att_out)
    middle = x + branch
    middle_ref[...] = middle
    mixed = norm(middle, gain_two[...])
    mixed_ref[...] = mixed
    hot, slots = route_tables(routes_ref, logits_ref.shape[1])
    set_slots(*outs, mm_tn(slots[0] + slots[1], mixed))

    def block(n, j, part):
        pre = mm(ent_ref[n, j], w_in[...])
        pre_ref[n, j] = pre
        hidden = gelu_parts(pre)[0].astype(BF16)
        part[n, j] = mm_nt(hidden, w_back[...]).astype(BF16)

    def find_logits():
        logits_ref[...] = mm(mixed_ref[...], router_ref[...])
        loads.wait(3, 4)

    def save(n):
        saves.start(ent_ref.at[n], ent_out.at[n])
        saves.start(pre_ref.at[n], pre_out.at[n])

    nothing = lambda: None
    run_experts(
        ids, outs, ent_ref, rets, block, save,
        (find_logits, nothing, nothing, nothing), scratch[24:]
    )
    gates = gates_of(logits_ref[...], hot)
    returned = get_slots(*rets)
    y = middle_ref[...]
    for c in range(TOP):
        picked = mm(slots[c], returned)
        picked_ref[c] = picked.astype(BF16)
        y = y + gates[c] * picked
    h_ref[...] = y.astype(BF16)
    saves.wait_all()


def layer_forward(x, layer, weights, kind, routes, slots):
    gains, w_qkv, w_out, table, router, w_in, w_back = weights
    rows, width = x.shape[-2:]
    seq, part, experts = 4 * rows, w_out.shape[1], router.shape[2]
    heads = part // HEAD_DIM
    vm, far = pl.BlockSpec(memory_space=pltpu.VMEM), pl.BlockSpec(memory_space=pl.ANY)
    shape = jax.ShapeDtypeStruct
    return pl.pallas_call(
        functools.partial(layer_kernel, layer),
        out_shape=(
            shape((rows, width), BF16),
            shape((rows, width), F32),
            shape((rows, width), BF16),
            shape((rows, experts), F32),
            shape((TOP, rows, width), BF16),
            shape((4, rows, width), BF16),
            shape((seq, 3 * part), BF16),
            shape((4, rows, part), BF16),
            shape((PARTS, 4, slots, width), BF16),
            shape((PARTS, 4, slots, w_in.shape[2]), F32),
        ),
        in_specs=[vm] * 5 + [far] * 5,
        out_specs=(vm,) * 5 + (far,) * 5,
        scratch_shapes=[
            pltpu.VMEM((heads, KINDS - 1, SPAN, seq), F32),
            pltpu.VMEM((seq, seq), F32),
            pltpu.VMEM((seq, seq), BF16),
            pltpu.VMEM((4, rows, width), BF16),
            pltpu.VMEM(w_in.shape[1:], BF16),
            pltpu.VMEM(w_back.shape[1:], BF16),
            pltpu.VMEM((PARTS, 4, slots, width), BF16),
            pltpu.VMEM((PARTS, 4, slots, w_in.shape[2]), F32),
            pltpu.SemaphoreType.DMA((5,)),
            pltpu.SemaphoreType.DMA((3 + 2 * PARTS,)),
            *slot_buffers(experts, width) * 2,
            pltpu.VMEM(w_qkv.shape[1:], BF16),
            pltpu.VMEM(w_out.shape[1:], BF16),
            pltpu.VMEM((4, rows, width), BF16),
            pltpu.VMEM((seq, 3 * part), BF16),
            pltpu.VMEM((4, rows, part), BF16),
            pltpu.VMEM((rows, width), BF16),
            *scatter_buffers(rows, width),
            *[pltpu.SemaphoreType.DMA((6,))] * 4,
            *expert_scratch(experts, slots, width),
        ],
        compiler_params=pltpu.CompilerParams(
            collective_id=layer, has_side_effects=True, vmem_limit_bytes=56 << 20
        ),
    )(gains, table, kind, router, routes, x, w_qkv, w_out, w_in, w_back)


def layer_back_kernel(
    layer, gains, tables, kind_ref, routers, routes_ref,
    middle_ref, mixed_ref, logits_ref, picked_ref, g_in, x_in, w_qkv_both, w_out_both, w_in_both, w_back_both, perm_in, perm_out_in, all_in, proj_in, att_in, ent_in, pre_in,
    dx_ref, dxb_ref, small_ref, pq_ref, po_ref,
    d_in_out, d_back_out, got_in, got_back, got_pq, got_po, *scratch
):
    (
        tiles_ref, dtiles_ref, s_ref, dp_ref, p_ref, ds_ref, da_ref, dproj_ref, db_ref, part,
        darr_ref, hid_ref, dpre_ref, e_in, e_back, drouter_ref, dtable_ref, s_x, r_x,
        d_in, d_back, w_in, w_back, perm_ref, perm_out_ref, all_ref, proj_ref, att_ref,
        ent_ref, pre_ref, sems, save_sems
    ) = scratch[:32]
    w_qkv, w_out, g_ref, x_ref = scratch[32:36]
    scratch = scratch[:32] + scratch[36:]
    outs, rets = scratch[32:34], scratch[34:36]
    loads, saves = Loads(sems), Loads(save_sems)
    loads.start(own_stream(g_in), g_ref)
    loads.start(w_back_both.at[layer], w_back)
    loads.start(w_in_both.at[layer], w_in)
    loads.start(pre_in, pre_ref)
    loads.start(ent_in, ent_ref)
    loads.start(all_in, all_ref)
    loads.start(proj_in, proj_ref)
    loads.start(att_in, att_ref)
    loads.start(perm_in, perm_ref)
    loads.start(perm_out_in, perm_out_ref)
    loads.start(w_qkv_both.at[layer], w_qkv)
    loads.start(w_out_both.at[layer], w_out)
    loads.start(own_stream(x_in), x_ref)
    gain_one, gain_two = gains.at[2 * layer], gains.at[2 * layer + 1]
    table_ref, router_ref = tables.at[layer], routers.at[layer]
    partner = 1 - lax.axis_index("section")
    ids, wait_all_here = meet_all(partner)
    rows, width = x_ref.shape
    loads.wait(0)

    def across(k, src, dst):
        return remote(src, dst, s_x, r_x, k, "section", partner)

    crossing = [
        across(0, e_back, got_back),
        across(1, e_in, got_in),
        across(2, pq_ref, got_pq),
        across(3, po_ref, got_po),
    ]
    g = g_ref[...].astype(F32)
    hot, slots = route_tables(routes_ref, logits_ref.shape[1])
    gates = gates_of(logits_ref[...], hot)
    dreturned = mm_tn(slots[0], (gates[0] * g).astype(BF16)) + mm_tn(
        slots[1], (gates[1] * g).astype(BF16)
    )
    set_slots(*outs, dreturned)
    wait_all_here()

    def logits_back():
        g = g_ref[...].astype(F32)
        dgates = [
            jnp.sum(g * picked_ref[c].astype(F32), -1, keepdims=True) for c in range(TOP)
        ]
        mean = gates[0] * dgates[0] + gates[1] * dgates[1]
        dchosen = [a * (b - mean) for a, b in zip(gates, dgates)]
        dlogits = (hot[0] * dchosen[0] + hot[1] * dchosen[1]).astype(BF16)
        drouter_ref[...] = mm_tn(mixed_ref[...], dlogits)
        dx_ref[...] = mm_nt(dlogits, router_ref[...])
        loads.wait(1, 2, 3)

    def block(n, j, expert_part):
        hidden, slope = gelu_parts(pre_ref[n, j])
        hid_ref[n, j] = hidden.astype(BF16)
        dpre = (mm(darr_ref[n, j], w_back[...]) * slope).astype(BF16)
        dpre_ref[n, j] = dpre
        expert_part[n, j] = mm_nt(dpre, w_in[...]).astype(BF16)

    def flat(ref):
        return ref[...].reshape(math.prod(ref.shape[:3]), ref.shape[3])

    def back_grad():
        grad = mm_tn(flat(darr_ref), flat(hid_ref))
        d_back[...] = grad
        saves.start(d_back, d_back_out)
        e_back[...] = grad.astype(BF16)
        crossing[0].start()

    def in_grad():
        loads.wait(4)
        grad = mm_tn(flat(ent_ref), flat(dpre_ref))
        d_in[...] = grad
        saves.start(d_in, d_in_out)
        e_in[...] = grad.astype(BF16)
        crossing[1].start()

    run_experts(
        ids, outs, darr_ref, rets, block, lambda n: None,
        (logits_back, back_grad, lambda: None, in_grad), scratch[46:]
    )
    dleft = get_slots(*rets)
    loads.wait(*range(5, 13))
    dmixed = mm(slots[0] + slots[1], dleft) + dx_ref[...]
    dnorm, dgain = norm_back(middle_ref[...], gain_two[...], dmixed)
    small_ref[...] = pack_gain(dgain, 1, small_ref.shape) + pack_router(
        drouter_ref[...], small_ref.shape
    )
    dmiddle = g_ref[...].astype(F32) + dnorm
    dx_ref[...] = dmiddle
    dnormed = attend_back(
        ids, dmiddle, all_ref, proj_ref, att_ref, w_qkv, w_out, table_ref, kind_ref,
        perm_ref, perm_out_ref, pq_ref, po_ref, dtable_ref, lambda k: crossing[2 + k].start(),
        tiles_ref, dtiles_ref, s_ref, dp_ref, p_ref, ds_ref, da_ref, dproj_ref, db_ref, part,
        scratch[36:46]
    )
    dnorm, dgain = norm_back(x_ref[...].astype(F32), gain_one[...], dnormed)
    small_ref[...] += pack_gain(dgain, 0, small_ref.shape) + pack_table(
        dtable_ref, small_ref.shape
    )
    dx = dx_ref[...] + dnorm
    dx_ref[...] = dx
    dxb_ref[...] = dx.astype(BF16)
    saves.wait_all()
    for c in crossing:
        c.wait()


def layer_backward(g, keep, layer, weights, kind, routes, slots, perm, perm_out):
    x, normed, proj, attended, middle, mixed, logits, picked, entering, pre = keep
    gains, w_qkv, w_out, table, router, w_in, w_back = weights
    rows, width = x.shape[-2:]
    seq, part, experts = 4 * rows, w_out.shape[1], router.shape[2]
    heads, hid = part // HEAD_DIM, w_in.shape[2]
    w_shape = w_in.shape[1:]
    vm, far = pl.BlockSpec(memory_space=pltpu.VMEM), pl.BlockSpec(memory_space=pl.ANY)
    shape = jax.ShapeDtypeStruct
    pq = shape((perm.shape[0], 3 * part), BF16)
    po = shape((perm_out.shape[0], width), BF16)
    loaded = (normed, proj, attended, entering, pre)
    return pl.pallas_call(
        functools.partial(layer_back_kernel, layer),
        out_shape=(
            shape((rows, width), F32),
            shape((rows, width), BF16),
            shape((perm.shape[0] // OWN, SMALL), F32),
            pq,
            po,
            shape(w_shape, F32),
            shape(w_shape, F32),
            shape(w_shape, BF16),
            shape(w_shape, BF16),
            pq,
            po,
        ),
        in_specs=[vm] * 9 + [far] * 13,
        out_specs=(vm,) * 5 + (far,) * 6,
        scratch_shapes=[
            pltpu.VMEM((heads, KINDS - 1, SPAN, seq), F32),
            pltpu.VMEM((KINDS, SPAN, seq), F32),
            pltpu.VMEM((seq, seq), F32),
            pltpu.VMEM((seq, seq), F32),
            pltpu.VMEM((seq, seq), BF16),
            pltpu.VMEM((seq, seq), BF16),
            pltpu.VMEM((seq, part), BF16),
            pltpu.VMEM((4, rows, 3 * part), BF16),
            pltpu.VMEM((4, rows, width), BF16),
            pltpu.VMEM((4, rows, width), BF16),
            pltpu.VMEM((PARTS, 4, slots, width), BF16),
            pltpu.VMEM((PARTS, 4, slots, hid), BF16),
            pltpu.VMEM((PARTS, 4, slots, hid), BF16),
            pltpu.VMEM(w_shape, BF16),
            pltpu.VMEM(w_shape, BF16),
            pltpu.VMEM((width, experts), F32),
            pltpu.VMEM((heads, BUCKETS, 2 * SPAN), F32),
            *[pltpu.SemaphoreType.DMA((4,))] * 2,
            *[pltpu.VMEM(w_shape, F32)] * 2,
            *[pltpu.VMEM(w_shape, BF16)] * 2,
            *[pltpu.VMEM(a.shape, a.dtype) for a in (perm, perm_out, *loaded)],
            pltpu.SemaphoreType.DMA((13,)),
            pltpu.SemaphoreType.DMA((2,)),
            pltpu.VMEM(w_qkv.shape[1:], BF16),
            pltpu.VMEM(w_out.shape[1:], BF16),
            pltpu.VMEM((rows, width), BF16),
            pltpu.VMEM((rows, width), BF16),
            *slot_buffers(experts, width) * 2,
            *scatter_buffers(rows, width),
            *[pltpu.SemaphoreType.DMA((6,))] * 4,
            *expert_scratch(experts, slots, width),
        ],
        compiler_params=pltpu.CompilerParams(
            collective_id=2 + layer, has_side_effects=True, vmem_limit_bytes=60 << 20
        ),
    )(
        gains, table, kind, router, routes, middle, mixed, logits, picked, g, x,
        w_qkv, w_out, w_in, w_back, perm, perm_out, *loaded
    )


SMALL = 256
OWN = 12
AT_TABLE = 2 * OWN


def grid_of(shape):
    return tuple(lax.broadcasted_iota(jnp.int32, shape, d) for d in (0, 1))


def one_hot(where):
    return jnp.where(where, 1.0, 0.0).astype(BF16)


def owner_rows(owners, width):
    row, col = grid_of((owners, width))
    return one_hot((col >= OWN * row) & (col < OWN * row + OWN))


def table_rows(owners):
    row, col = grid_of((BUCKETS, owners))
    return one_hot(col == 2 * row + lax.axis_index("ctx") // 2)


def table_column(head):
    return AT_TABLE + HEADS // 4 * lax.rem(lax.axis_index("ctx"), 2) + head


def at_router(experts):
    return AT_TABLE + BUCKETS * HEADS // 64


def router_mask(width, experts):
    row, col = grid_of((width, SMALL))
    first = at_router(experts) + experts * lax.rem(row, OWN)
    return (col >= first) & (col < first + experts)


def unpack_small(small, width, experts, heads):
    owners = small.shape[0]
    small = small.astype(BF16)
    own = owner_rows(owners, width)
    spread = mm_tn(small[:, :128], own)
    row, col = grid_of(spread.shape)
    gains = [
        jnp.sum(jnp.where(row == lax.rem(col, OWN) + n * OWN, spread, 0.0), 0, keepdims=True)
        for n in range(2)
    ]
    wide = mm_tn(own, small)
    wide = jnp.where(router_mask(width, experts), wide, 0.0).astype(BF16)
    row, col = grid_of((SMALL, experts))
    first = at_router(experts)
    inside = (row >= first) & (row < first + OWN * experts)
    router = mm(wide, one_hot(inside & (lax.rem(row + experts - first % experts, experts) == col)))
    table = mm(table_rows(owners), small[:, :128]).astype(BF16)
    row, col = grid_of((128, heads))
    table = mm(table, one_hot(row == table_column(col)))
    return gains, router.astype(BF16), table


def pack_gain(dgain, n, shape):
    width = dgain.shape[1]
    row, col = grid_of((width, shape[1]))
    own = owner_rows(shape[0], width).astype(F32) * dgain
    return mm(own.astype(BF16), one_hot(col == lax.rem(row, OWN) + n * OWN))


def pack_router(drouter, shape):
    width, experts = drouter.shape
    row, col = grid_of((experts, shape[1]))
    first = at_router(experts)
    wide = mm(
        drouter.astype(BF16), one_hot(lax.rem(col + experts - first % experts, experts) == row)
    )
    wide = jnp.where(router_mask(width, experts), wide, 0.0).astype(BF16)
    return mm(owner_rows(shape[0], width), wide)


def pack_table(dtable_ref, shape):
    total = jnp.zeros((BUCKETS, shape[1]), F32)
    col = grid_of(total.shape)[1]
    for h in range(dtable_ref.shape[0]):
        column = jnp.sum(dtable_ref[h], -1, keepdims=True)
        total = total + jnp.where(col == table_column(h), column, 0.0)
    return mm_tn(table_rows(shape[0]), total.astype(BF16))


def meet_everyone():
    barrier = pltpu.get_barrier_semaphore()
    peers = [("exp", 16), ("ctx", 4), ("section", 2)]
    for axis, count in peers:
        me = lax.axis_index(axis)

        def greet(k, carry, axis=axis, me=me, count=count):
            peer = lax.rem(me + k, count)
            pl.semaphore_signal(barrier, inc=1, device_id={axis: peer}, device_id_type=MESH)
            return carry

        lax.fori_loop(1, count, greet, 0)
    pl.semaphore_wait(barrier, sum(count - 1 for _, count in peers))


def ctx_exchange(src, dst, send, recv):
    me = lax.axis_index("ctx")
    copies = []
    for k in (1, 3, 2):
        peer = lax.rem(me + k, 4)
        copies.append(remote(src.at[peer], dst.at[me], send, recv, k, "ctx", peer))
    return copies


def weights_kernel(
    cols_ref, outp_ref, w_in, w_back, perm_ref, perm_out_ref, pick_ref, fill_ref, fill_small_ref,
    w_qkv, w_out, gains, routers, tables, both_in, both_back,
    zin, grid, grid_out, s_z, r_z, s_q, r_q, s_o, r_o, s_fq, r_fq, s_fo, r_fo, s_x, r_x, s_own
):
    meet_everyone()
    section, ctx, exp = (lax.axis_index(a) for a in ("section", "ctx", "exp"))
    partner = 1 - section
    count = grid.shape[1]
    turn = ctx_exchange(cols_ref, zin, s_z, r_z)
    for c in turn:
        c.start()
    w_in, w_back = w_in.at[0, 0], w_back.at[0, 0]
    cross_in = remote(w_in, both_in.at[section], s_x, r_x, 0, "section", partner)
    cross_back = remote(w_back, both_back.at[section], s_x, r_x, 1, "section", partner)
    cross_in.start()
    cross_back.start()
    zin[ctx] = cols_ref[ctx]

    def spread(ref, send, recv, k):
        peer = lax.rem(exp + k, count)
        at = ref.at[section, exp]
        return remote(at, at, send, recv, k, "exp", peer)

    def forward(ref, send, recv, k):
        at = ref.at[section, lax.rem(exp + count - k, count)]
        return remote(at, at, send, recv, k, "section", partner)

    def each(act, first=1):
        def body(k, carry):
            act(k)
            return carry

        lax.fori_loop(first, count, body, 0)

    for c in turn:
        c.wait_recv()
    came = zin[...].reshape(zin.shape[0] * zin.shape[1], zin.shape[2])
    small = mm(fill_small_ref[...], came[:, :SMALL]).astype(BF16)
    outp = outp_ref[...]
    grid_out[section, exp] = jnp.concatenate([outp[:, :SMALL] + small, outp[:, SMALL:]], 1)
    each(lambda k: spread(grid_out, s_o, r_o, k).start())
    grid[section, exp] = mm(fill_ref[...], came).astype(BF16)
    each(lambda k: spread(grid, s_q, r_q, k).start())
    forward(grid_out, s_fo, r_fo, 0).start()
    forward(grid, s_fq, r_fq, 0).start()
    own_in = pltpu.make_async_copy(w_in, both_in.at[section], s_own.at[0])
    own_back = pltpu.make_async_copy(w_back, both_back.at[section], s_own.at[1])
    own_in.start()
    own_back.start()

    def relay(ref, s, r, sf, rf, k):
        spread(ref, s, r, k).wait_recv()
        forward(ref, sf, rf, k).start()

    each(lambda k: relay(grid_out, s_o, r_o, s_fo, r_fo, k))
    each(lambda k: relay(grid, s_q, r_q, s_fq, r_fq, k))

    def unpack(layer):
        flat = grid[layer].reshape(perm_ref.shape[1], grid.shape[3])
        w_qkv[layer] = mm(perm_ref[...], flat).astype(BF16)
        flat = grid_out[layer].reshape(perm_out_ref.shape[1], grid_out.shape[3])
        w_out[layer] = mm(perm_out_ref[...], flat).astype(BF16)
        small = mm(pick_ref[...], flat[:, :SMALL])
        two, routers[layer], tables[layer] = unpack_small(
            small, routers.shape[1], routers.shape[2], tables.shape[2]
        )
        gains[2 * layer], gains[2 * layer + 1] = two

    unpack(section)
    each(lambda k: forward(grid_out, s_fo, r_fo, k).wait_recv(), 0)
    each(lambda k: forward(grid, s_fq, r_fq, k).wait_recv(), 0)
    unpack(partner)
    each(lambda k: spread(grid_out, s_o, r_o, k).wait_send())
    each(lambda k: spread(grid, s_q, r_q, k).wait_send())
    each(lambda k: forward(grid_out, s_fo, r_fo, k).wait_send(), 0)
    each(lambda k: forward(grid, s_fq, r_fq, k).wait_send(), 0)
    for c in turn:
        c.wait_send()
    own_in.wait()
    own_back.wait()
    cross_in.wait()
    cross_back.wait()


def gather_weights(cols, outp, w_in, w_back, perm, perm_out, pick, fill, fill_small):
    width, part = outp.shape[1], cols.shape[2]
    count = perm_out.shape[1] // TILE
    vm, far = pl.BlockSpec(memory_space=pltpu.VMEM), pl.BlockSpec(memory_space=pl.ANY)
    dma = lambda n: pltpu.SemaphoreType.DMA((n,))
    return pl.pallas_call(
        weights_kernel,
        out_shape=(
            jax.ShapeDtypeStruct((2, width, part), BF16),
            jax.ShapeDtypeStruct((2, perm_out.shape[0], width), BF16),
            jax.ShapeDtypeStruct((4, 1, width), F32),
            jax.ShapeDtypeStruct((2, width, count), BF16),
            jax.ShapeDtypeStruct((2, BUCKETS, part // (3 * HEAD_DIM)), F32),
            jax.ShapeDtypeStruct((2, *w_in.shape[2:]), BF16),
            jax.ShapeDtypeStruct((2, *w_back.shape[2:]), BF16),
        ),
        in_specs=[vm] * 2 + [far] * 2 + [vm] * 5,
        out_specs=(vm,) * 5 + (far,) * 2,
        scratch_shapes=[
            pltpu.VMEM(cols.shape, BF16),
            pltpu.VMEM((2, count, fill.shape[0], part), BF16),
            pltpu.VMEM((2, count, 16, width), BF16),
            dma(4), dma(4), *[dma(count)] * 8, dma(2), dma(2), dma(2),
        ],
        compiler_params=pltpu.CompilerParams(
            collective_id=4, has_side_effects=True, vmem_limit_bytes=48 << 20
        ),
    )(cols, outp, w_in, w_back, perm, perm_out, pick, fill, fill_small)


def owners_kernel(
    small0, small1, spread_ref, y0, y1, dx0, dx1,
    pq0, pq1, gq0, gq1, po0, po1, go0, go1, in0, in1, gin0, gin1, back0, back1, gback0, gback1,
    turned, out_grad, d_in_out, d_back_out, layer_out, input_grad,
    pq, gq, po, go, d_in, gin, d_back, gback,
    sent_small, got_small, sent_y, sent_dx, pieces, box, pieces_out, box_out, summed,
    s_s, r_s, s_q, r_q, s_o, r_o, s_z, r_z, sems, save_sems
):
    section, ctx, exp = (lax.axis_index(a) for a in ("section", "ctx", "exp"))
    partner = 1 - section
    first = section == 0
    of_first = (po0, go0, pq0, gq0, in0, gin0, back0, gback0)
    of_second = (po1, go1, pq1, gq1, in1, gin1, back1, gback1)
    held = (po, go, pq, gq, d_in, gin, d_back, gback)

    def load(sources):
        for k, (src, dst) in enumerate(zip(sources, held)):
            pltpu.make_async_copy(src, dst, sems.at[k]).start()

    @pl.when(first)
    def _():
        load(of_first)

    @pl.when(jnp.logical_not(first))
    def _():
        load(of_second)

    def loaded(*which):
        for k in which:
            pltpu.make_async_copy(of_first[k], held[k], sems.at[k]).wait()

    meet_everyone()
    sent_small[...] = jnp.where(first, small1[...], small0[...])
    cross = [
        remote(sent_small, got_small, s_s, r_s, 0, "section", partner),
        remote(sent_y, layer_out.at[section], s_s, r_s, 1, "section", partner),
        remote(sent_dx, input_grad.at[section], s_s, r_s, 2, "section", partner),
    ]
    cross[0].start()

    def both(a, b):
        return a[...].astype(F32) + b[...].astype(F32)

    loaded(2, 3)
    pieces[...] = both(pq, gq).astype(BF16).reshape(pieces.shape)
    swap = exchange_out(pieces, box, s_q, r_q)
    swap.start()
    loaded(0, 1)
    dense = both(po, go)
    cross[0].wait_recv()
    small = jnp.where(first, small0[...], small1[...]) + got_small[...]
    wide = mm(spread_ref[...], small.astype(BF16))
    dense = jnp.concatenate([dense[:, :SMALL] + wide, dense[:, SMALL:]], 1)
    pieces_out[...] = dense.astype(BF16).reshape(pieces_out.shape)
    swap_out = exchange_out(pieces_out, box_out, s_o, r_o)
    swap_out.start()
    box[0] = pieces[exp]
    box_out[0] = pieces_out[exp]
    sent_y[...] = jnp.where(first, y1[...], y0[...])
    cross[1].start()
    sent_dx[...] = jnp.where(first, dx1[...].astype(F32), dx0[...])
    cross[2].start()
    layer_out[section] = jnp.where(first, y0[...], y1[...])
    input_grad[section] = jnp.where(first, dx0[...], dx1[...].astype(F32))
    saves = Loads(save_sems)
    loaded(4, 5)
    d_in[...] += gin[...].astype(F32)
    saves.start(d_in, d_in_out.at[0, 0])
    loaded(6, 7)
    d_back[...] += gback[...].astype(F32)
    saves.start(d_back, d_back_out.at[0, 0])
    swap.wait_recv()
    total = box[0].astype(F32)
    for k in range(1, box.shape[0]):
        total = total + box[k].astype(F32)
    summed[...] = jnp.zeros(summed.shape, F32)
    for c in range(4):
        summed[c, :OWN, :] = total[c * OWN : (c + 1) * OWN]
    swap_out.wait_recv()
    total = box_out[0].astype(F32)
    for k in range(1, box_out.shape[0]):
        total = total + box_out[k].astype(F32)
    out_grad[...] = total
    for c in range(4):
        summed[c, OWN : OWN + 1, :SMALL] = total[OWN + c : OWN + c + 1, :SMALL]
    turn = ctx_exchange(summed, turned, s_z, r_z)
    for c in turn:
        c.start()
    turned[ctx] = summed[ctx]
    for c in turn:
        c.wait()
    cross[0].wait_send()
    cross[1].wait()
    cross[2].wait()
    swap.wait_send()
    swap_out.wait_send()
    saves.wait_all()


def sum_at_owners(pq, gq, po, go, small, spread, d_in, g_in, d_back, g_back, y, dx, count):
    rows, part = pq[0].shape
    out_rows, width = po[0].shape
    vm, far = pl.BlockSpec(memory_space=pltpu.VMEM), pl.BlockSpec(memory_space=pl.ANY)
    dma = lambda n: pltpu.SemaphoreType.DMA((n,))
    own = (rows // count, part)
    own_out = (out_rows // count, width)
    quarter = (4, TILE, part)
    held = [a[0] for a in (pq, gq, po, go, d_in, g_in, d_back, g_back)]
    return pl.pallas_call(
        owners_kernel,
        out_shape=(
            jax.ShapeDtypeStruct(quarter, F32),
            jax.ShapeDtypeStruct(own_out, F32),
            jax.ShapeDtypeStruct((1, 1, *d_in[0].shape), F32),
            jax.ShapeDtypeStruct((1, 1, *d_back[0].shape), F32),
            jax.ShapeDtypeStruct((2, *y[0].shape), BF16),
            jax.ShapeDtypeStruct((2, *dx[0].shape), F32),
        ),
        in_specs=[vm] * 7 + [far] * 16,
        out_specs=(vm, vm, far, far, vm, vm),
        scratch_shapes=[
            *[pltpu.VMEM(a.shape, a.dtype) for a in held],
            pltpu.VMEM(small[0].shape, F32),
            pltpu.VMEM(small[0].shape, F32),
            pltpu.VMEM(y[0].shape, BF16),
            pltpu.VMEM(dx[0].shape, F32),
            pltpu.VMEM((count, *own), BF16),
            pltpu.VMEM((count, *own), BF16),
            pltpu.VMEM((count, *own_out), BF16),
            pltpu.VMEM((count, *own_out), BF16),
            pltpu.VMEM(quarter, F32),
            dma(3), dma(3), *[dma(count)] * 4, dma(4), dma(4), dma(8), dma(2),
        ],
        compiler_params=pltpu.CompilerParams(
            collective_id=5, has_side_effects=True, vmem_limit_bytes=52 << 20
        ),
    )(*small, spread, *y, *dx, *pq, *gq, *po, *go, *d_in, *g_in, *d_back, *g_back)


def packing(n_ctx, n_exp, own_rows):
    blocks = n_ctx * n_exp
    perm = np.zeros((blocks, own_rows, blocks, own_rows), np.float32)
    pick = np.zeros((blocks, n_exp, TILE), np.float32)
    perm_out = np.zeros((n_exp, TILE, n_exp, own_rows), np.float32)
    fill = np.zeros((n_ctx, own_rows, n_ctx, TILE), np.float32)
    fill_small = np.zeros((TILE, n_ctx, TILE), np.float32)
    for c in range(n_ctx):
        fill_small[own_rows + c, c, own_rows] = 1
        for i in range(own_rows):
            fill[c, i, c, i] = 1
    for e in range(n_exp):
        for i in range(own_rows):
            perm_out[e, i, e, i] = 1
        for c in range(n_ctx):
            for i in range(own_rows):
                perm[e * n_ctx + c, i, c * n_exp + e, i] = 1
            pick[c * n_exp + e, e, own_rows + c] = 1
    perm = perm.reshape(blocks * own_rows, blocks * own_rows)
    pick = pick.reshape(blocks, n_exp * TILE)
    perm_out = perm_out.reshape(n_exp * TILE, n_exp * own_rows)
    fill = fill.reshape(n_ctx * own_rows, n_ctx * TILE)
    fill_small = fill_small.reshape(TILE, n_ctx * TILE)
    pack = (perm, perm_out, pick.T.copy())
    unpack = (perm.T.copy(), perm_out.T.copy(), pick, fill, fill_small)
    return tuple(tuple(jnp.asarray(m, BF16) for m in ms) for ms in (pack, unpack))


def norm_scale(v):
    return lax.rsqrt(jnp.mean(v * v, -1, keepdims=True) + EPS)


def norm(v, gain):
    return (v * norm_scale(v) * gain).astype(BF16)


def norm_back(v, gain, du):
    r = norm_scale(v)
    dug = du * gain
    dv = r * dug - v * (r * r * r) * jnp.mean(dug * v, -1, keepdims=True)
    return dv, jnp.sum(du * v * r, 0, keepdims=True)


def gelu_parts(v):
    t = jnp.tanh(GELU_C * (v + 0.044715 * v * v * v))
    value = 0.5 * v * (1.0 + t)
    slope = 0.5 * (1.0 + t) + 0.5 * v * (1.0 - t * t) * GELU_C * (1.0 + 3 * 0.044715 * v * v)
    return value, slope


def on_device(
    inputs,
    cotangent,
    routes,
    block_order,
    attn_gain,
    qkv_weight,
    out_weight,
    rel_bias,
    moe_gain,
    router_weight,
    expert_in,
    expert_out,
):
    rows, width = inputs.shape[2:]
    n_ctx, n_exp = lax.axis_size("ctx"), lax.axis_size("exp")
    seq = rows * n_ctx
    own_rows = qkv_weight.shape[1]
    heads = HEADS // n_ctx
    part = heads * HEAD_DIM
    capacity = rows * TOP // n_exp + max(1, rows * TOP // (16 * n_exp))
    slots = part_rows(n_exp, capacity)
    section = lax.axis_index("section")
    ctx = lax.axis_index("ctx")
    first = section == 0

    (perm, perm_out, place), unpack = packing(n_ctx, n_exp, own_rows)
    small = jnp.concatenate(
        [attn_gain[0], moe_gain[0], rel_bias[0], router_weight[0].reshape(-1)]
    )
    n_small = small.shape[0]
    columns = qkv_weight[0].reshape(own_rows, 3, n_ctx, part).transpose(2, 0, 1, 3)
    columns = columns.reshape(n_ctx, own_rows, 3 * part)
    small_row = jnp.pad(small, (0, 3 * part - n_small))
    small_rows = jnp.broadcast_to(small_row, (n_ctx, 1, 3 * part))
    columns = jnp.concatenate([columns, small_rows], 1)
    columns = jnp.pad(columns, ((0, 0), (0, 15 - own_rows), (0, 0)))
    out_rows = jnp.pad(out_weight[0], ((0, 16 - own_rows), (0, 0)))
    w_qkv, w_out, gains, routers, tables, w_in, w_back = gather_weights(
        columns, out_rows, expert_in, expert_out, *unpack
    )
    weights = (gains, w_qkv, w_out, tables, routers, w_in, w_back)
    n_bias = BUCKETS * HEADS // (n_ctx * n_exp)
    ahead = block_order[:, None] - block_order[None, :]
    kind = jnp.repeat(jnp.where(ahead < 0, -1, jnp.minimum(ahead, 3)), SPAN, 1)

    own_routes = routes[0, :, 0]
    kept = jnp.where(first, own_routes[0], own_routes[1])
    given = jnp.where(first, own_routes[1], own_routes[0])
    taken = lax.ppermute(given, "section", [(0, 1), (1, 0)])
    layer_routes = (jnp.where(first, kept, taken), jnp.where(first, taken, kept))
    def forward(x, layer):
        h, middle, mixed, logits, picked, normed, proj, attended, *rest = layer_forward(
            x, layer, weights, kind, layer_routes[layer], slots
        )
        return h, (x, normed, proj, attended, middle, mixed, logits, picked, *rest)

    def backward(g, keep, layer):
        dx, dxb, d_small, pq, po, d_in, d_back, g_in, g_back, gq, go = layer_backward(
            g, keep, layer, weights, kind, layer_routes[layer], slots, perm, perm_out
        )
        return dx, dxb, (pq, gq, po, go, d_small, d_in, g_in, d_back, g_back)

    h, keep0 = forward(inputs, 0)
    top, keep1 = forward(h, 1)
    _, dh, grads1 = backward(cotangent, keep1, 1)
    dx, _, grads0 = backward(dh, keep0, 0)
    pq, gq, po, go, d_small, d_in, g_in, d_back, g_back = zip(grads0, grads1)
    pieces, out_grad, d_in, d_back, layer_out, input_grad = sum_at_owners(
        pq, gq, po, go, d_small, place, d_in, g_in, d_back, g_back,
        (h, top), (dx, dh), n_exp
    )
    qkv_grad = pieces[:, :own_rows].reshape(n_ctx, own_rows, 3, part)
    qkv_grad = qkv_grad.transpose(1, 2, 0, 3).reshape(own_rows, 3 * width)
    out_grad = out_grad[:own_rows]
    small = jnp.sum(pieces[:, own_rows, :n_small], 0)

    layer_out = layer_out.reshape(1, 2, 1, rows, width)
    input_grad = input_grad.reshape(1, 2, 1, rows, width)
    return (
        layer_out,
        input_grad,
        small[:own_rows][None],
        qkv_grad[None],
        out_grad[None],
        small[2 * own_rows : 2 * own_rows + n_bias][None],
        small[own_rows : 2 * own_rows][None],
        small[2 * own_rows + n_bias :].reshape(1, own_rows, n_exp),
        d_in,
        d_back,
    )


def solution(mesh):
    return jax.shard_map(
        on_device,
        mesh=mesh,
        in_specs=(
            P(None, "exp", "ctx", None),
            P(None, "exp", "ctx", None),
            P("section", None, "exp", "ctx", None),
            P(),
            P("section", ("ctx", "exp")),
            P("section", ("ctx", "exp"), None),
            P("section", ("ctx", "exp"), None),
            P("section", ("ctx", "exp")),
            P("section", ("ctx", "exp")),
            P("section", ("ctx", "exp"), None),
            P("section", "exp", None, "ctx"),
            P("section", "exp", None, "ctx"),
        ),
        out_specs=(
            P("section", None, "exp", "ctx", None),
            P("section", None, "exp", "ctx", None),
            P("section", ("ctx", "exp")),
            P("section", ("ctx", "exp"), None),
            P("section", ("ctx", "exp"), None),
            P("section", ("ctx", "exp")),
            P("section", ("ctx", "exp")),
            P("section", ("ctx", "exp"), None),
            P("section", "exp", None, "ctx"),
            P("section", "exp", None, "ctx"),
        ),
        check_vma=False,
    )
```
